32 devices in a mesh: replica: 8 (over y, x, core), shard: 4 (over z).
Axes of the slice: x: 2, y: 2, z: 4, core: 2. Of those that a mesh axis runs over, the one named last changes fastest.
Arguments:
- layer_input: bfloat16 [8192, 2048], P(('replica', 'shard')), may hold values from -6 to 6
- attn_gain: bfloat16 [2048], P('shard'), may hold values from 0.5 to 1.5
- attn_shift: bfloat16 [2048], P('shard'), may hold values from -1.796875 to 1.796875
- qkv_weight: bfloat16 [2048, 6144], P('shard'), may hold values from -0.125 to 0.125
- qkv_bias: bfloat16 [6144], P('shard'), may hold values from -1.796875 to 1.796875
- out_weight: bfloat16 [2048, 2048], P('shard'), may hold values from -2 to 2
- out_bias: bfloat16 [2048], P('shard'), may hold values from -1.796875 to 1.796875
- mlp_gain: bfloat16 [2048], P('shard'), may hold values from 0.5 to 1.5
- mlp_shift: bfloat16 [2048], P('shard'), may hold values from -1.796875 to 1.796875
- up_weight: bfloat16 [2048, 8192], P('shard'), may hold values from -0.125 to 0.125
- up_bias: bfloat16 [8192], P('shard'), may hold values from -1.796875 to 1.796875
- down_weight: bfloat16 [8192, 2048], P('shard'), may hold values from -0.0625 to 0.0625
- down_bias: bfloat16 [2048], P('shard'), may hold values from -1.796875 to 1.796875
- seq_lengths: int32 [8, 4], P('replica'), may hold values from 1 to 896, 1024 in all within a row
- upstream: bfloat16 [8192, 2048], P(('replica', 'shard')), may hold values from -6 to 6
Outputs:
- layer_output: bfloat16 [8192, 2048], P(('replica', 'shard'))
- input_grad: float32 [8192, 2048], P(('replica', 'shard'))
- attn_gain_grad: float32 [2048], P('shard')
- attn_shift_grad: float32 [2048], P('shard')
- qkv_weight_grad: float32 [2048, 6144], P('shard')
- qkv_bias_grad: float32 [6144], P('shard')
- out_weight_grad: float32 [2048, 2048], P('shard')
- out_bias_grad: float32 [2048], P('shard')
- mlp_gain_grad: float32 [2048], P('shard')
- mlp_shift_grad: float32 [2048], P('shard')
- up_weight_grad: float32 [2048, 8192], P('shard')
- up_bias_grad: float32 [8192], P('shard')
- down_weight_grad: float32 [8192, 2048], P('shard')
- down_bias_grad: float32 [2048], P('shard')
The draws below stay inside these ranges and needn't reach their ends.
Inputs may be any that keep to these rules, and one draw needn't show every extreme that they name: `seq_lengths`: each row sums to 1024; its largest entry is exactly 896, so one sequence of every group spans all of its stretches.
All inputs are finite; a program needn't handle non-finite values.
Results may differ from the reference program's by a relative error of at most 0.0092.
Values may be sent and summed in bfloat16 or wider, within the bound.
A program may use at most 640 MiB of HBM per device.

```python
import math
import jax
import jax.numpy as jnp
import numpy as np
from jax import lax

D = 2048
HEADS = 8
HEAD = 256
ROT = 64
FF = 8192
SEQS = 4
GROUP_TOK = 1024
LONGEST = 896
TOKENS = 8192
N_REPLICA = 8


def levels(stream_key, extent, cuts, least, largest):
    level, own = 1.0, jax.random.fold_in(stream_key, 6)
    for axis_at, parts in cuts:
        steps = jnp.exp(jax.random.uniform(jax.random.fold_in(own, axis_at), (parts,), jnp.float32, least / len(cuts), largest / len(cuts)))
        level = level * jnp.repeat(steps, extent[axis_at] // parts).reshape([-1 if axis == axis_at else 1 for axis in range(len(extent))])
    return level


def length_profile(count, total, reach, skew):
    weights = [(1 << 20) // math.isqrt(standing ** skew) + 1 for standing in range(2, count + 1)]
    spare, given = total - reach - (count - 1), [1] * (count - 1)
    while spare > 0:
        candidates = [i for i in range(count - 1) if given[i] < reach]
        pool, left = sum([weights[i] for i in candidates]), spare
        for i in candidates:
            addition = min(reach - given[i], max(1, left * weights[i] // pool), spare)
            given[i] = given[i] + addition
            spare = spare - addition
    return np.array([reach] + given)


def uneven(own_key, amount, total, limit, slope):
    if amount == 2:
        one = jax.random.randint(own_key, (), max(1, total - limit), min(limit, total - 1) + 1)
        return jnp.stack([one, total - one])
    sizes = jnp.asarray(length_profile(amount, total, limit, slope), jnp.int32)
    couples = (amount - 1) // 2
    donor, taker = sizes[1:1 + 2 * couples:2], sizes[2:2 + 2 * couples:2]
    margin = jnp.minimum(donor - 1, limit - taker)
    moved = jax.random.randint(jax.random.fold_in(own_key, 1), (couples,), 0, 1 << 20) % (margin + 1)
    sizes = sizes.at[1:1 + 2 * couples:2].set(donor - moved).at[2:2 + 2 * couples:2].set(taker + moved)
    return sizes[jax.random.permutation(jax.random.fold_in(own_key, 2), amount)]


def centred(stream_key, extent, scale, reach, pieces=(), kind=jnp.bfloat16):
    gain = levels(stream_key, extent, pieces, -0.22, 0.18) if pieces else 1.0
    array = jax.random.normal(stream_key, extent, jnp.float32) * scale * gain
    return jnp.minimum(jnp.maximum(array, -reach), reach).astype(kind)


def setup_inputs(seed: int = 0) -> dict:
    keys = jax.random.split(jax.random.key(seed), 16)
    return {
        "layer_input": centred(keys[0], (TOKENS, D), 1.0, 6.0, ((0, 32),)),
        "attn_gain": jnp.clip(1.0 + 0.1 * jax.random.normal(keys[1], (D,), jnp.float32), 0.5, 1.5).astype(jnp.bfloat16),
        "attn_shift": centred(keys[2], (D,), 0.3, 1.796875, ((0, 4),)),
        "qkv_weight": centred(keys[3], (D, 3 * D), D ** -0.5, 0.125, ((0, 4),)),
        "qkv_bias": centred(keys[4], (3 * D,), 0.3, 1.796875, ((0, 4),)),
        "out_weight": centred(keys[5], (D, D), (max(D // 256, 1)) ** -0.5, 2.0, ((0, 4),)),
        "out_bias": centred(keys[6], (D,), 0.3, 1.796875, ((0, 4),)),
        "mlp_gain": jnp.clip(1.0 + 0.1 * jax.random.normal(keys[7], (D,), jnp.float32), 0.5, 1.5).astype(jnp.bfloat16),
        "mlp_shift": centred(keys[8], (D,), 0.3, 1.796875, ((0, 4),)),
        "up_weight": centred(keys[9], (D, FF), D ** -0.5, 0.125, ((0, 4),)),
        "up_bias": centred(keys[10], (FF,), 0.3, 1.796875, ((0, 4),)),
        "down_weight": centred(keys[11], (FF, D), FF ** -0.5, 0.0625, ((0, 4),)),
        "down_bias": centred(keys[12], (D,), 0.3, 1.796875, ((0, 4),)),
        "seq_lengths": jax.vmap(lambda own: uneven(own, SEQS, GROUP_TOK, LONGEST, 0))(jax.random.split(keys[13], N_REPLICA)).reshape((N_REPLICA, SEQS)).astype(jnp.int32),
        "upstream": centred(keys[14], (TOKENS, D), 1.0, 6.0, ((0, 32),)),
    }


@jax.custom_vjp
def low(v):
    return lax.optimization_barrier(v.astype(jnp.bfloat16)).astype(jnp.float32)

@jax.custom_vjp
def low_back(v):
    return v

def low_keep(v):
    return (low(v), None)

def low_pass(kept, grad):
    return (grad,)

def back_keep(v):
    return (v, None)

def back_low(kept, grad):
    return (low(grad),)
low.defvjp(low_keep, low_pass)
low_back.defvjp(back_keep, back_low)
EPSILON = 1e-05
ROPE_BASE = 10000.0
NEG_LARGE = -1e+30

def high_dot(left, right):
    return jnp.dot(left, right, precision=lax.Precision.HIGHEST, preferred_element_type=jnp.float32)

def normalize(layer_rows):
    centered = layer_rows - lax.optimization_barrier(jnp.mean(layer_rows, -1, keepdims=True))
    variance = lax.optimization_barrier(jnp.mean(centered * centered, -1, keepdims=True))
    return centered * lax.rsqrt(variance + EPSILON)

def rotation_tables(positions):
    exponent = jnp.arange(ROT // 2, dtype=jnp.float32) * (2.0 / ROT)
    inv_freq = jnp.power(jnp.float32(ROPE_BASE), -exponent)
    angles = positions.astype(jnp.float32)[:, None] * inv_freq[None, :]
    cosine_table = jnp.cos(angles)
    sine_table = jnp.sin(angles)
    return (jnp.concatenate([cosine_table, cosine_table], 1), jnp.concatenate([sine_table, sine_table], 1))

def turn(values, cosine_table, sine_table):
    rotary = values[..., :ROT]
    first_half = rotary[..., :ROT // 2]
    second_half = rotary[..., ROT // 2:]
    swapped = jnp.concatenate([-second_half, first_half], -1)
    turned = rotary * cosine_table[:, None, :] + swapped * sine_table[:, None, :]
    return jnp.concatenate([turned, values[..., ROT:]], -1)

def sequence_layout(lengths):
    seq_ends = jnp.cumsum(lengths).astype(jnp.int32)
    where_in = jnp.arange(GROUP_TOK, dtype=jnp.int32)
    seg_ids = lax.optimization_barrier(jnp.sum((where_in[:, None] >= seq_ends[None, :]).astype(jnp.int32), 1))
    starts = seq_ends - lengths
    chosen = (seg_ids[:, None] == jnp.arange(SEQS, dtype=jnp.int32)[None, :]).astype(jnp.int32)
    positions = where_in - lax.optimization_barrier(jnp.sum(chosen * starts[None, :], 1))
    return (seg_ids, positions)

def group_forward(params, layer_rows, seg_ids, positions):
    attn_gain, attn_shift, qkv_weight, qkv_bias, out_weight, out_bias, mlp_gain, mlp_shift, up_weight, up_bias, down_weight, down_bias = params
    row_count = layer_rows.shape[0]
    normed = normalize(layer_rows)
    attn_in = low(normed * attn_gain + attn_shift)
    joined_qkv = low_back(high_dot(attn_in, qkv_weight) + qkv_bias)
    cosine_table, sine_table = rotation_tables(positions)
    queries = low(turn(joined_qkv[:, :D].reshape(row_count, HEADS, HEAD), cosine_table, sine_table))
    keys_all = low(turn(joined_qkv[:, D:2 * D].reshape(row_count, HEADS, HEAD), cosine_table, sine_table))
    values_all = low(joined_qkv[:, 2 * D:].reshape(row_count, HEADS, HEAD))
    row_block = min(512, row_count)
    blocks = row_count // row_block
    score_scale = 1.0 / math.sqrt(HEAD)
    key_index = jnp.arange(row_count, dtype=jnp.int32)

    def attend(block_index):
        row_start = (block_index * row_block).astype(jnp.int32)
        block_queries = lax.dynamic_slice_in_dim(queries, row_start, row_block, 0)
        block_segs = lax.dynamic_slice_in_dim(seg_ids, row_start, row_block, 0)
        query_index = row_start + jnp.arange(row_block, dtype=jnp.int32)
        raw_scores = jnp.einsum('qhd,khd->hqk', block_queries, keys_all, precision=lax.Precision.HIGHEST)
        scores = low_back(score_scale * raw_scores)
        allowed = (block_segs[:, None] == seg_ids[None, :]) & (key_index[None, :] <= query_index[:, None])
        scores = jnp.where(allowed[None], scores, NEG_LARGE)
        row_max = lax.optimization_barrier(jnp.max(scores, -1, keepdims=True))
        shifted = jnp.exp(scores - row_max)
        attn_probs = shifted / lax.optimization_barrier(jnp.sum(shifted, -1, keepdims=True))
        return jnp.einsum('hqk,khd->qhd', low(attn_probs), values_all, precision=lax.Precision.HIGHEST)
    mixed_heads = lax.map(jax.checkpoint(attend), jnp.arange(blocks, dtype=jnp.int32))
    mixed_heads = low(low_back(mixed_heads.reshape(row_count, D)))
    attn_out = high_dot(mixed_heads, out_weight) + out_bias
    mlp_in = low(normed * mlp_gain + mlp_shift)
    up_pre = low_back(high_dot(mlp_in, up_weight) + up_bias)
    activated = low(jax.nn.gelu(up_pre, approximate=False))
    mlp_out = high_dot(activated, down_weight) + down_bias
    return layer_rows + attn_out + mlp_out

def reference(layer_input, attn_gain, attn_shift, qkv_weight, qkv_bias, out_weight, out_bias, mlp_gain, mlp_shift, up_weight, up_bias, down_weight, down_bias, seq_lengths, upstream):
    params = (attn_gain.astype(jnp.float32), attn_shift.astype(jnp.float32), qkv_weight.astype(jnp.float32), qkv_bias.astype(jnp.float32), out_weight.astype(jnp.float32), out_bias.astype(jnp.float32), mlp_gain.astype(jnp.float32), mlp_shift.astype(jnp.float32), up_weight.astype(jnp.float32), up_bias.astype(jnp.float32), down_weight.astype(jnp.float32), down_bias.astype(jnp.float32))
    rows_all = layer_input.astype(jnp.float32).reshape(N_REPLICA, GROUP_TOK, D)
    seg_all, pos_all = jax.vmap(sequence_layout)(seq_lengths)

    def forward(weights, group_rows):

        def one_group(inputs):
            return group_forward(weights, inputs[0], inputs[1], inputs[2])
        return lax.map(jax.checkpoint(one_group), (group_rows, seg_all, pos_all))
    output, pullback = jax.vjp(forward, params, rows_all)
    weight_grads, input_grad = pullback(upstream.astype(jnp.float32).reshape(N_REPLICA, GROUP_TOK, D))
    return (output.reshape(TOKENS, D).astype(jnp.bfloat16), input_grad.reshape(TOKENS, D), weight_grads[0], weight_grads[1], weight_grads[2], weight_grads[3], weight_grads[4], weight_grads[5], weight_grads[6], weight_grads[7], weight_grads[8], weight_grads[9], weight_grads[10], weight_grads[11])
```

```python
from functools import partial
import math

import jax
import jax.numpy as jnp
from jax import lax
from jax.experimental import pallas as pl
from jax.experimental.pallas import tpu as pltpu
from jax.sharding import PartitionSpec as P

D = 2048
HEADS = 8
HEAD = 256
ROT = 64


EPSILON = 1e-05
ROPE_BASE = 10000.0
NEG_LARGE = -1e30
MESH = pl.DeviceIdType.MESH
CONTRACT_ROWS = (((0,), (0,)), ((), ()))
CONTRACT_COLS = (((1,), (1,)), ((), ()))


def normalize(layer_rows):
    centered = layer_rows - jnp.mean(layer_rows, -1, keepdims=True)
    variance = jnp.mean(centered * centered, -1, keepdims=True)
    inverse_std = lax.rsqrt(variance + EPSILON)
    return (centered * inverse_std, inverse_std)


def norm_backward(grad_normed, normed, inverse_std):
    mean_grad = jnp.mean(grad_normed, -1, keepdims=True)
    mean_cross = jnp.mean(grad_normed * normed, -1, keepdims=True)
    return (grad_normed - mean_grad - normed * mean_cross) * inverse_std


def rotation_tables(positions):
    exponent = jnp.arange(ROT // 2, dtype=jnp.float32) * (2.0 / ROT)
    inv_freq = jnp.power(jnp.float32(ROPE_BASE), -exponent)
    angles = positions.astype(jnp.float32)[:, None] * inv_freq[None, :]
    cosine_table = jnp.cos(angles)
    sine_table = jnp.sin(angles)
    return (
        jnp.concatenate([cosine_table, cosine_table], 1),
        jnp.concatenate([sine_table, sine_table], 1),
    )


def turn(values, cosine_table, sine_table):
    rotary = values[..., :ROT]
    first_half = rotary[..., : ROT // 2]
    second_half = rotary[..., ROT // 2 :]
    swapped = jnp.concatenate([-second_half, first_half], -1)
    turned = rotary * cosine_table[:, None, :] + swapped * sine_table[:, None, :]
    return jnp.concatenate([turned, values[..., ROT:]], -1)


def turn_back(values, cosine_table, sine_table):
    rotary = values[..., :ROT]
    scaled = rotary * sine_table[:, None, :]
    swapped = jnp.concatenate([scaled[..., ROT // 2 :], -scaled[..., : ROT // 2]], -1)
    turned = rotary * cosine_table[:, None, :] + swapped
    return jnp.concatenate([turned, values[..., ROT:]], -1)


def sequence_layout(lengths, group_rows):
    seq_count = lengths.shape[0]
    seq_ends = jnp.cumsum(lengths)
    where_in = jnp.arange(group_rows, dtype=jnp.int32)
    seg_ids = jnp.sum((where_in[:, None] >= seq_ends[None, :]).astype(jnp.int32), 1)
    starts = seq_ends - lengths
    chosen = (seg_ids[:, None] == jnp.arange(seq_count, dtype=jnp.int32)[None, :]).astype(jnp.int32)
    positions = where_in - jnp.sum(chosen * starts[None, :], 1)
    return (seg_ids, positions)


def dot(left, right):
    return jnp.dot(left, right, preferred_element_type=jnp.float32)


def dot_rows(left, right):
    return lax.dot_general(left, right, CONTRACT_ROWS, preferred_element_type=jnp.float32)


def dot_cols(left, right):
    return lax.dot_general(left, right, CONTRACT_COLS, preferred_element_type=jnp.float32)


def bit_of(index, bit):
    return lax.rem(lax.div(index, 1 << bit), 2)


def flip(index, bit):
    return index + (1 << bit) * (1 - 2 * bit_of(index, bit))


def plane_orders(replicas):
    far = list(range(1, replicas.bit_length() - 1))
    return far, far[1:] + far[:1]


def remote(src, dst, sems, at, device):
    return pltpu.make_async_remote_copy(
        src_ref=src,
        dst_ref=dst,
        send_sem=sems.at[(0,) + at],
        recv_sem=sems.at[(1,) + at],
        device_id=device,
        device_id_type=MESH,
    )


def greet(rep, place, replicas, shards_n):
    barrier = pltpu.get_barrier_semaphore()
    bits = replicas.bit_length() - 1
    for bit in range(bits):
        pl.semaphore_signal(
            barrier, inc=1, device_id={"replica": flip(rep, bit)}, device_id_type=MESH
        )
    for step in range(1, shards_n):
        pl.semaphore_signal(
            barrier,
            inc=1,
            device_id={"shard": lax.rem(place + step, shards_n)},
            device_id_type=MESH,
        )
    pl.semaphore_wait(barrier, bits + shards_n - 1)


def columns_kernel(
    replicas,
    shards_n,
    small_ref,
    up_ref,
    qkv_ref,
    small_out,
    up_out,
    qkv_out,
    own_sem,
    small_sem,
    turn_sem,
    plane_sem,
):
    rep, place = lax.axis_index("replica"), lax.axis_index("shard")
    bits = replicas.bit_length() - 1
    part, hidden = up_out.shape[1:]
    wide = qkv_out.shape[3]
    full = wide * shards_n
    rows = part // replicas
    orders = [order + [0] for order in plane_orders(replicas)]
    starts = []
    for order in orders:
        start = 0
        for level, bit in enumerate(order):
            start = start + bit_of(rep, bit) * (rows << level)
        starts.append(start)
    greet(rep, place, replicas, shards_n)

    def up_source(shard, path):
        return up_ref.at[
            pl.ds(starts[path], rows),
            pl.ds(pl.multiple_of(shard * hidden + path * (hidden // 2), 128), hidden // 2),
        ]

    def up_target(shard, start, count, path):
        return up_out.at[shard, pl.ds(start, count), pl.ds(path * (hidden // 2), hidden // 2)]

    def qkv_source(third, shard, path):
        return qkv_ref.at[
            pl.ds(starts[path], rows),
            pl.ds(
                pl.multiple_of(third * full + shard * wide + path * (wide // 2), 128), wide // 2
            ),
        ]

    def qkv_target(third, shard, start, count, path):
        return qkv_out.at[
            third, shard, pl.ds(start, count), pl.ds(path * (wide // 2), wide // 2)
        ]

    def source(thing, shard, path):
        return up_source(shard, path) if thing == 0 else qkv_source(thing - 1, shard, path)

    def target(thing, shard, start, count, path):
        if thing == 0:
            return up_target(shard, start, count, path)
        return qkv_target(thing - 1, shard, start, count, path)

    items = [(thing, step) for thing in range(4) for step in range(1, shards_n)]

    def turned(item, path, sending):
        thing, step = items[item]
        to = lax.rem(place + step, shards_n)
        shard = place if sending else lax.rem(place - step + shards_n, shards_n)
        return remote(
            source(thing, to, path),
            target(thing, shard, starts[path], rows, path),
            turn_sem,
            (item, path),
            {"shard": to},
        )

    def spread(item, path, level):
        thing, step = items[item]
        shard = lax.rem(place - step + shards_n, shards_n)
        order = orders[path]
        start = 0
        for above in range(level, bits):
            start = start + bit_of(rep, order[above]) * (rows << above)
        here = target(thing, shard, pl.multiple_of(start, rows), rows << level, path)
        return remote(
            here, here, plane_sem, (item, path, level), {"replica": flip(rep, order[level])}
        )

    def small_copy(step, sending):
        to = lax.rem(place + step, shards_n)
        shard = place if sending else lax.rem(place - step + shards_n, shards_n)
        return remote(small_ref, small_out.at[shard], small_sem, (step,), {"shard": to})

    for item in range(len(items)):
        for path in range(2):
            turned(item, path, True).start()
    for step in range(1, shards_n):
        small_copy(step, True).start()
    own = [
        pltpu.make_async_copy(small_ref, small_out.at[place], own_sem.at[0]),
        pltpu.make_async_copy(
            up_ref.at[:, pl.ds(pl.multiple_of(place * hidden, 128), hidden)],
            up_out.at[place],
            own_sem.at[1],
        ),
    ] + [
        pltpu.make_async_copy(
            qkv_ref.at[:, pl.ds(pl.multiple_of(third * full + place * wide, 128), wide)],
            qkv_out.at[third, place],
            own_sem.at[2 + third],
        )
        for third in range(3)
    ]
    for copy in own:
        copy.start()
    for tick in range(len(items) + bits):
        for level in reversed(range(bits + 1)):
            item = tick - level
            if not 0 <= item < len(items):
                continue
            for path in range(2):
                if level == 0:
                    turned(item, path, False).wait_recv()
                else:
                    spread(item, path, level - 1).wait_recv()
                if level < bits:
                    spread(item, path, level).start()
    for item in range(len(items)):
        for path in range(2):
            turned(item, path, True).wait_send()
            for level in range(bits):
                spread(item, path, level).wait_send()
    for step in range(1, shards_n):
        small_copy(step, False).wait()
    for copy in own:
        copy.wait()


def column_blocks(small, up_weight, qkv_weight):
    replicas, count = lax.axis_size("replica"), lax.axis_size("shard")
    bits = replicas.bit_length() - 1
    part = up_weight.shape[0]
    hidden, wide = up_weight.shape[1] // count, qkv_weight.shape[1] // (3 * count)
    items = 4 * (count - 1)
    any_spec = pl.BlockSpec(memory_space=pl.ANY)
    return pl.pallas_call(
        partial(columns_kernel, replicas, count),
        out_shape=(
            jax.ShapeDtypeStruct((count,) + small.shape, small.dtype),
            jax.ShapeDtypeStruct((count, part, hidden), jnp.bfloat16),
            jax.ShapeDtypeStruct((3, count, part, wide), jnp.bfloat16),
        ),
        in_specs=[any_spec] * 3,
        out_specs=(any_spec,) * 3,
        scratch_shapes=[
            pltpu.SemaphoreType.DMA((5,)),
            pltpu.SemaphoreType.DMA((2, count)),
            pltpu.SemaphoreType.DMA((2, items, 2)),
            pltpu.SemaphoreType.DMA((2, items, 2, bits)),
        ],
        compiler_params=pltpu.CompilerParams(collective_id=0, has_side_effects=True),
        cost_estimate=pl.CostEstimate(flops=0, bytes_accessed=200_000_000, transcendentals=0),
    )(small, up_weight, qkv_weight)


RING = 3
TILE = 256


def grads_kernel(
    replicas,
    shards_n,
    act_ref,
    up_ref,
    mixed_ref,
    mlp_ref,
    attn_ref,
    slope_ref,
    down_ref,
    proj_ref,
    heads_ref,
    rows_ref,
    cols_up_ref,
    cols_qkv_ref,
    tables_ref,
    first_ref,
    stats_ref,
    gains_ref,
    out_ref,
    vec_out,
    sum_out,
    work,
    from_core,
    *rest,
):
    rep, place = lax.axis_index("replica"), lax.axis_index("shard")
    bits = replicas.bit_length() - 1
    far = bits - 1
    from_far = rest[:far]
    (
        big,
        narrow,
        pre,
        joined,
        wide_rows,
        slope,
        heads,
        key_sum,
        value_sum,
        tile_x,
        tile_up,
        tile_qkv,
        shared,
        vec_got,
        vec_sum,
        load_sem,
        core_sem,
        far_sem,
        turn_sem,
        own_sem,
        plane_sem,
        vec_sem,
        sum_sem,
    ) = rest[far:]
    chunks, _, rows, cols = out_ref.shape
    slots = work.shape[0]
    half, side = rows // 2, cols // 2
    piece = rows // replicas
    orders = plane_orders(replicas)
    core = bit_of(rep, 0)
    tokens, width = up_ref.shape
    local = tokens // shards_n
    hiddens = pre.shape[0]
    natives = hiddens + 1
    mine = pl.multiple_of(core * half, half)
    theirs = pl.multiple_of((1 - core) * half, half)

    starts = []
    for order in orders:
        line, size = [core * half], half
        for bit in order:
            size //= 2
            line.append(line[-1] + bit_of(rep, bit) * size)
        starts.append(line)

    def spot(k):
        if k < natives:
            return k + hiddens
        return k - natives if k < natives + hiddens else k

    def load(source, target, number):
        return pltpu.make_async_copy(source, target, load_sem.at[number])

    def narrow_load(k):
        source = act_ref.at[:, pl.ds(k * cols, cols)] if k < hiddens else mixed_ref
        return load(source, narrow.at[k % 2], k % 2)

    def big_load(which):
        return load((up_ref, mlp_ref, attn_ref)[which], big.at[which % 2], 2 + which)

    def pre_loads(k):
        return [
            load(down_ref.at[pl.ds(k * cols, cols), :], wide_rows.at[k % 2], 5 + k % 2),
            load(slope_ref.at[:, pl.ds(k * cols, cols)], slope.at[k % 2], 7 + k % 2),
        ]

    def proj_load():
        return load(proj_ref, wide_rows.at[1], 6)

    def heads_load():
        return load(heads_ref, heads.at[pl.ds(0, 3)], 9)

    def tile_loads(j):
        some = pl.ds(j * TILE, TILE)
        return [
            load(rows_ref.at[:, some], tile_x.at[j % 2], 10 + j % 2),
            load(cols_up_ref.at[some, :], tile_up.at[j % 2], 12 + j % 2),
            load(cols_qkv_ref.at[:, some, :], tile_qkv.at[j % 2], 14 + j % 2),
        ]

    def to_core(k):
        return remote(
            work.at[k % slots, :, pl.ds(theirs, half), :],
            from_core.at[k % RING],
            core_sem,
            (0, k),
            {"replica": flip(rep, 0)},
        )

    def to_far(k, level, path):
        size = half >> (level + 1)
        bit = orders[path][level]
        start = starts[path][level] + (1 - bit_of(rep, bit)) * size
        return remote(
            work.at[k % slots, :, pl.ds(pl.multiple_of(start, size), size), pl.ds(path * side, side)],
            from_far[level].at[k % RING, path],
            far_sem,
            (k, level, path),
            {"replica": flip(rep, bit)},
        )

    def own_piece(k, path, block):
        return work.at[
            k % slots,
            block,
            pl.ds(pl.multiple_of(starts[path][far], piece), piece),
            pl.ds(path * side, side),
        ]

    def place_piece(k, path, block):
        return out_ref.at[
            spot(k),
            block,
            pl.ds(pl.multiple_of(starts[path][far], piece), piece),
            pl.ds(path * side, side),
        ]

    def settle(k, path):
        block = pl.ds(0, shards_n) if k < natives else place
        return pltpu.make_async_copy(
            own_piece(k, path, block), place_piece(k, path, block), own_sem.at[k % 2, path]
        )

    def turned(k, path, step, sending):
        to = lax.rem(place + step, shards_n)
        shard = place if sending else lax.rem(place - step + shards_n, shards_n)
        return remote(
            own_piece(k, path, to),
            place_piece(k, path, shard),
            turn_sem,
            (k - natives, path, step - 1),
            {"shard": to},
        )

    def spread(k, path, level):
        size = piece << level
        bit = orders[path][far - 1 - level]
        here = out_ref.at[
            spot(k),
            :,
            pl.ds(pl.multiple_of(starts[path][far - level], size), size),
            pl.ds(path * side, side),
        ]
        return remote(here, here, plane_sem, (k, level, path), {"replica": flip(rep, bit)})

    def spread_core(k):
        here = out_ref.at[spot(k), :, pl.ds(mine, half), :]
        return remote(here, here, core_sem, (1, k), {"replica": flip(rep, 0)})

    def put(offset, sums):
        for i in range(sums.shape[1] // 128):
            vec_sum[pl.ds(offset // 128 + i, 1), :] = sums[:, i * 128 : (i + 1) * 128]

    def compute(k):
        if k < natives:
            narrow_load(k).wait()
            if k + 1 < natives:
                narrow_load(k + 1).start()
        if k == 0:
            big_load(0).wait()
        if k == natives:
            big_load(1).wait()
            big_load(2).start()
        if k == natives + hiddens:
            big_load(2).wait()
        slot = k % slots
        which = 1 if natives <= k < natives + hiddens else 0

        for begin, send in ((theirs, True), (mine, False)):

            def block(g, carry):
                if k < natives:
                    left = narrow[k % 2, :, pl.ds(begin, half)]
                    right = big[which, :, pl.ds(pl.multiple_of(g * cols, cols), cols)]
                else:
                    left = big[which, :, pl.ds(pl.multiple_of(g * rows + begin, half), half)]
                    if k < natives + hiddens:
                        right = pre[k - natives]
                    else:
                        right = joined[k - natives - hiddens]
                work[slot, g, pl.ds(begin, half), :] = dot_rows(left, right).astype(jnp.bfloat16)
                return carry

            lax.fori_loop(0, shards_n, block, 0)
            if send:
                to_core(k).start()

    def add(k, start, size, left, width, got):
        def block(g, carry):
            where = (k % slots, g, pl.ds(pl.multiple_of(start, size), size), pl.ds(left, width))
            work[where] = (
                work[where].astype(jnp.float32) + got(g).astype(jnp.float32)
            ).astype(jnp.bfloat16)
            return carry

        lax.fori_loop(0, shards_n, block, 0)

    def grad_mixed():
        proj_load().wait()

        def block(i, carry):
            some = pl.ds(pl.multiple_of(i * TILE, TILE), TILE)
            heads[3, some, :] = dot_cols(big[0, some, :], wide_rows[1]).astype(jnp.bfloat16)
            return carry

        lax.fori_loop(0, tokens // TILE, block, 0)
        pre_loads(1)[0].start()
        own = pl.ds(pl.multiple_of(place * cols, cols), cols)
        put(4 * width + place * cols, jnp.sum(big[0, :, own].astype(jnp.float32), 0, keepdims=True))

    def grad_pre(k):
        for copy in pre_loads(k):
            copy.wait()

        def block(i, total):
            some = pl.ds(pl.multiple_of(i * TILE, TILE), TILE)
            found = dot_cols(big[0, some, :], wide_rows[k % 2]) * slope[k % 2, some, :].astype(
                jnp.float32
            )
            low = found.astype(jnp.bfloat16)
            pre[k, some, :] = low
            return total + jnp.sum(low.astype(jnp.float32), 0, keepdims=True)

        total = lax.fori_loop(0, tokens // TILE, block, jnp.zeros((1, cols), jnp.float32))
        put(8 * width + (place * hiddens + k) * cols, total)
        if k + 2 < hiddens:
            for copy in pre_loads(k + 2):
                copy.start()

    def turn_rows(found, some):
        lead = found[:, :128]
        lead = (
            lead * tables_ref[0, some, :]
            + pltpu.roll(lead, 96, 1) * tables_ref[1, some, :]
            - pltpu.roll(lead, 32, 1) * tables_ref[2, some, :]
        )
        return jnp.concatenate([lead, found[:, 128:]], 1)

    def attention(head):
        lanes = pl.ds(head * HEAD, HEAD)
        scale = 1.0 / math.sqrt(HEAD)
        key_sum[...] = jnp.zeros_like(key_sum)
        value_sum[...] = jnp.zeros_like(value_sum)
        sums = [jnp.zeros((1, HEAD), jnp.float32)] * 3
        for i in range(tokens // TILE):
            some, keys = pl.ds(i * TILE, TILE), pl.ds(0, (i + 1) * TILE)
            shape = (TILE, (i + 1) * TILE)
            query = heads[0, some, lanes]
            key = heads[1, keys, lanes]
            scores = dot_cols(query, key) * scale
            at = lax.broadcasted_iota(jnp.int32, shape, 1)
            upto = lax.broadcasted_iota(jnp.int32, shape, 0) + i * TILE
            scores = jnp.where((at >= first_ref[some, :]) & (at <= upto), scores, NEG_LARGE)
            shifted = jnp.exp(scores - jnp.max(scores, -1, keepdims=True))
            probs = shifted / jnp.sum(shifted, -1, keepdims=True)
            grad = heads[3, some, lanes]
            grad_probs = dot_cols(grad, heads[2, keys, lanes])
            delta = jnp.sum(probs * grad_probs, -1, keepdims=True)
            low = (probs * (grad_probs - delta)).astype(jnp.bfloat16)
            found = turn_rows(dot(low, key) * scale, some).astype(jnp.bfloat16)
            joined[0, some, lanes] = found
            sums[0] = sums[0] + jnp.sum(found.astype(jnp.float32), 0, keepdims=True)
            key_sum[keys, :] = key_sum[keys, :] + dot_rows(low, query)
            value_sum[keys, :] = value_sum[keys, :] + dot_rows(probs.astype(jnp.bfloat16), grad)
        for i in range(tokens // TILE):
            some = pl.ds(i * TILE, TILE)
            for third, found in (
                (1, turn_rows(key_sum[some, :] * scale, some)),
                (2, value_sum[some, :]),
            ):
                low = found.astype(jnp.bfloat16)
                joined[third, some, lanes] = low
                sums[third] = sums[third] + jnp.sum(low.astype(jnp.float32), 0, keepdims=True)
        for third in range(3):
            put(5 * width + third * width + place * cols + head * HEAD, sums[third])

    def sum_part(j, step, sending):
        to = lax.rem(place + step, shards_n)
        shard = place if sending else lax.rem(place - step + shards_n, shards_n)
        some = pl.ds(j * TILE, TILE)
        source = shared.at[pl.ds(pl.multiple_of(to * local, local), local), some]
        if step == 0:
            return pltpu.make_async_copy(source, sum_out.at[place, :, some], sum_sem.at[0, j, 0])
        return remote(source, sum_out.at[shard, :, some], sum_sem, (j, step), {"shard": to})

    def tile(j):
        for copy in tile_loads(j):
            copy.wait()
        if j + 1 < width // TILE:
            for copy in tile_loads(j + 1):
                copy.start()
        lanes = pl.ds(j * TILE, TILE)

        def block(i, totals):
            some = pl.ds(pl.multiple_of(i * local, local), local)
            normed = (tile_x[j % 2, some, :].astype(jnp.float32) - stats_ref[0, some, :]) * stats_ref[
                1, some, :
            ]
            mlp = sum(
                dot_cols(pre[k, some, :], tile_up[j % 2, :, k * cols : (k + 1) * cols])
                for k in range(hiddens)
            )
            attn = sum(dot_cols(joined[p, some, :], tile_qkv[j % 2, p]) for p in range(3))
            shared[some, lanes] = (
                attn * gains_ref[0:1, lanes] + mlp * gains_ref[1:2, lanes]
            ).astype(jnp.bfloat16)
            found = (attn * normed, attn, mlp * normed, mlp)
            return tuple(t + jnp.sum(f, 0, keepdims=True) for t, f in zip(totals, found))

        zero = jnp.zeros((1, TILE), jnp.float32)
        totals = lax.fori_loop(0, shards_n, block, (zero,) * 4)
        for number, total in enumerate(totals):
            put(number * width + j * TILE, total)
        for step in range(shards_n):
            sum_part(j, step, True).start()

    def stage(k, number):
        if number == 0:
            compute(k)
        elif number == 1:
            to_core(k).wait()
            add(k, mine, half, 0, cols, lambda g: from_core[k % RING, g])
            for path in range(2):
                to_far(k, 0, path).start()
        elif number <= 1 + far:
            level = number - 2
            for path in range(2):
                to_far(k, level, path).wait()
                size = half >> (level + 1)
                add(
                    k,
                    starts[path][level + 1],
                    size,
                    path * side,
                    side,
                    lambda g: from_far[level][k % RING, path, g],
                )
                if level + 1 < far:
                    to_far(k, level + 1, path).start()
                else:
                    if k >= natives:
                        for step in range(1, shards_n):
                            turned(k, path, step, True).start()
                    settle(k, path).start()
        elif number == 2 + far:
            for path in range(2):
                settle(k, path).wait()
                if k >= natives:
                    for step in range(1, shards_n):
                        turned(k, path, step, False).wait_recv()
                spread(k, path, 0).start()
            if k >= natives:
                for path in range(2):
                    for step in range(1, shards_n):
                        turned(k, path, step, True).wait_send()
        elif number <= 2 + 2 * far:
            level = number - 3 - far
            for path in range(2):
                spread(k, path, level).wait()
                if level + 1 < far:
                    spread(k, path, level + 1).start()
            if level + 1 == far:
                spread_core(k).start()
        else:
            spread_core(k).wait()

    stages = 4 + 2 * far
    n_heads, n_tiles = cols // HEAD, width // TILE
    extras = {0: [grad_mixed, lambda: grad_pre(0)]}
    for k in range(1, hiddens):
        extras.setdefault(k, []).append(partial(grad_pre, k))
    for head in range(n_heads):
        extras.setdefault(1 + head, []).append(partial(attention, head))
    tile_at = hiddens + 1
    for j in range(n_tiles):
        extras.setdefault(tile_at + j, []).append(partial(tile, j))
    vec_at = tile_at + n_tiles

    for copy in [narrow_load(0), big_load(0), proj_load()] + pre_loads(0):
        copy.start()
    pre_loads(1)[1].start()
    for copy in [heads_load(), big_load(1)] + tile_loads(0):
        copy.start()
    vec_sum[...] = jnp.zeros_like(vec_sum)
    greet(rep, place, replicas, shards_n)
    peers = [{"replica": flip(rep, bit)} for bit in range(bits)]
    peers += [{"shard": flip(place, bit)} for bit in range(shards_n.bit_length() - 1)]

    def vec_copy(number):
        return remote(vec_sum, vec_got.at[number], vec_sem, (number,), peers[number])

    for tick in range(max(chunks + stages - 1, vec_at + len(peers) + 1)):
        for number in reversed(range(stages)):
            if 0 <= tick - number < chunks:
                stage(tick - number, number)
        if tick == 1:
            heads_load().wait()
        for extra in extras.get(tick, []):
            extra()
        turn_of = tick - vec_at
        if 0 < turn_of <= len(peers):
            vec_copy(turn_of - 1).wait()
            vec_sum[...] = vec_sum[...] + vec_got[turn_of - 1]
        if 0 <= turn_of < len(peers):
            vec_copy(turn_of).start()
    vec_out[...] = vec_sum[...]
    for j in range(n_tiles):
        for step in range(shards_n):
            sum_part(j, step, False).wait()


def summed_grads(*operands):
    act, up, mixed, mlp_in = operands[:4]
    replicas, count = lax.axis_size("replica"), lax.axis_size("shard")
    bits = replicas.bit_length() - 1
    far = bits - 1
    tokens, width = up.shape
    cols = width // count
    hidden = act.shape[1]
    hiddens = hidden // cols
    natives = hiddens + 1
    chunks = natives + hiddens + 3
    peers = bits + count.bit_length() - 1
    slots = 2 + far
    vector = ((8 * width + count * hidden) // 128, 128)
    any_spec = pl.BlockSpec(memory_space=pl.ANY)
    vmem_spec = pl.BlockSpec(memory_space=pltpu.VMEM)
    low = lambda *shape: pltpu.VMEM(shape, jnp.bfloat16)
    full = lambda *shape: pltpu.VMEM(shape, jnp.float32)
    dma = lambda *shape: pltpu.SemaphoreType.DMA(shape)
    return pl.pallas_call(
        partial(grads_kernel, replicas, count),
        out_shape=(
            jax.ShapeDtypeStruct((chunks, count, cols, cols), jnp.bfloat16),
            jax.ShapeDtypeStruct(vector, jnp.float32),
            jax.ShapeDtypeStruct((count, tokens // count, width), jnp.bfloat16),
        ),
        in_specs=[any_spec] * 12 + [vmem_spec] * 4,
        out_specs=(any_spec, vmem_spec, any_spec),
        scratch_shapes=[
            low(slots, count, cols, cols),
            low(RING, count, cols // 2, cols),
        ]
        + [low(RING, 2, count, cols >> (level + 2), cols // 2) for level in range(far)]
        + [
            low(2, tokens, width),
            low(2, tokens, cols),
            low(hiddens, tokens, cols),
            low(3, tokens, cols),
            low(2, cols, width),
            low(2, tokens, cols),
            low(4, tokens, cols),
            full(tokens, HEAD),
            full(tokens, HEAD),
            low(2, tokens, TILE),
            low(2, TILE, hidden),
            low(2, 3, TILE, cols),
            low(tokens, width),
            full(peers, *vector),
            full(*vector),
            dma(16),
            dma(2, 2, chunks),
            dma(2, chunks, far, 2),
            dma(2, chunks - natives, 2, count - 1),
            dma(2, 2),
            dma(2, chunks, far, 2),
            dma(2, peers),
            dma(2, width // TILE, count),
        ],
        compiler_params=pltpu.CompilerParams(
            collective_id=1, has_side_effects=True, vmem_limit_bytes=60 * 2**20
        ),
        cost_estimate=pl.CostEstimate(
            flops=4 * tokens * chunks * count * cols * cols,
            bytes_accessed=600_000_000,
            transcendentals=0,
        ),
    )(*operands)


def widen_kernel(by_shard, in_ref, out_ref):
    number, count, _, cols = in_ref.shape
    for k in range(number):
        for g in range(count):
            at = (g * number + k if by_shard else k * count + g) * cols
            out_ref[:, at : at + cols] = in_ref[k, g].astype(jnp.float32)


def widen(blocks, first, number, down):
    count, rows, cols = blocks.shape[1:]
    some = 256 if down else 64
    if down:
        shape, depth = (number * rows, count * cols), 1
        grid = (number, rows // some)
        source = lambda k, i: (first + k, 0, i, 0)
        target = lambda k, i: (k * (rows // some) + i, 0)
    else:
        shape, depth = (rows, number * count * cols), number
        grid = (1, rows // some)
        source = lambda k, i: (first // number, 0, i, 0)
        target = lambda k, i: (i, 0)
    return pl.pallas_call(
        partial(widen_kernel, number != 3),
        out_shape=jax.ShapeDtypeStruct(shape, jnp.float32),
        grid=grid,
        in_specs=[pl.BlockSpec((depth, count, some, cols), source)],
        out_specs=pl.BlockSpec((some, shape[1]), target),
        compiler_params=pltpu.CompilerParams(vmem_limit_bytes=32 * 2**20),
    )(blocks)


def shards(
    layer_input,
    attn_gain,
    attn_shift,
    qkv_weight,
    qkv_bias,
    out_weight,
    out_bias,
    mlp_gain,
    mlp_shift,
    up_weight,
    up_bias,
    down_weight,
    down_bias,
    seq_lengths,
    upstream,
):
    local_rows = layer_input.shape[0]
    count = lax.axis_size("shard")
    group_rows = local_rows * count
    place = lax.axis_index("shard")
    heads = HEADS // count
    wide = heads * HEAD
    part = D // count
    hidden = up_bias.shape[0]
    score_scale = 1.0 / math.sqrt(HEAD)

    small = jnp.concatenate(
        [attn_gain, attn_shift, out_bias, mlp_gain, mlp_shift, down_bias, qkv_bias]
    )
    length = small.shape[0]
    small = jnp.pad(small, (0, -length % 2048)).reshape(16, -1)
    small_all, up_cols, qkv_cols = column_blocks(small, up_weight, qkv_weight)
    up_cols = up_cols.reshape(D, hidden)
    qkv_cols = qkv_cols.reshape(3, D, wide)
    small_all = small_all.reshape(count, -1)[:, :length].astype(jnp.float32)
    gain_a, shift_a, bias_o, gain_m, shift_m, bias_d = (
        small_all[:, i * part : (i + 1) * part].reshape(D) for i in range(6)
    )
    bias_j = lax.dynamic_index_in_dim(
        small_all[:, 6 * part :].reshape(3, count, wide), place, 1, keepdims=False
    )

    rows_all = lax.all_gather(layer_input, "shard", axis=0, tiled=True)
    upper, rows_all = lax.optimization_barrier((upstream, rows_all))
    up_all = lax.all_gather(upper, "shard", axis=0, tiled=True)

    seg_ids, positions = sequence_layout(seq_lengths[0], group_rows)
    key_index = jnp.arange(group_rows, dtype=jnp.int32)
    allowed = (seg_ids[:, None] == seg_ids[None, :]) & (key_index[None, :] <= key_index[:, None])
    cosine_table, sine_table = rotation_tables(positions)

    rows_all_f = rows_all.astype(jnp.float32)
    row_mean = jnp.mean(rows_all_f, -1, keepdims=True)
    normed, inverse_std_all = normalize(rows_all_f)
    mlp_in = (normed * gain_m + shift_m).astype(jnp.bfloat16)
    attn_in = (normed * gain_a + shift_a).astype(jnp.bfloat16)

    up_pre = dot(mlp_in, up_cols) + up_bias.astype(jnp.float32)
    cdf = 0.5 * (1.0 + lax.erf(up_pre * math.sqrt(0.5)))
    act_low = (up_pre * cdf).astype(jnp.bfloat16)
    slope = cdf + up_pre * jnp.exp(-0.5 * up_pre * up_pre) * (1.0 / math.sqrt(2.0 * math.pi))

    joined_q, joined_k, joined_v = (dot(attn_in, qkv_cols[i]) + bias_j[i] for i in range(3))
    queries = turn(joined_q.reshape(group_rows, heads, HEAD), cosine_table, sine_table).astype(
        jnp.bfloat16
    )
    keys = turn(joined_k.reshape(group_rows, heads, HEAD), cosine_table, sine_table).astype(
        jnp.bfloat16
    )
    values = joined_v.reshape(group_rows, heads, HEAD).astype(jnp.bfloat16)

    scores = (
        jnp.einsum("qhd,khd->hqk", queries, keys, preferred_element_type=jnp.float32) * score_scale
    )
    scores = jnp.where(allowed[None], scores, NEG_LARGE)
    row_max = jnp.max(scores, -1, keepdims=True)
    shifted = jnp.exp(scores - row_max)
    row_total = jnp.sum(shifted, -1, keepdims=True)
    attn_probs = shifted / row_total
    probs_low = attn_probs.astype(jnp.bfloat16)
    mixed = jnp.einsum("hqk,khd->qhd", probs_low, values, preferred_element_type=jnp.float32)
    mixed_low = mixed.reshape(group_rows, wide).astype(jnp.bfloat16)

    branch_sum = (dot(mixed_low, out_weight) + dot(act_low, down_weight)).astype(jnp.bfloat16)
    branch_own = lax.psum_scatter(branch_sum, "shard", scatter_dimension=0, tiled=True)
    rows_f = layer_input.astype(jnp.float32)
    grad_rows = upstream.astype(jnp.float32)
    heads_all = jnp.stack(
        [queries.reshape(group_rows, wide), keys.reshape(group_rows, wide), values.reshape(group_rows, wide)]
    )
    lane = jnp.arange(128, dtype=jnp.int32)[None, :]
    cosine_lanes = jnp.where(lane < ROT, jnp.tile(cosine_table, (1, 128 // ROT)), 1.0)
    sine_lanes = jnp.tile(sine_table, (1, 128 // ROT))
    tables = jnp.stack(
        [
            cosine_lanes,
            jnp.where(lane < ROT // 2, sine_lanes, 0.0),
            jnp.where((lane >= ROT // 2) & (lane < ROT), sine_lanes, 0.0),
        ]
    )
    grads, vector, normed_parts = summed_grads(
        act_low,
        up_all,
        mixed_low,
        mlp_in,
        attn_in,
        slope.astype(jnp.bfloat16),
        down_weight,
        out_weight,
        heads_all,
        rows_all,
        up_cols,
        qkv_cols,
        tables,
        (key_index - positions)[:, None],
        jnp.stack([row_mean, inverse_std_all]),
        jnp.stack([gain_a, gain_m]),
    )
    grads, branch_own = lax.optimization_barrier((grads, branch_own))
    vector = vector.reshape(-1)
    several = hidden // part
    down_grad = widen(grads, several, several, True)
    out_grad = widen(grads, 2 * several, 1, True)
    up_grad = widen(grads, 0, several, False)
    qkv_grad = widen(grads, 2 * several + 1, 3, False)
    layer_output = (rows_f + branch_own.astype(jnp.float32) + (bias_o + bias_d)).astype(jnp.bfloat16)
    normed_own, inverse_std = normalize(rows_f)
    input_grad = grad_rows + norm_backward(
        jnp.sum(normed_parts.astype(jnp.float32), 0), normed_own, inverse_std
    )
    own = lambda i: lax.dynamic_slice_in_dim(vector, i * D + place * part, part, 0)
    bias_grad = own(4)
    qkv_bias_grad = lax.dynamic_slice_in_dim(vector, 5 * D + place * 3 * part, 3 * part, 0)
    up_bias_grad = lax.dynamic_slice_in_dim(vector, 8 * D + place * hidden, hidden, 0)
    return (
        layer_output,
        input_grad,
        own(0),
        own(1),
        qkv_grad,
        qkv_bias_grad,
        out_grad,
        bias_grad,
        own(2),
        own(3),
        up_grad,
        up_bias_grad,
        down_grad,
        bias_grad,
    )


def solution(mesh):
    in_specs = (
        P(("replica", "shard"), None),
        P("shard"),
        P("shard"),
        P("shard", None),
        P("shard"),
        P("shard", None),
        P("shard"),
        P("shard"),
        P("shard"),
        P("shard", None),
        P("shard"),
        P("shard", None),
        P("shard"),
        P("replica", None),
        P(("replica", "shard"), None),
    )
    out_specs = (
        P(("replica", "shard"), None),
        P(("replica", "shard"), None),
        P("shard"),
        P("shard"),
        P("shard", None),
        P("shard"),
        P("shard", None),
        P("shard"),
        P("shard"),
        P("shard"),
        P("shard", None),
        P("shard"),
        P("shard", None),
        P("shard"),
    )
    return jax.shard_map(shards, mesh=mesh, in_specs=in_specs, out_specs=out_specs, check_vma=False)
```

```python
from functools import partial
import math

import jax
import jax.numpy as jnp
from jax import lax
from jax.experimental import pallas as pl
from jax.experimental.pallas import tpu as pltpu
from jax.sharding import PartitionSpec as P

D = 2048
HEADS = 8
HEAD = 256
ROT = 64


EPSILON = 1e-05
ROPE_BASE = 10000.0
NEG_LARGE = -1e30
MESH = pl.DeviceIdType.MESH
CONTRACT_ROWS = (((0,), (0,)), ((), ()))
CONTRACT_COLS = (((1,), (1,)), ((), ()))


def normalize(layer_rows):
    centered = layer_rows - jnp.mean(layer_rows, -1, keepdims=True)
    variance = jnp.mean(centered * centered, -1, keepdims=True)
    inverse_std = lax.rsqrt(variance + EPSILON)
    return (centered * inverse_std, inverse_std)


def norm_backward(grad_normed, normed, inverse_std):
    mean_grad = jnp.mean(grad_normed, -1, keepdims=True)
    mean_cross = jnp.mean(grad_normed * normed, -1, keepdims=True)
    return (grad_normed - mean_grad - normed * mean_cross) * inverse_std


def dot(left, right):
    return jnp.dot(left, right, preferred_element_type=jnp.float32)


def dot_rows(left, right):
    return lax.dot_general(left, right, CONTRACT_ROWS, preferred_element_type=jnp.float32)


def dot_cols(left, right):
    return lax.dot_general(left, right, CONTRACT_COLS, preferred_element_type=jnp.float32)


def bit_of(index, bit):
    return lax.rem(lax.div(index, 1 << bit), 2)


def flip(index, bit):
    return index + (1 << bit) * (1 - 2 * bit_of(index, bit))


def plane_orders(replicas):
    far = list(range(1, replicas.bit_length() - 1))
    return far, far[1:] + far[:1]


def remote(src, dst, sems, at, device):
    return pltpu.make_async_remote_copy(
        src_ref=src,
        dst_ref=dst,
        send_sem=sems.at[(0,) + at],
        recv_sem=sems.at[(1,) + at],
        device_id=device,
        device_id_type=MESH,
    )


def greet(rep, place, replicas, shards_n):
    barrier = pltpu.get_barrier_semaphore()
    bits = replicas.bit_length() - 1
    for bit in range(bits):
        pl.semaphore_signal(
            barrier, inc=1, device_id={"replica": flip(rep, bit)}, device_id_type=MESH
        )
    for step in range(1, shards_n):
        pl.semaphore_signal(
            barrier,
            inc=1,
            device_id={"shard": lax.rem(place + step, shards_n)},
            device_id_type=MESH,
        )
    pl.semaphore_wait(barrier, bits + shards_n - 1)


TILE = 256


def causal_probs(query, key, first, row):
    shape = (query.shape[0], key.shape[0])
    scores = dot_cols(query, key) * (1.0 / math.sqrt(HEAD))
    at = lax.broadcasted_iota(jnp.int32, shape, 1)
    upto = lax.broadcasted_iota(jnp.int32, shape, 0) + row
    scores = jnp.where((at >= first) & (at <= upto), scores, NEG_LARGE)
    shifted = jnp.exp(scores - jnp.max(scores, -1, keepdims=True))
    return shifted / jnp.sum(shifted, -1, keepdims=True)


def forward_kernel(
    replicas,
    shards_n,
    small_ref,
    up_ref,
    qkv_ref,
    x_ref,
    g_ref,
    down_ref,
    proj_ref,
    bias_ref,
    tables_ref,
    first_ref,
    small_out,
    up_out,
    qkv_out,
    x_out,
    g_out,
    mlp_out,
    attn_out,
    act_out,
    slope_out,
    heads_out,
    mixed_out,
    branch_out,
    stats_out,
    small_low,
    small,
    x_rows,
    mlp,
    attn,
    up,
    qkv,
    act,
    slope,
    heads,
    mixed,
    down,
    proj,
    branch,
    own_sem,
    load_sem,
    keep_sem,
    small_sem,
    turn_sem,
    plane_sem,
    hop_sem,
    g_sem,
):
    rep, place = lax.axis_index("replica"), lax.axis_index("shard")
    bits = replicas.bit_length() - 1
    width, hidden = up_out.shape
    part = width // shards_n
    wide = qkv_out.shape[2]
    rows = part // replicas
    tokens = x_out.shape[0]
    local = tokens // shards_n
    cols = down.shape[2]
    orders = [order + [0] for order in plane_orders(replicas)]
    starts = []
    for order in orders:
        start = 0
        for level, bit in enumerate(order):
            start = start + bit_of(rep, bit) * (rows << level)
        starts.append(start)

    items = [(thing, step) for thing in range(4) for step in range(1, shards_n)]

    def source(thing, shard, path):
        some = pl.ds(pl.multiple_of(starts[path], rows), rows)
        if thing == 0:
            at = shard * hidden + path * (hidden // 2)
            return up_ref.at[some, pl.ds(pl.multiple_of(at, 128), hidden // 2)]
        at = (thing - 1) * width + shard * wide + path * (wide // 2)
        return qkv_ref.at[some, pl.ds(pl.multiple_of(at, 128), wide // 2)]

    def target(thing, shard, start, count, path):
        some = pl.ds(pl.multiple_of(shard * part + start, rows), count)
        if thing == 0:
            return up_out.at[some, pl.ds(path * (hidden // 2), hidden // 2)]
        return qkv_out.at[thing - 1, some, pl.ds(path * (wide // 2), wide // 2)]

    def turned(item, path, sending):
        thing, step = items[item]
        to = lax.rem(place + step, shards_n)
        shard = place if sending else lax.rem(place - step + shards_n, shards_n)
        return remote(
            source(thing, to, path),
            target(thing, shard, starts[path], rows, path),
            turn_sem,
            (item, path),
            {"shard": to},
        )

    def spread(item, path, level):
        thing, step = items[item]
        shard = lax.rem(place - step + shards_n, shards_n)
        order = orders[path]
        start = 0
        for above in range(level, bits):
            start = start + bit_of(rep, order[above]) * (rows << above)
        here = target(thing, shard, start, rows << level, path)
        return remote(
            here, here, plane_sem, (item, path, level), {"replica": flip(rep, order[level])}
        )

    def small_copy(step, sending):
        to = lax.rem(place + step, shards_n)
        shard = place if sending else lax.rem(place - step + shards_n, shards_n)
        return remote(small_ref, small_out.at[shard], small_sem, (step,), {"shard": to})

    def column_tick(tick):
        for level in reversed(range(bits + 1)):
            item = tick - level
            if not 0 <= item < len(items):
                continue
            for path in range(2):
                if level == 0:
                    turned(item, path, False).wait_recv()
                else:
                    spread(item, path, level - 1).wait_recv()
                if level < bits:
                    spread(item, path, level).start()

    def block_rows(block):
        return pl.ds(pl.multiple_of(block * local, local), local)

    def hop(way, step, sending):
        sign = 1 - 2 * way
        block = place - sign * (step if sending else step + 1)
        there = x_out.at[block_rows(block), :]
        return remote(
            x_ref if sending and step == 0 else there,
            there,
            hop_sem,
            (way, step),
            {"shard": lax.rem(place + sign + shards_n, shards_n)},
        )

    def upstream_copy(step, sending):
        to = lax.rem(place + step, shards_n)
        shard = place if sending else lax.rem(place - step + shards_n, shards_n)
        return remote(g_ref, g_out.at[block_rows(shard), :], g_sem, (step,), {"shard": to})

    def holds(way, step):
        return place >= step if way == 0 else place + step < shards_n

    def goes(way, step):
        onward = place + 1 < shards_n if way == 0 else place >= 1
        return holds(way, step) & onward

    def send_hop(step):
        for way in range(2):

            @pl.when(goes(way, step))
            def _():
                hop(way, step, True).start()

    def pass_on(step):
        for way in range(2):

            @pl.when(holds(way, step))
            def _():
                hop(way, step - 1, False).wait_recv()

        if step + 1 < shards_n:
            send_hop(step)

    def load(number, src, dst):
        return pltpu.make_async_copy(src, dst, load_sem.at[number])

    def keep(number, src, dst):
        return pltpu.make_async_copy(src, dst, keep_sem.at[number])

    def norm(block, from_ref, slot):
        copy = load(slot, from_ref, x_rows.at[slot])
        copy.start()
        copy.wait()

        def some_rows(i, carry):
            here = pl.ds(pl.multiple_of(i * 32, 32), 32)
            there = pl.ds(pl.multiple_of(block * local + i * 32, 32), 32)
            values = x_rows[slot, here, :].astype(jnp.float32)
            mean = jnp.mean(values, -1, keepdims=True)
            centered = values - mean
            scale = lax.rsqrt(jnp.mean(centered * centered, -1, keepdims=True) + EPSILON)
            stats_out[0, there, :] = mean
            stats_out[1, there, :] = scale
            normed = centered * scale
            for z in range(shards_n):
                lanes = slice(z * part, (z + 1) * part)
                some = normed[:, lanes]
                attn[there, lanes] = (some * small[z, 0:1, :] + small[z, 1:2, :]).astype(jnp.bfloat16)
                mlp[there, lanes] = (some * small[z, 3:4, :] + small[z, 4:5, :]).astype(jnp.bfloat16)
            return carry

        lax.fori_loop(0, local // 32, some_rows, 0)

    def hidden_units(block):
        here = block_rows(block)

        def some_cols(k, carry):
            lanes = pl.ds(pl.multiple_of(k * cols, cols), cols)
            found = dot(mlp[here, :], up[:, lanes]) + bias_ref[0:1, lanes]
            cdf = 0.5 * (1.0 + lax.erf(found * math.sqrt(0.5)))
            act[here, lanes] = (found * cdf).astype(jnp.bfloat16)
            bell = jnp.exp(-0.5 * found * found) * (1.0 / math.sqrt(2.0 * math.pi))
            slope[here, lanes] = (cdf + found * bell).astype(jnp.bfloat16)
            return carry

        lax.fori_loop(0, hidden // cols, some_cols, 0)

    def on_step(step, todo):
        for way in range(2):
            if step == 0 and way == 1:
                continue
            block = place - (1 - 2 * way) * step

            @pl.when(holds(way, step))
            def _():
                todo(block, way)

    def project(third):
        number = third * shards_n + place
        bias = small[lax.div(number, 3), pl.ds(6 + lax.rem(number, 3), 1), :]

        def some_rows(i, carry):
            here = pl.ds(pl.multiple_of(i * TILE, TILE), TILE)
            found = dot(attn[here, :], qkv[third]) + bias
            for head in range(wide // HEAD):
                mine = found[:, head * HEAD : (head + 1) * HEAD]
                if third < 2:
                    lead = mine[:, :128]
                    lead = (
                        lead * tables_ref[0, here, :]
                        - pltpu.roll(lead, 96, 1) * tables_ref[1, here, :]
                        + pltpu.roll(lead, 32, 1) * tables_ref[2, here, :]
                    )
                    mine = jnp.concatenate([lead, mine[:, 128:]], 1)
                heads[third, here, head * HEAD : (head + 1) * HEAD] = mine.astype(jnp.bfloat16)
            return carry

        lax.fori_loop(0, tokens // TILE, some_rows, 0)

    def attend(head):
        lanes = slice(head * HEAD, (head + 1) * HEAD)
        for i in range(tokens // TILE):
            here, keys = slice(i * TILE, (i + 1) * TILE), slice(0, (i + 1) * TILE)
            probs = causal_probs(heads[0, here, lanes], heads[1, keys, lanes], first_ref[here, :], i * TILE)
            mixed[here, lanes] = dot(probs.astype(jnp.bfloat16), heads[2, keys, lanes]).astype(jnp.bfloat16)

    def down_load(j):
        return load(4 + j % 2, down_ref.at[:, pl.ds(j * cols, cols)], down.at[j % 2])

    def branch_keep(j):
        return keep(6 + j, branch.at[j % 2], branch_out.at[:, pl.ds(j * cols, cols)])

    def branch_cols(j):
        down_load(j).wait()
        if j >= 2:
            branch_keep(j - 2).wait()

        def some_rows(i, carry):
            here = pl.ds(pl.multiple_of(i * TILE, TILE), TILE)
            found = dot(act[here, :], down[j % 2]) + dot(mixed[here, :], proj[:, j * cols : (j + 1) * cols])
            branch[j % 2, here, :] = found.astype(jnp.bfloat16)
            return carry

        lax.fori_loop(0, tokens // TILE, some_rows, 0)
        branch_keep(j).start()
        if j + 2 < width // cols:
            down_load(j + 2).start()

    greet(rep, place, replicas, shards_n)
    for step in range(1, shards_n):
        small_copy(step, True).start()
    send_hop(0)
    for item in range(shards_n - 1):
        for path in range(2):
            turned(item, path, True).start()
    own = [
        (small_ref, small_out.at[place]),
        (
            up_ref.at[:, pl.ds(pl.multiple_of(place * hidden, 128), hidden)],
            up_out.at[pl.ds(pl.multiple_of(place * part, part), part), :],
        ),
        (x_ref, x_out.at[block_rows(place), :]),
        (g_ref, g_out.at[block_rows(place), :]),
    ] + [
        (
            qkv_ref.at[:, pl.ds(pl.multiple_of(third * width + place * wide, 128), wide)],
            qkv_out.at[third, pl.ds(pl.multiple_of(place * part, part), part), :],
        )
        for third in range(3)
    ]
    own = [pltpu.make_async_copy(src, dst, own_sem.at[i]) for i, (src, dst) in enumerate(own)]
    for copy in own:
        copy.start()
    down_load(0).start()
    down_load(1).start()
    load_proj = load(6, proj_ref, proj)
    load_proj.start()

    for step in range(1, shards_n):
        small_copy(step, False).wait()
    own[0].wait()
    load_small = load(0, small_out, small_low)
    load_small.start()
    load_small.wait()
    small[...] = small_low[...].astype(jnp.float32)
    on_step(0, lambda block, way: norm(block, x_ref, way))

    load_up = load(2, up_out, up)
    load_qkv = load(3, qkv_out, qkv)
    ticks = list(range(len(items) + bits))

    def some_ticks(number):
        for tick in ticks[:number]:
            column_tick(tick)
        del ticks[:number]

    def arrive(step):
        pass_on(step)
        if step == 1:
            for item in range(shards_n - 1, len(items)):
                for path in range(2):
                    turned(item, path, True).start()
        if step == max(shards_n - 2, 1):
            for other in range(1, shards_n):
                upstream_copy(other, True).start()
        on_step(step, lambda block, way: norm(block, x_out.at[block_rows(block), :], way))

    arrive(1)
    some_ticks(shards_n - 1 + bits)
    own[1].wait()
    load_up.start()
    for step in range(2, shards_n):
        arrive(step)
        some_ticks(2)
        if step == 2:
            load_up.wait()
        on_step(step - 2, lambda block, way: hidden_units(block))
    keeps = [keep(0, mlp, mlp_out), keep(1, attn, attn_out)]
    keeps[0].start()
    keeps[1].start()
    for step in range(shards_n - 2, shards_n):
        some_ticks(2)
        on_step(step, lambda block, way: hidden_units(block))
    some_ticks(len(ticks))
    for copy in own[4:]:
        copy.wait()
    load_qkv.start()
    keeps += [keep(2, act, act_out), keep(3, slope, slope_out)]
    keeps[2].start()
    keeps[3].start()
    load_qkv.wait()
    for third in range(3):
        project(third)
    keeps.append(keep(4, heads, heads_out))
    keeps[4].start()
    for head in range(wide // HEAD):
        attend(head)
    keeps.append(keep(5, mixed, mixed_out))
    keeps[5].start()
    load_proj.wait()
    for j in range(width // cols):
        branch_cols(j)
    for step in range(1, shards_n):
        upstream_copy(step, False).wait()
    for j in range(max(width // cols - 2, 0), width // cols):
        branch_keep(j).wait()
    for copy in keeps:
        copy.wait()
    for item in range(len(items)):
        for path in range(2):
            turned(item, path, True).wait_send()
            for level in range(bits):
                spread(item, path, level).wait_send()
    for step in range(shards_n - 1):
        for way in range(2):

            @pl.when(goes(way, step))
            def _():
                hop(way, step, True).wait_send()

    for copy in own[2:4]:
        copy.wait()


def forward(small, up_weight, qkv_weight, x, g, down_weight, proj_weight, bias, tables, first):
    replicas, count = lax.axis_size("replica"), lax.axis_size("shard")
    bits = replicas.bit_length() - 1
    local, width = x.shape
    tokens = local * count
    hidden, wide = up_weight.shape[1] // count, width // count
    cols = wide
    items = 4 * (count - 1)
    any_spec = pl.BlockSpec(memory_space=pl.ANY)
    vmem_spec = pl.BlockSpec(memory_space=pltpu.VMEM)
    shapes = dict(
        small=(count,) + small.shape,
        up_cols=(width, hidden),
        qkv_cols=(3, width, wide),
        x=(tokens, width),
        g=(tokens, width),
        mlp_in=(tokens, width),
        attn_in=(tokens, width),
        act=(tokens, hidden),
        slope=(tokens, hidden),
        heads=(3, tokens, wide),
        mixed=(tokens, wide),
        branch=(tokens, width),
    )
    low = lambda *shape: pltpu.VMEM(shape, jnp.bfloat16)
    dma = lambda *shape: pltpu.SemaphoreType.DMA(shape)
    found = pl.pallas_call(
        partial(forward_kernel, replicas, count),
        out_shape=tuple(jax.ShapeDtypeStruct(shape, jnp.bfloat16) for shape in shapes.values())
        + (jax.ShapeDtypeStruct((2, tokens, 1), jnp.float32),),
        in_specs=[any_spec] * 7 + [vmem_spec] * 3,
        out_specs=(any_spec,) * len(shapes) + (vmem_spec,),
        scratch_shapes=[
            low(*shapes["small"]),
            pltpu.VMEM(shapes["small"], jnp.float32),
            low(2, local, width),
            low(tokens, width),
            low(tokens, width),
            low(width, hidden),
            low(3, width, wide),
            low(tokens, hidden),
            low(tokens, hidden),
            low(3, tokens, wide),
            low(tokens, wide),
            low(2, hidden, cols),
            low(wide, width),
            low(2, tokens, cols),
            dma(7),
            dma(7),
            dma(6 + width // cols),
            dma(2, count),
            dma(2, items, 2),
            dma(2, items, 2, bits),
            dma(2, 2, count - 1),
            dma(2, count),
        ],
        compiler_params=pltpu.CompilerParams(
            collective_id=0, has_side_effects=True, vmem_limit_bytes=58 * 2**20
        ),
        cost_estimate=pl.CostEstimate(
            flops=2 * tokens * width * (hidden * 2 + wide * 4),
            bytes_accessed=500_000_000,
            transcendentals=0,
        ),
    )(small, up_weight, qkv_weight, x, g, down_weight, proj_weight, bias, tables, first)
    return dict(zip(list(shapes) + ["stats"], found))


RING = 3


def grads_kernel(
    replicas,
    shards_n,
    act_ref,
    up_ref,
    mixed_ref,
    mlp_ref,
    attn_ref,
    slope_ref,
    down_ref,
    proj_ref,
    heads_ref,
    rows_ref,
    cols_up_ref,
    cols_qkv_ref,
    tables_ref,
    first_ref,
    stats_ref,
    small_ref,
    out_ref,
    vec_out,
    sum_out,
    work,
    from_core,
    *rest,
):
    rep, place = lax.axis_index("replica"), lax.axis_index("shard")
    bits = replicas.bit_length() - 1
    far = bits - 1
    from_far = rest[:far]
    (
        big,
        narrow,
        pre,
        joined,
        wide_rows,
        slope,
        heads,
        key_sum,
        value_sum,
        tile_x,
        tile_up,
        tile_qkv,
        shared,
        vec_got,
        vec_sum,
        load_sem,
        core_sem,
        far_sem,
        turn_sem,
        own_sem,
        plane_sem,
        vec_sem,
        sum_sem,
    ) = rest[far:]
    chunks, _, rows, cols = out_ref.shape
    slots = work.shape[0]
    half, side = rows // 2, cols // 2
    piece = rows // replicas
    orders = plane_orders(replicas)
    core = bit_of(rep, 0)
    tokens, width = up_ref.shape
    local = tokens // shards_n
    hiddens = pre.shape[0]
    natives = hiddens + 1
    mine = pl.multiple_of(core * half, half)
    theirs = pl.multiple_of((1 - core) * half, half)

    starts = []
    for order in orders:
        line, size = [core * half], half
        for bit in order:
            size //= 2
            line.append(line[-1] + bit_of(rep, bit) * size)
        starts.append(line)

    def spot(k):
        if k < natives:
            return k + hiddens
        return k - natives if k < natives + hiddens else k

    def load(source, target, number):
        return pltpu.make_async_copy(source, target, load_sem.at[number])

    def narrow_load(k):
        source = act_ref.at[:, pl.ds(k * cols, cols)] if k < hiddens else mixed_ref
        return load(source, narrow.at[k % 2], k % 2)

    def big_load(which):
        return load((up_ref, mlp_ref, attn_ref)[which], big.at[which % 2], 2 + which)

    def down_load(k):
        return load(down_ref.at[pl.ds(k * cols, cols), :], wide_rows.at[k % 2], 5 + k % 2)

    def slope_load(k):
        return load(slope_ref.at[:, pl.ds(k * cols, cols)], slope.at[k % 2], 7 + k % 2)

    def pre_loads(k):
        return [down_load(k), slope_load(k)]

    def proj_load():
        return load(proj_ref, wide_rows.at[1], 6)

    def heads_load():
        return load(heads_ref, heads.at[pl.ds(0, 3)], 9)

    def tile_loads(j):
        some = pl.ds(j * TILE, TILE)
        return [
            load(rows_ref.at[:, some], tile_x.at[j % 2], 10 + j % 2),
            load(cols_up_ref.at[some, :], tile_up.at[j % 2], 12 + j % 2),
            load(cols_qkv_ref.at[:, some, :], tile_qkv.at[j % 2], 14 + j % 2),
        ]

    def to_core(k):
        return remote(
            work.at[k % slots, :, pl.ds(theirs, half), :],
            from_core.at[k % RING],
            core_sem,
            (0, k),
            {"replica": flip(rep, 0)},
        )

    def to_far(k, level, path):
        size = half >> (level + 1)
        bit = orders[path][level]
        start = starts[path][level] + (1 - bit_of(rep, bit)) * size
        return remote(
            work.at[k % slots, :, pl.ds(pl.multiple_of(start, size), size), pl.ds(path * side, side)],
            from_far[level].at[k % RING, path],
            far_sem,
            (k, level, path),
            {"replica": flip(rep, bit)},
        )

    def own_piece(k, path, block):
        return work.at[
            k % slots,
            block,
            pl.ds(pl.multiple_of(starts[path][far], piece), piece),
            pl.ds(path * side, side),
        ]

    def place_piece(k, path, block):
        return out_ref.at[
            spot(k),
            block,
            pl.ds(pl.multiple_of(starts[path][far], piece), piece),
            pl.ds(path * side, side),
        ]

    def settle(k, path):
        block = pl.ds(0, shards_n) if k < natives else place
        return pltpu.make_async_copy(
            own_piece(k, path, block), place_piece(k, path, block), own_sem.at[k % 2, path]
        )

    def turned(k, path, step, sending):
        to = lax.rem(place + step, shards_n)
        shard = place if sending else lax.rem(place - step + shards_n, shards_n)
        return remote(
            own_piece(k, path, to),
            place_piece(k, path, shard),
            turn_sem,
            (k - natives, path, step - 1),
            {"shard": to},
        )

    def spread(k, path, level):
        size = piece << level
        bit = orders[path][far - 1 - level]
        here = out_ref.at[
            spot(k),
            :,
            pl.ds(pl.multiple_of(starts[path][far - level], size), size),
            pl.ds(path * side, side),
        ]
        return remote(here, here, plane_sem, (k, level, path), {"replica": flip(rep, bit)})

    def spread_core(k):
        here = out_ref.at[spot(k), :, pl.ds(mine, half), :]
        return remote(here, here, core_sem, (1, k), {"replica": flip(rep, 0)})

    def put(offset, sums):
        for i in range(sums.shape[1] // 128):
            vec_sum[pl.ds(offset // 128 + i, 1), :] = sums[:, i * 128 : (i + 1) * 128]

    def compute(k):
        if k < natives:
            narrow_load(k).wait()
            if k + 1 < natives:
                narrow_load(k + 1).start()
        if k == 0:
            big_load(0).wait()
        if k == natives:
            big_load(1).wait()
            big_load(2).start()
        if k == natives + hiddens:
            big_load(2).wait()
        slot = k % slots
        which = 1 if natives <= k < natives + hiddens else 0

        for begin, send in ((theirs, True), (mine, False)):

            def block(g, carry):
                if k < natives:
                    left = narrow[k % 2, :, pl.ds(begin, half)]
                    right = big[which, :, pl.ds(pl.multiple_of(g * cols, cols), cols)]
                else:
                    left = big[which, :, pl.ds(pl.multiple_of(g * rows + begin, half), half)]
                    if k < natives + hiddens:
                        right = pre[k - natives]
                    else:
                        right = joined[k - natives - hiddens]
                work[slot, g, pl.ds(begin, half), :] = dot_rows(left, right).astype(jnp.bfloat16)
                return carry

            lax.fori_loop(0, shards_n, block, 0)
            if send:
                to_core(k).start()

    def add(k, start, size, left, width, got):
        def block(g, carry):
            where = (k % slots, g, pl.ds(pl.multiple_of(start, size), size), pl.ds(left, width))
            work[where] = (
                work[where].astype(jnp.float32) + got(g).astype(jnp.float32)
            ).astype(jnp.bfloat16)
            return carry

        lax.fori_loop(0, shards_n, block, 0)

    def grad_mixed():
        proj_load().wait()

        def block(i, carry):
            some = pl.ds(pl.multiple_of(i * TILE, TILE), TILE)
            heads[3, some, :] = dot_cols(big[0, some, :], wide_rows[1]).astype(jnp.bfloat16)
            return carry

        lax.fori_loop(0, tokens // TILE, block, 0)
        down_load(1).start()
        own = pl.ds(pl.multiple_of(place * cols, cols), cols)
        put(4 * width + place * cols, jnp.sum(big[0, :, own].astype(jnp.float32), 0, keepdims=True))

    def grad_pre(k):
        for copy in pre_loads(k):
            copy.wait()

        def block(i, total):
            some = pl.ds(pl.multiple_of(i * TILE, TILE), TILE)
            found = dot_cols(big[0, some, :], wide_rows[k % 2]) * slope[k % 2, some, :].astype(
                jnp.float32
            )
            low = found.astype(jnp.bfloat16)
            pre[k, some, :] = low
            return total + jnp.sum(low.astype(jnp.float32), 0, keepdims=True)

        total = lax.fori_loop(0, tokens // TILE, block, jnp.zeros((1, cols), jnp.float32))
        put(8 * width + (place * hiddens + k) * cols, total)
        if k + 2 < hiddens:
            for copy in pre_loads(k + 2):
                copy.start()

    def turn_rows(found, some):
        lead = found[:, :128]
        lead = (
            lead * tables_ref[0, some, :]
            + pltpu.roll(lead, 96, 1) * tables_ref[1, some, :]
            - pltpu.roll(lead, 32, 1) * tables_ref[2, some, :]
        )
        return jnp.concatenate([lead, found[:, 128:]], 1)

    def attention(head):
        lanes = pl.ds(head * HEAD, HEAD)
        scale = 1.0 / math.sqrt(HEAD)
        key_sum[...] = jnp.zeros_like(key_sum)
        value_sum[...] = jnp.zeros_like(value_sum)
        sums = [jnp.zeros((1, HEAD), jnp.float32)] * 3
        for i in range(tokens // TILE):
            some, keys = pl.ds(i * TILE, TILE), pl.ds(0, (i + 1) * TILE)
            query = heads[0, some, lanes]
            key = heads[1, keys, lanes]
            probs = causal_probs(query, key, first_ref[some, :], i * TILE)
            grad = heads[3, some, lanes]
            grad_probs = dot_cols(grad, heads[2, keys, lanes])
            delta = jnp.sum(probs * grad_probs, -1, keepdims=True)
            low = (probs * (grad_probs - delta)).astype(jnp.bfloat16)
            found = turn_rows(dot(low, key) * scale, some).astype(jnp.bfloat16)
            joined[0, some, lanes] = found
            sums[0] = sums[0] + jnp.sum(found.astype(jnp.float32), 0, keepdims=True)
            key_sum[keys, :] = key_sum[keys, :] + dot_rows(low, query)
            value_sum[keys, :] = value_sum[keys, :] + dot_rows(probs.astype(jnp.bfloat16), grad)
        for i in range(tokens // TILE):
            some = pl.ds(i * TILE, TILE)
            for third, found in (
                (1, turn_rows(key_sum[some, :] * scale, some)),
                (2, value_sum[some, :]),
            ):
                low = found.astype(jnp.bfloat16)
                joined[third, some, lanes] = low
                sums[third] = sums[third] + jnp.sum(low.astype(jnp.float32), 0, keepdims=True)
        for third in range(3):
            put(5 * width + third * width + place * cols + head * HEAD, sums[third])

    def sum_part(j, step, sending):
        to = lax.rem(place + step, shards_n)
        shard = place if sending else lax.rem(place - step + shards_n, shards_n)
        some = pl.ds(j * TILE, TILE)
        source = shared.at[pl.ds(pl.multiple_of(to * local, local), local), some]
        if step == 0:
            return pltpu.make_async_copy(source, sum_out.at[place, :, some], sum_sem.at[0, j, 0])
        return remote(source, sum_out.at[shard, :, some], sum_sem, (j, step), {"shard": to})

    def tile(j):
        for copy in tile_loads(j):
            copy.wait()
        if j + 1 < width // TILE:
            for copy in tile_loads(j + 1):
                copy.start()
        lanes = pl.ds(j * TILE, TILE)
        owner, begin = divmod(j * TILE, cols)
        theirs_at = slice(begin, begin + TILE)

        def block(i, totals):
            some = pl.ds(pl.multiple_of(i * local, local), local)
            normed = (tile_x[j % 2, some, :].astype(jnp.float32) - stats_ref[0, some, :]) * stats_ref[
                1, some, :
            ]
            mlp = sum(
                dot_cols(pre[k, some, :], tile_up[j % 2, :, k * cols : (k + 1) * cols])
                for k in range(hiddens)
            )
            attn = sum(dot_cols(joined[p, some, :], tile_qkv[j % 2, p]) for p in range(3))
            shared[some, lanes] = (
                attn * small_ref[owner, 0:1, theirs_at].astype(jnp.float32)
                + mlp * small_ref[owner, 3:4, theirs_at].astype(jnp.float32)
            ).astype(jnp.bfloat16)
            found = (attn * normed, attn, mlp * normed, mlp)
            return tuple(t + jnp.sum(f, 0, keepdims=True) for t, f in zip(totals, found))

        zero = jnp.zeros((1, TILE), jnp.float32)
        totals = lax.fori_loop(0, shards_n, block, (zero,) * 4)
        for number, total in enumerate(totals):
            put(number * width + j * TILE, total)
        for step in range(shards_n):
            sum_part(j, step, True).start()

    def stage(k, number):
        if number == 0:
            compute(k)
        elif number == 1:
            to_core(k).wait()
            add(k, mine, half, 0, cols, lambda g: from_core[k % RING, g])
            for path in range(2):
                to_far(k, 0, path).start()
        elif number <= 1 + far:
            level = number - 2
            for path in range(2):
                to_far(k, level, path).wait()
                size = half >> (level + 1)
                add(
                    k,
                    starts[path][level + 1],
                    size,
                    path * side,
                    side,
                    lambda g: from_far[level][k % RING, path, g],
                )
                if level + 1 < far:
                    to_far(k, level + 1, path).start()
                else:
                    if k >= natives:
                        for step in range(1, shards_n):
                            turned(k, path, step, True).start()
                    settle(k, path).start()
        elif number == 2 + far:
            for path in range(2):
                settle(k, path).wait()
                if k >= natives:
                    for step in range(1, shards_n):
                        turned(k, path, step, False).wait_recv()
                spread(k, path, 0).start()
            if k >= natives:
                for path in range(2):
                    for step in range(1, shards_n):
                        turned(k, path, step, True).wait_send()
        elif number <= 2 + 2 * far:
            level = number - 3 - far
            for path in range(2):
                spread(k, path, level).wait()
                if level + 1 < far:
                    spread(k, path, level + 1).start()
            if level + 1 == far:
                spread_core(k).start()
        else:
            spread_core(k).wait()

    stages = 4 + 2 * far
    n_heads, n_tiles = cols // HEAD, width // TILE
    extras = {0: [grad_mixed, lambda: grad_pre(0)]}
    for k in range(1, hiddens):
        extras.setdefault(k, []).append(partial(grad_pre, k))
    for head in range(n_heads):
        extras.setdefault(1 + head, []).append(partial(attention, head))
    tile_at = hiddens + 1
    for j in range(n_tiles):
        extras.setdefault(tile_at + j, []).append(partial(tile, j))
    vec_at = tile_at + n_tiles

    for copy in [narrow_load(0), big_load(0), proj_load()] + pre_loads(0):
        copy.start()
    slope_load(1).start()
    for copy in [heads_load(), big_load(1)] + tile_loads(0):
        copy.start()
    vec_sum[...] = jnp.zeros_like(vec_sum)
    greet(rep, place, replicas, shards_n)
    peers = [{"replica": flip(rep, bit)} for bit in range(bits)]
    peers += [{"shard": flip(place, bit)} for bit in range(shards_n.bit_length() - 1)]

    def vec_copy(number):
        return remote(vec_sum, vec_got.at[number], vec_sem, (number,), peers[number])

    for tick in range(max(chunks + stages - 1, vec_at + len(peers) + 1)):
        for number in reversed(range(stages)):
            if 0 <= tick - number < chunks:
                stage(tick - number, number)
        if tick == 1:
            heads_load().wait()
        for extra in extras.get(tick, []):
            extra()
        turn_of = tick - vec_at
        if 0 < turn_of <= len(peers):
            vec_copy(turn_of - 1).wait()
            vec_sum[...] = vec_sum[...] + vec_got[turn_of - 1]
        if 0 <= turn_of < len(peers):
            vec_copy(turn_of).start()
    vec_out[...] = vec_sum[...]
    for j in range(n_tiles):
        for step in range(shards_n):
            sum_part(j, step, False).wait()


def summed_grads(*operands):
    act, up, mixed, mlp_in = operands[:4]
    replicas, count = lax.axis_size("replica"), lax.axis_size("shard")
    bits = replicas.bit_length() - 1
    far = bits - 1
    tokens, width = up.shape
    cols = width // count
    hidden = act.shape[1]
    hiddens = hidden // cols
    natives = hiddens + 1
    chunks = natives + hiddens + 3
    peers = bits + count.bit_length() - 1
    slots = 2 + far
    vector = ((8 * width + count * hidden) // 128, 128)
    any_spec = pl.BlockSpec(memory_space=pl.ANY)
    vmem_spec = pl.BlockSpec(memory_space=pltpu.VMEM)
    low = lambda *shape: pltpu.VMEM(shape, jnp.bfloat16)
    full = lambda *shape: pltpu.VMEM(shape, jnp.float32)
    dma = lambda *shape: pltpu.SemaphoreType.DMA(shape)
    return pl.pallas_call(
        partial(grads_kernel, replicas, count),
        out_shape=(
            jax.ShapeDtypeStruct((chunks, count, cols, cols), jnp.bfloat16),
            jax.ShapeDtypeStruct(vector, jnp.float32),
            jax.ShapeDtypeStruct((count, tokens // count, width), jnp.bfloat16),
        ),
        in_specs=[any_spec] * 12 + [vmem_spec] * 4,
        out_specs=(any_spec, vmem_spec, any_spec),
        scratch_shapes=[
            low(slots, count, cols, cols),
            low(RING, count, cols // 2, cols),
        ]
        + [low(RING, 2, count, cols >> (level + 2), cols // 2) for level in range(far)]
        + [
            low(2, tokens, width),
            low(2, tokens, cols),
            low(hiddens, tokens, cols),
            low(3, tokens, cols),
            low(2, cols, width),
            low(2, tokens, cols),
            low(4, tokens, cols),
            full(tokens, HEAD),
            full(tokens, HEAD),
            low(2, tokens, TILE),
            low(2, TILE, hidden),
            low(2, 3, TILE, cols),
            low(tokens, width),
            full(peers, *vector),
            full(*vector),
            dma(16),
            dma(2, 2, chunks),
            dma(2, chunks, far, 2),
            dma(2, chunks - natives, 2, count - 1),
            dma(2, 2),
            dma(2, chunks, far, 2),
            dma(2, peers),
            dma(2, width // TILE, count),
        ],
        compiler_params=pltpu.CompilerParams(
            collective_id=1, has_side_effects=True, vmem_limit_bytes=60 * 2**20
        ),
        cost_estimate=pl.CostEstimate(
            flops=4 * tokens * chunks * count * cols * cols,
            bytes_accessed=600_000_000,
            transcendentals=0,
        ),
    )(*operands)


def last_kernel(
    up_blocks,
    down_blocks,
    out_blocks,
    qkv_blocks,
    parts_ref,
    branch_ref,
    x_ref,
    g_ref,
    small_ref,
    layer_out,
    input_out,
    up_out,
    down_out,
    out_out,
    qkv_out,
):
    number, count, _, cols = up_blocks.shape
    for g in range(count):
        lanes = slice(g * cols, (g + 1) * cols)
        for k in range(number):
            at = (g * number + k) * cols
            up_out[:, at : at + cols] = up_blocks[k, g].astype(jnp.float32)
        for k in range(3):
            at = (k * count + g) * cols
            qkv_out[:, at : at + cols] = qkv_blocks[k, g].astype(jnp.float32)
        down_out[:, lanes] = down_blocks[0, g].astype(jnp.float32)
        out_out[:, lanes] = out_blocks[0, g].astype(jnp.float32)
    rows = x_ref[...].astype(jnp.float32)
    normed, inverse_std = normalize(rows)
    grad = sum(parts_ref[g].astype(jnp.float32) for g in range(count))
    input_out[...] = g_ref[...].astype(jnp.float32) + norm_backward(grad, normed, inverse_std)
    for g in range(count):
        lanes = slice(g * cols, (g + 1) * cols)
        bias = small_ref[g, 2:3, :].astype(jnp.float32) + small_ref[g, 5:6, :].astype(jnp.float32)
        layer_out[:, lanes] = (
            rows[:, lanes] + branch_ref[:, lanes].astype(jnp.float32) + bias
        ).astype(jnp.bfloat16)


def last(blocks, parts, branch, x, g, small):
    count, rows, cols = blocks.shape[1:]
    number = (blocks.shape[0] - 4) // 2
    local, width = x.shape
    steps = local // 16
    some, tall = rows // steps, number * rows // steps
    turns = rows // tall
    whole = lambda i: (i, 0)
    return pl.pallas_call(
        last_kernel,
        out_shape=(
            jax.ShapeDtypeStruct((local, width), jnp.bfloat16),
            jax.ShapeDtypeStruct((local, width), jnp.float32),
            jax.ShapeDtypeStruct((rows, number * width), jnp.float32),
            jax.ShapeDtypeStruct((number * rows, width), jnp.float32),
            jax.ShapeDtypeStruct((rows, width), jnp.float32),
            jax.ShapeDtypeStruct((rows, 3 * width), jnp.float32),
        ),
        grid=(steps,),
        in_specs=[
            pl.BlockSpec((number, count, some, cols), lambda i: (0, 0, i, 0)),
            pl.BlockSpec((1, count, tall, cols), lambda i: (number + i // turns, 0, i % turns, 0)),
            pl.BlockSpec((1, count, some, cols), lambda i: (2 * number, 0, i, 0)),
            pl.BlockSpec((3, count, some, cols), lambda i: ((2 * number + 1) // 3, 0, i, 0)),
            pl.BlockSpec((count, 16, width), lambda i: (0, i, 0)),
            pl.BlockSpec((16, width), whole),
            pl.BlockSpec((16, width), whole),
            pl.BlockSpec((16, width), whole),
            pl.BlockSpec(small.shape, lambda i: (0, 0, 0)),
        ],
        out_specs=(
            pl.BlockSpec((16, width), whole),
            pl.BlockSpec((16, width), whole),
            pl.BlockSpec((some, number * width), whole),
            pl.BlockSpec((tall, width), whole),
            pl.BlockSpec((some, width), whole),
            pl.BlockSpec((some, 3 * width), whole),
        ),
        compiler_params=pltpu.CompilerParams(vmem_limit_bytes=40 * 2**20),
    )(blocks, blocks, blocks, blocks, parts, branch, x, g, small)


def shards(
    layer_input,
    attn_gain,
    attn_shift,
    qkv_weight,
    qkv_bias,
    out_weight,
    out_bias,
    mlp_gain,
    mlp_shift,
    up_weight,
    up_bias,
    down_weight,
    down_bias,
    seq_lengths,
    upstream,
):
    local_rows = layer_input.shape[0]
    count = lax.axis_size("shard")
    group_rows = local_rows * count
    place = lax.axis_index("shard")
    part = D // count
    hidden = up_bias.shape[0]

    params = [attn_gain, attn_shift, out_bias, mlp_gain, mlp_shift, down_bias]
    params += [qkv_bias[i * part : (i + 1) * part] for i in range(3)]
    row = lax.broadcasted_iota(jnp.int32, (16, part), 0)
    small = jnp.zeros((16, part), jnp.bfloat16)
    for i, param in enumerate(params):
        small = jnp.where(row == i, param[None], small)

    token = lax.broadcasted_iota(jnp.int32, (group_rows, 1), 0)
    first, end = jnp.zeros((group_rows, 1), jnp.int32), 0
    for i in range(seq_lengths.shape[1]):
        end = end + seq_lengths[0, i]
        first = first + jnp.where(token >= end, seq_lengths[0, i], 0)
    lane = lax.broadcasted_iota(jnp.int32, (1, 128), 1)
    exponent = lax.rem(lane, ROT // 2).astype(jnp.float32) * (2.0 / ROT)
    angles = (token - first).astype(jnp.float32) * jnp.power(jnp.float32(ROPE_BASE), -exponent)
    cosine, sine = jnp.cos(angles), jnp.sin(angles)
    tables = jnp.stack(
        [
            jnp.where(lane < ROT, cosine, 1.0),
            jnp.where(lane < ROT // 2, sine, 0.0),
            jnp.where((lane >= ROT // 2) & (lane < ROT), sine, 0.0),
        ]
    )
    known = forward(
        small,
        up_weight,
        qkv_weight,
        layer_input,
        upstream,
        down_weight,
        out_weight,
        up_bias.astype(jnp.float32)[None],
        tables,
        first,
    )
    branch_own = lax.psum_scatter(known["branch"], "shard", scatter_dimension=0, tiled=True)
    grads, vector, normed_parts = summed_grads(
        known["act"],
        known["g"],
        known["mixed"],
        known["mlp_in"],
        known["attn_in"],
        known["slope"],
        down_weight,
        out_weight,
        known["heads"],
        known["x"],
        known["up_cols"],
        known["qkv_cols"],
        tables,
        first,
        known["stats"],
        known["small"],
    )
    grads, branch_own = lax.optimization_barrier((grads, branch_own))
    vector = vector.reshape(-1)
    layer_output, input_grad, up_grad, down_grad, out_grad, qkv_grad = last(
        grads, normed_parts, branch_own, layer_input, upstream, known["small"]
    )
    own = lambda i: lax.dynamic_slice_in_dim(vector, i * D + place * part, part, 0)
    bias_grad = own(4)
    qkv_bias_grad = lax.dynamic_slice_in_dim(vector, 5 * D + place * 3 * part, 3 * part, 0)
    up_bias_grad = lax.dynamic_slice_in_dim(vector, 8 * D + place * hidden, hidden, 0)
    return (
        layer_output,
        input_grad,
        own(0),
        own(1),
        qkv_grad,
        qkv_bias_grad,
        out_grad,
        bias_grad,
        own(2),
        own(3),
        up_grad,
        up_bias_grad,
        down_grad,
        bias_grad,
    )


def solution(mesh):
    in_specs = (
        P(("replica", "shard"), None),
        P("shard"),
        P("shard"),
        P("shard", None),
        P("shard"),
        P("shard", None),
        P("shard"),
        P("shard"),
        P("shard"),
        P("shard", None),
        P("shard"),
        P("shard", None),
        P("shard"),
        P("replica", None),
        P(("replica", "shard"), None),
    )
    out_specs = (
        P(("replica", "shard"), None),
        P(("replica", "shard"), None),
        P("shard"),
        P("shard"),
        P("shard", None),
        P("shard"),
        P("shard", None),
        P("shard"),
        P("shard"),
        P("shard"),
        P("shard", None),
        P("shard"),
        P("shard", None),
        P("shard"),
    )
    return jax.shard_map(shards, mesh=mesh, in_specs=in_specs, out_specs=out_specs, check_vma=False)
```

```python
from functools import partial
import math

import jax
import jax.numpy as jnp
import numpy as np
from jax import lax
from jax.experimental import pallas as pl
from jax.experimental.pallas import tpu as pltpu
from jax.sharding import PartitionSpec as P

D = 2048
HEADS = 8
HEAD = 256
ROT = 64


EPSILON = 1e-05
ROPE_BASE = 10000.0
NEG_LARGE = -1e30
MESH = pl.DeviceIdType.MESH
CONTRACT_ROWS = (((0,), (0,)), ((), ()))
CONTRACT_COLS = (((1,), (1,)), ((), ()))


def normalize(layer_rows):
    centered = layer_rows - jnp.mean(layer_rows, -1, keepdims=True)
    variance = jnp.mean(centered * centered, -1, keepdims=True)
    inverse_std = lax.rsqrt(variance + EPSILON)
    return (centered * inverse_std, inverse_std)


def norm_backward(grad_normed, normed, inverse_std):
    mean_grad = jnp.mean(grad_normed, -1, keepdims=True)
    mean_cross = jnp.mean(grad_normed * normed, -1, keepdims=True)
    return (grad_normed - mean_grad - normed * mean_cross) * inverse_std


def dot(left, right):
    return jnp.dot(left, right, preferred_element_type=jnp.float32)


def dot_rows(left, right):
    return lax.dot_general(left, right, CONTRACT_ROWS, preferred_element_type=jnp.float32)


def dot_cols(left, right):
    return lax.dot_general(left, right, CONTRACT_COLS, preferred_element_type=jnp.float32)


def bit_of(index, bit):
    return lax.rem(lax.div(index, 1 << bit), 2)


def flip(index, bit):
    return index + (1 << bit) * (1 - 2 * bit_of(index, bit))


def plane_orders(replicas):
    far = list(range(1, replicas.bit_length() - 1))
    return far, far[1:] + far[:1]


def remote(src, dst, sems, at, device):
    return pltpu.make_async_remote_copy(
        src_ref=src,
        dst_ref=dst,
        send_sem=sems.at[(0,) + at],
        recv_sem=sems.at[(1,) + at],
        device_id=device,
        device_id_type=MESH,
    )


def greet(rep, place, replicas, shards_n):
    barrier = pltpu.get_barrier_semaphore()
    bits = replicas.bit_length() - 1
    for bit in range(bits):
        pl.semaphore_signal(
            barrier, inc=1, device_id={"replica": flip(rep, bit)}, device_id_type=MESH
        )
    for step in range(1, shards_n):
        pl.semaphore_signal(
            barrier,
            inc=1,
            device_id={"shard": lax.rem(place + step, shards_n)},
            device_id_type=MESH,
        )
    pl.semaphore_wait(barrier, bits + shards_n - 1)


TILE = 256
TALL = 512


def causal_probs(query, key, first, row):
    shape = (query.shape[0], key.shape[0])
    scores = dot_cols(query, key) * (1.0 / math.sqrt(HEAD))
    at = lax.broadcasted_iota(jnp.int32, shape, 1)
    upto = lax.broadcasted_iota(jnp.int32, shape, 0) + row
    scores = jnp.where((at >= first) & (at <= upto), scores, NEG_LARGE)
    shifted = jnp.exp(scores - jnp.max(scores, -1, keepdims=True))
    return shifted / jnp.sum(shifted, -1, keepdims=True)


def forward_kernel(
    replicas,
    shards_n,
    small_ref,
    up_ref,
    qkv_ref,
    x_ref,
    g_ref,
    down_ref,
    proj_ref,
    bias_ref,
    frequency_ref,
    lengths_ref,
    small_out,
    up_out,
    qkv_out,
    x_out,
    g_out,
    mlp_out,
    attn_out,
    act_out,
    slope_out,
    heads_out,
    mixed_out,
    branch_out,
    stats_out,
    tables_out,
    first_out,
    small_low,
    small,
    x_rows,
    mlp,
    attn,
    up,
    qkv,
    act,
    slope,
    heads,
    mixed,
    down,
    proj,
    branch,
    own_sem,
    load_sem,
    keep_sem,
    small_sem,
    turn_sem,
    plane_sem,
    hop_sem,
    g_sem,
):
    rep, place = lax.axis_index("replica"), lax.axis_index("shard")
    bits = replicas.bit_length() - 1
    width, hidden = up_out.shape
    part = width // shards_n
    wide = qkv_out.shape[2]
    rows = part // replicas
    tokens = x_out.shape[0]
    local = tokens // shards_n
    cols = down.shape[2]
    orders = [order + [0] for order in plane_orders(replicas)]
    starts = []
    for order in orders:
        start = 0
        for level, bit in enumerate(order):
            start = start + bit_of(rep, bit) * (rows << level)
        starts.append(start)

    items = [(thing, step) for thing in range(2) for step in range(1, shards_n)]

    def source(third, shard, path):
        some = pl.ds(pl.multiple_of(starts[path], rows), rows)
        if third is None:
            at = shard * hidden + path * (hidden // 2)
            return up_ref.at[some, pl.ds(pl.multiple_of(at, 128), hidden // 2)]
        at = third * width + shard * wide + path * (wide // 2)
        return qkv_ref.at[some, pl.ds(pl.multiple_of(at, 128), wide // 2)]

    def target(third, shard, start, count, path):
        some = pl.ds(pl.multiple_of(shard * part + start, rows), count)
        if third is None:
            return up_out.at[some, pl.ds(path * (hidden // 2), hidden // 2)]
        return qkv_out.at[third, some, pl.ds(path * (wide // 2), wide // 2)]

    def turned(item, path, sending):
        thing, step = items[item]
        to = lax.rem(place + step, shards_n)
        shard = place if sending else lax.rem(place - step + shards_n, shards_n)
        return [
            remote(
                source(third, to, path),
                target(third, shard, starts[path], rows, path),
                turn_sem,
                (item, path, third or 0),
                {"shard": to},
            )
            for third in (range(3) if thing else (None,))
        ]

    def spread(item, path, level):
        thing, step = items[item]
        shard = lax.rem(place - step + shards_n, shards_n)
        order = orders[path]
        start = 0
        for above in range(level, bits):
            start = start + bit_of(rep, order[above]) * (rows << above)
        here = target(pl.ds(0, 3) if thing else None, shard, start, rows << level, path)
        return remote(
            here, here, plane_sem, (item, path, level), {"replica": flip(rep, order[level])}
        )

    def small_copy(step, sending):
        to = lax.rem(place + step, shards_n)
        shard = place if sending else lax.rem(place - step + shards_n, shards_n)
        return remote(small_ref, small_out.at[shard], small_sem, (step,), {"shard": to})

    def column_tick(tick):
        for level in reversed(range(bits + 1)):
            item = tick - level
            if not 0 <= item < len(items):
                continue
            for path in range(2):
                if level == 0:
                    for copy in turned(item, path, False):
                        copy.wait_recv()
                else:
                    spread(item, path, level - 1).wait_recv()
                if level < bits:
                    spread(item, path, level).start()

    def block_rows(block):
        return pl.ds(pl.multiple_of(block * local, local), local)

    def hop(way, step, sending):
        sign = 1 - 2 * way
        block = place - sign * (step if sending else step + 1)
        there = x_out.at[block_rows(block), :]
        return remote(
            x_ref if sending and step == 0 else there,
            there,
            hop_sem,
            (way, step),
            {"shard": lax.rem(place + sign + shards_n, shards_n)},
        )

    def upstream_copy(step, sending):
        to = lax.rem(place + step, shards_n)
        shard = place if sending else lax.rem(place - step + shards_n, shards_n)
        return remote(g_ref, g_out.at[block_rows(shard), :], g_sem, (step,), {"shard": to})

    def holds(way, step):
        return place >= step if way == 0 else place + step < shards_n

    def goes(way, step):
        onward = place + 1 < shards_n if way == 0 else place >= 1
        return holds(way, step) & onward

    def send_hop(step):
        for way in range(2):

            @pl.when(goes(way, step))
            def _():
                hop(way, step, True).start()

    def pass_on(step):
        for way in range(2):

            @pl.when(holds(way, step))
            def _():
                hop(way, step - 1, False).wait_recv()

        if step + 1 < shards_n:
            send_hop(step)

    def load(number, src, dst):
        return pltpu.make_async_copy(src, dst, load_sem.at[number])

    def keep(number, src, dst):
        return pltpu.make_async_copy(src, dst, keep_sem.at[number])

    def norm(block, from_ref, slot):
        copy = load(slot, from_ref, x_rows.at[slot])
        copy.start()
        copy.wait()

        def some_rows(i, carry):
            here = pl.ds(pl.multiple_of(i * 32, 32), 32)
            there = pl.ds(pl.multiple_of(block * local + i * 32, 32), 32)
            values = x_rows[slot, here, :].astype(jnp.float32)
            mean = jnp.mean(values, -1, keepdims=True)
            centered = values - mean
            scale = lax.rsqrt(jnp.mean(centered * centered, -1, keepdims=True) + EPSILON)
            stats_out[0, there, :] = mean
            stats_out[1, there, :] = scale
            normed = centered * scale
            for z in range(shards_n):
                lanes = slice(z * part, (z + 1) * part)
                some = normed[:, lanes]
                attn[there, lanes] = (some * small[z, 0:1, :] + small[z, 1:2, :]).astype(jnp.bfloat16)
                mlp[there, lanes] = (some * small[z, 3:4, :] + small[z, 4:5, :]).astype(jnp.bfloat16)
            return carry

        lax.fori_loop(0, local // 32, some_rows, 0)

    def hidden_units(block):
        here = block_rows(block)

        def some_cols(k, carry):
            lanes = pl.ds(pl.multiple_of(k * cols, cols), cols)
            found = dot(mlp[here, :], up[:, lanes]) + bias_ref[0:1, lanes]
            cdf = 0.5 * (1.0 + lax.erf(found * math.sqrt(0.5)))
            act[here, lanes] = (found * cdf).astype(jnp.bfloat16)
            bell = jnp.exp(-0.5 * found * found) * (1.0 / math.sqrt(2.0 * math.pi))
            slope[here, lanes] = (cdf + found * bell).astype(jnp.bfloat16)
            return carry

        lax.fori_loop(0, hidden // cols, some_cols, 0)

    def tables(i, carry):
        some = local // 2
        here = pl.ds(pl.multiple_of(i * some, some), some)
        token = lax.broadcasted_iota(jnp.int32, (some, 128), 0) + i * some
        lane = lax.broadcasted_iota(jnp.int32, (some, 128), 1)
        first, end = jnp.zeros((some, 128), jnp.int32), 0
        for j in range(lengths_ref.shape[1]):
            length = lengths_ref[0, j]
            end = end + length
            first = first + jnp.where(token >= end, length, 0)
        first_out[here, :] = first[:, :1]
        angles = (token - first).astype(jnp.float32) * frequency_ref[0:1, :]
        sine = jnp.sin(angles)
        tables_out[0, here, :] = jnp.where(lane < ROT, jnp.cos(angles), 1.0)
        tables_out[1, here, :] = jnp.where(lane < ROT // 2, sine, 0.0)
        tables_out[2, here, :] = jnp.where((lane >= ROT // 2) & (lane < ROT), sine, 0.0)
        return carry

    def on_step(step, todo):
        for way in range(2):
            if step == 0 and way == 1:
                continue
            block = place - (1 - 2 * way) * step

            @pl.when(holds(way, step))
            def _():
                todo(block, way)

    def project(third):
        number = third * shards_n + place
        bias = small[lax.div(number, 3), pl.ds(6 + lax.rem(number, 3), 1), :]

        def some_rows(i, carry):
            here = pl.ds(pl.multiple_of(i * TALL, TALL), TALL)
            found = dot(attn[here, :], qkv[third]) + bias
            for head in range(wide // HEAD):
                mine = found[:, head * HEAD : (head + 1) * HEAD]
                if third < 2:
                    lead = mine[:, :128]
                    lead = (
                        lead * tables_out[0, here, :]
                        - pltpu.roll(lead, 96, 1) * tables_out[1, here, :]
                        + pltpu.roll(lead, 32, 1) * tables_out[2, here, :]
                    )
                    mine = jnp.concatenate([lead, mine[:, 128:]], 1)
                heads[third, here, head * HEAD : (head + 1) * HEAD] = mine.astype(jnp.bfloat16)
            return carry

        lax.fori_loop(0, tokens // TALL, some_rows, 0)

    def attend(head):
        lanes = slice(head * HEAD, (head + 1) * HEAD)
        for i in range(tokens // TILE):
            here, keys = slice(i * TILE, (i + 1) * TILE), slice(0, (i + 1) * TILE)
            probs = causal_probs(heads[0, here, lanes], heads[1, keys, lanes], first_out[here, :], i * TILE)
            mixed[here, lanes] = dot(probs.astype(jnp.bfloat16), heads[2, keys, lanes]).astype(jnp.bfloat16)

    def down_load(j):
        return load(4 + j % 2, down_ref.at[:, pl.ds(j * cols, cols)], down.at[j % 2])

    def branch_keep(j):
        return keep(6 + j, branch.at[j % 2], branch_out.at[:, pl.ds(j * cols, cols)])

    def branch_cols(j):
        down_load(j).wait()
        if j >= 2:
            branch_keep(j - 2).wait()

        def some_rows(i, carry):
            here = pl.ds(pl.multiple_of(i * TALL, TALL), TALL)
            found = dot(act[here, :], down[j % 2]) + dot(mixed[here, :], proj[:, j * cols : (j + 1) * cols])
            branch[j % 2, here, :] = found.astype(jnp.bfloat16)
            return carry

        lax.fori_loop(0, tokens // TALL, some_rows, 0)
        branch_keep(j).start()
        if j + 2 < width // cols:
            down_load(j + 2).start()

    greet(rep, place, replicas, shards_n)
    for step in range(1, shards_n):
        small_copy(step, True).start()
    for item in range(shards_n - 1):
        for path in range(2):
            for copy in turned(item, path, True):
                copy.start()
    send_hop(0)
    own = [
        (small_ref, small_out.at[place]),
        (
            up_ref.at[:, pl.ds(pl.multiple_of(place * hidden, 128), hidden)],
            up_out.at[pl.ds(pl.multiple_of(place * part, part), part), :],
        ),
        (x_ref, x_out.at[block_rows(place), :]),
        (g_ref, g_out.at[block_rows(place), :]),
    ] + [
        (
            qkv_ref.at[:, pl.ds(pl.multiple_of(third * width + place * wide, 128), wide)],
            qkv_out.at[third, pl.ds(pl.multiple_of(place * part, part), part), :],
        )
        for third in range(3)
    ]
    own = [pltpu.make_async_copy(src, dst, own_sem.at[i]) for i, (src, dst) in enumerate(own)]
    for copy in own:
        copy.start()
    down_load(0).start()
    down_load(1).start()
    load_proj = load(6, proj_ref, proj)
    load_proj.start()

    lax.fori_loop(0, 2 * shards_n, tables, 0)
    for step in range(1, shards_n):
        small_copy(step, False).wait()
    own[0].wait()
    load_small = load(0, small_out, small_low)
    load_small.start()
    load_small.wait()
    small[...] = small_low[...].astype(jnp.float32)
    on_step(0, lambda block, way: norm(block, x_ref, way))

    load_up = load(2, up_out, up)
    load_qkv = load(3, qkv_out, qkv)
    ticks = list(range(len(items) + bits))

    def some_ticks(number):
        for tick in ticks[:number]:
            column_tick(tick)
        del ticks[:number]

    def arrive(step):
        pass_on(step)
        if step == 1:
            for item in range(shards_n - 1, len(items)):
                for path in range(2):
                    for copy in turned(item, path, True):
                        copy.start()
        on_step(step, lambda block, way: norm(block, x_out.at[block_rows(block), :], way))

    some_ticks(3)
    arrive(1)
    some_ticks(shards_n - 1 + bits - 3)
    own[1].wait()
    load_up.start()
    load_up.wait()
    on_step(0, lambda block, way: hidden_units(block))
    for step in range(2, shards_n - 1):
        arrive(step)
    some_ticks(1)
    on_step(1, lambda block, way: hidden_units(block))
    some_ticks(1)
    for way in range(2):

        @pl.when(goes(way, shards_n - 2))
        def _():
            hop(way, shards_n - 2, True).wait_send()

    for other in range(1, shards_n):
        upstream_copy(other, True).start()
    some_ticks(len(ticks))
    arrive(shards_n - 1)
    keeps = [keep(0, mlp, mlp_out), keep(1, attn, attn_out)]
    keeps[0].start()
    keeps[1].start()
    for copy in own[4:]:
        copy.wait()
    load_qkv.start()
    for step in range(2, shards_n):
        on_step(step, lambda block, way: hidden_units(block))
    keeps += [keep(2, act, act_out), keep(3, slope, slope_out)]
    keeps[2].start()
    keeps[3].start()
    load_qkv.wait()
    for third in range(3):
        project(third)
    keeps.append(keep(4, heads, heads_out))
    keeps[4].start()
    for head in range(wide // HEAD):
        attend(head)
    keeps.append(keep(5, mixed, mixed_out))
    keeps[5].start()
    load_proj.wait()
    for j in range(width // cols):
        branch_cols(j)
    for step in range(1, shards_n):
        upstream_copy(step, False).wait()
    for j in range(max(width // cols - 2, 0), width // cols):
        branch_keep(j).wait()
    for copy in keeps:
        copy.wait()
    for item in range(len(items)):
        for path in range(2):
            for copy in turned(item, path, True):
                copy.wait_send()
            for level in range(bits):
                spread(item, path, level).wait_send()
    for step in range(shards_n - 2):
        for way in range(2):

            @pl.when(goes(way, step))
            def _():
                hop(way, step, True).wait_send()

    for copy in own[2:4]:
        copy.wait()


def forward(small, up_weight, qkv_weight, x, g, down_weight, proj_weight, bias, frequency, lengths):
    replicas, count = lax.axis_size("replica"), lax.axis_size("shard")
    bits = replicas.bit_length() - 1
    local, width = x.shape
    tokens = local * count
    hidden, wide = up_weight.shape[1] // count, width // count
    cols = wide
    items = 2 * (count - 1)
    any_spec = pl.BlockSpec(memory_space=pl.ANY)
    vmem_spec = pl.BlockSpec(memory_space=pltpu.VMEM)
    shapes = dict(
        small=(count,) + small.shape,
        up_cols=(width, hidden),
        qkv_cols=(3, width, wide),
        x=(tokens, width),
        g=(tokens, width),
        mlp_in=(tokens, width),
        attn_in=(tokens, width),
        act=(tokens, hidden),
        slope=(tokens, hidden),
        heads=(3, tokens, wide),
        mixed=(tokens, wide),
        branch=(tokens, width),
    )
    low = lambda *shape: pltpu.VMEM(shape, jnp.bfloat16)
    dma = lambda *shape: pltpu.SemaphoreType.DMA(shape)
    found = pl.pallas_call(
        partial(forward_kernel, replicas, count),
        out_shape=tuple(jax.ShapeDtypeStruct(shape, jnp.bfloat16) for shape in shapes.values())
        + (
            jax.ShapeDtypeStruct((2, tokens, 1), jnp.float32),
            jax.ShapeDtypeStruct((3, tokens, 128), jnp.float32),
            jax.ShapeDtypeStruct((tokens, 1), jnp.int32),
        ),
        in_specs=[any_spec] * 7 + [vmem_spec] * 2 + [pl.BlockSpec(memory_space=pltpu.SMEM)],
        out_specs=(any_spec,) * len(shapes) + (vmem_spec,) * 3,
        scratch_shapes=[
            low(*shapes["small"]),
            pltpu.VMEM(shapes["small"], jnp.float32),
            low(2, local, width),
            low(tokens, width),
            low(tokens, width),
            low(width, hidden),
            low(3, width, wide),
            low(tokens, hidden),
            low(tokens, hidden),
            low(3, tokens, wide),
            low(tokens, wide),
            low(2, hidden, cols),
            low(wide, width),
            low(2, tokens, cols),
            dma(7),
            dma(7),
            dma(6 + width // cols),
            dma(2, count),
            dma(2, items, 2, 3),
            dma(2, items, 2, bits),
            dma(2, 2, count - 1),
            dma(2, count),
        ],
        compiler_params=pltpu.CompilerParams(
            collective_id=0, has_side_effects=True, vmem_limit_bytes=58 * 2**20
        ),
        cost_estimate=pl.CostEstimate(
            flops=2 * tokens * width * (hidden * 2 + wide * 4),
            bytes_accessed=500_000_000,
            transcendentals=0,
        ),
    )(small, up_weight, qkv_weight, x, g, down_weight, proj_weight, bias, frequency, lengths)
    return dict(zip(list(shapes) + ["stats", "tables", "first"], found))


RING = 3


def grads_kernel(
    replicas,
    shards_n,
    act_ref,
    up_ref,
    mixed_ref,
    mlp_ref,
    attn_ref,
    slope_ref,
    down_ref,
    proj_ref,
    heads_ref,
    rows_ref,
    cols_up_ref,
    cols_qkv_ref,
    tables_ref,
    first_ref,
    stats_ref,
    small_ref,
    out_ref,
    vec_out,
    sum_out,
    work,
    from_core,
    *rest,
):
    rep, place = lax.axis_index("replica"), lax.axis_index("shard")
    bits = replicas.bit_length() - 1
    far = bits - 1
    from_far = rest[:far]
    (
        big,
        narrow,
        pre,
        joined,
        wide_rows,
        slope,
        heads,
        key_sum,
        value_sum,
        tile_x,
        tile_up,
        tile_qkv,
        shared,
        vec_got,
        vec_sum,
        load_sem,
        core_sem,
        far_sem,
        turn_sem,
        own_sem,
        plane_sem,
        vec_sem,
        sum_sem,
    ) = rest[far:]
    chunks, _, rows, cols = out_ref.shape
    slots = work.shape[0]
    half, side = rows // 2, cols // 2
    piece = rows // replicas
    orders = plane_orders(replicas)
    core = bit_of(rep, 0)
    tokens, width = up_ref.shape
    local = tokens // shards_n
    hiddens = pre.shape[0]
    natives = hiddens + 1
    mine = pl.multiple_of(core * half, half)
    theirs = pl.multiple_of((1 - core) * half, half)

    starts = []
    for order in orders:
        line, size = [core * half], half
        for bit in order:
            size //= 2
            line.append(line[-1] + bit_of(rep, bit) * size)
        starts.append(line)

    def spot(k):
        if k < natives:
            return k + hiddens
        return k - natives if k < natives + hiddens else k

    def load(source, target, number):
        return pltpu.make_async_copy(source, target, load_sem.at[number])

    def narrow_load(k):
        source = act_ref.at[:, pl.ds(k * cols, cols)] if k < hiddens else mixed_ref
        return load(source, narrow.at[k % 2], k % 2)

    def big_load(which):
        return load((up_ref, mlp_ref, attn_ref)[which], big.at[which % 2], 2 + which)

    def down_load(k):
        return load(down_ref.at[pl.ds(k * cols, cols), :], wide_rows.at[k % 2], 5 + k % 2)

    def slope_load(k):
        return load(slope_ref.at[:, pl.ds(k * cols, cols)], slope.at[k % 2], 7 + k % 2)

    def pre_loads(k):
        return [down_load(k), slope_load(k)]

    def proj_load():
        return load(proj_ref, wide_rows.at[1], 6)

    def heads_load():
        return load(heads_ref, heads.at[pl.ds(0, 3)], 9)

    def tile_loads(j):
        some = pl.ds(j * TILE, TILE)
        return [
            load(rows_ref.at[:, some], tile_x.at[j % 2], 10 + j % 2),
            load(cols_up_ref.at[some, :], tile_up.at[j % 2], 12 + j % 2),
            load(cols_qkv_ref.at[:, some, :], tile_qkv.at[j % 2], 14 + j % 2),
        ]

    def to_core(k):
        return remote(
            work.at[k % slots, :, pl.ds(theirs, half), :],
            from_core.at[k % RING],
            core_sem,
            (0, k),
            {"replica": flip(rep, 0)},
        )

    def to_far(k, level, path):
        size = half >> (level + 1)
        bit = orders[path][level]
        start = starts[path][level] + (1 - bit_of(rep, bit)) * size
        return remote(
            work.at[k % slots, :, pl.ds(pl.multiple_of(start, size), size), pl.ds(path * side, side)],
            from_far[level].at[k % RING, path],
            far_sem,
            (k, level, path),
            {"replica": flip(rep, bit)},
        )

    def own_piece(k, path, block):
        return work.at[
            k % slots,
            block,
            pl.ds(pl.multiple_of(starts[path][far], piece), piece),
            pl.ds(path * side, side),
        ]

    def place_piece(k, path, block):
        return out_ref.at[
            spot(k),
            block,
            pl.ds(pl.multiple_of(starts[path][far], piece), piece),
            pl.ds(path * side, side),
        ]

    def settle(k, path):
        block = pl.ds(0, shards_n) if k < natives else place
        return pltpu.make_async_copy(
            own_piece(k, path, block), place_piece(k, path, block), own_sem.at[k % 2, path]
        )

    def turned(k, path, step, sending):
        to = lax.rem(place + step, shards_n)
        shard = place if sending else lax.rem(place - step + shards_n, shards_n)
        return remote(
            own_piece(k, path, to),
            place_piece(k, path, shard),
            turn_sem,
            (k - natives, path, step - 1),
            {"shard": to},
        )

    def spread(k, path, level):
        size = piece << level
        bit = orders[path][far - 1 - level]
        here = out_ref.at[
            spot(k),
            :,
            pl.ds(pl.multiple_of(starts[path][far - level], size), size),
            pl.ds(path * side, side),
        ]
        return remote(here, here, plane_sem, (k, level, path), {"replica": flip(rep, bit)})

    def spread_core(k):
        here = out_ref.at[spot(k), :, pl.ds(mine, half), :]
        return remote(here, here, core_sem, (1, k), {"replica": flip(rep, 0)})

    def put(offset, sums):
        for i in range(sums.shape[1] // 128):
            vec_sum[pl.ds(offset // 128 + i, 1), :] = sums[:, i * 128 : (i + 1) * 128]

    def compute(k):
        if k < natives:
            narrow_load(k).wait()
            if k + 1 < natives:
                narrow_load(k + 1).start()
        if k == 0:
            big_load(0).wait()
        if k == natives:
            big_load(1).wait()
        if k == natives + hiddens:
            big_load(2).wait()
        slot = k % slots
        which = 1 if natives <= k < natives + hiddens else 0

        for begin, send in ((theirs, True), (mine, False)):

            def block(g, carry):
                if k < natives:
                    left = narrow[k % 2, :, pl.ds(begin, half)]
                    right = big[which, :, pl.ds(pl.multiple_of(g * cols, cols), cols)]
                else:
                    left = big[which, :, pl.ds(pl.multiple_of(g * rows + begin, half), half)]
                    if k < natives + hiddens:
                        right = pre[k - natives]
                    else:
                        right = joined[k - natives - hiddens]
                work[slot, g, pl.ds(begin, half), :] = dot_rows(left, right).astype(jnp.bfloat16)
                return carry

            lax.fori_loop(0, shards_n, block, 0)
            if send:
                to_core(k).start()

    def add(k, start, size, left, width, got):
        def block(g, carry):
            where = (k % slots, g, pl.ds(pl.multiple_of(start, size), size), pl.ds(left, width))
            work[where] = (
                work[where].astype(jnp.float32) + got(g).astype(jnp.float32)
            ).astype(jnp.bfloat16)
            return carry

        lax.fori_loop(0, shards_n, block, 0)

    def grad_mixed():
        proj_load().wait()

        def block(i, carry):
            some = pl.ds(pl.multiple_of(i * TILE, TILE), TILE)
            heads[3, some, :] = dot_cols(big[0, some, :], wide_rows[1]).astype(jnp.bfloat16)
            return carry

        lax.fori_loop(0, tokens // TILE, block, 0)
        down_load(1).start()
        own = pl.ds(pl.multiple_of(place * cols, cols), cols)
        put(4 * width + place * cols, jnp.sum(big[0, :, own].astype(jnp.float32), 0, keepdims=True))

    def grad_pre(k):
        for copy in pre_loads(k):
            copy.wait()

        def block(i, total):
            some = pl.ds(pl.multiple_of(i * TILE, TILE), TILE)
            found = dot_cols(big[0, some, :], wide_rows[k % 2]) * slope[k % 2, some, :].astype(
                jnp.float32
            )
            low = found.astype(jnp.bfloat16)
            pre[k, some, :] = low
            return total + jnp.sum(low.astype(jnp.float32), 0, keepdims=True)

        total = lax.fori_loop(0, tokens // TILE, block, jnp.zeros((1, cols), jnp.float32))
        put(8 * width + (place * hiddens + k) * cols, total)
        if k + 2 < hiddens:
            for copy in pre_loads(k + 2):
                copy.start()

    def turn_rows(found, some):
        lead = found[:, :128]
        lead = (
            lead * tables_ref[0, some, :]
            + pltpu.roll(lead, 96, 1) * tables_ref[1, some, :]
            - pltpu.roll(lead, 32, 1) * tables_ref[2, some, :]
        )
        return jnp.concatenate([lead, found[:, 128:]], 1)

    def attention(head):
        lanes = pl.ds(head * HEAD, HEAD)
        scale = 1.0 / math.sqrt(HEAD)
        key_sum[...] = jnp.zeros_like(key_sum)
        value_sum[...] = jnp.zeros_like(value_sum)
        sums = [jnp.zeros((1, HEAD), jnp.float32)] * 3
        for i in range(tokens // TILE):
            some, keys = pl.ds(i * TILE, TILE), pl.ds(0, (i + 1) * TILE)
            query = heads[0, some, lanes]
            key = heads[1, keys, lanes]
            probs = causal_probs(query, key, first_ref[some, :], i * TILE)
            grad = heads[3, some, lanes]
            grad_probs = dot_cols(grad, heads[2, keys, lanes])
            delta = jnp.sum(probs * grad_probs, -1, keepdims=True)
            low = (probs * (grad_probs - delta)).astype(jnp.bfloat16)
            found = turn_rows(dot(low, key) * scale, some).astype(jnp.bfloat16)
            joined[0, some, lanes] = found
            sums[0] = sums[0] + jnp.sum(found.astype(jnp.float32), 0, keepdims=True)
            key_sum[keys, :] = key_sum[keys, :] + dot_rows(low, query)
            value_sum[keys, :] = value_sum[keys, :] + dot_rows(probs.astype(jnp.bfloat16), grad)
        for i in range(tokens // TILE):
            some = pl.ds(i * TILE, TILE)
            for third, found in (
                (1, turn_rows(key_sum[some, :] * scale, some)),
                (2, value_sum[some, :]),
            ):
                low = found.astype(jnp.bfloat16)
                joined[third, some, lanes] = low
                sums[third] = sums[third] + jnp.sum(low.astype(jnp.float32), 0, keepdims=True)
        for third in range(3):
            put(5 * width + third * width + place * cols + head * HEAD, sums[third])

    def sum_part(j, step, sending):
        to = lax.rem(place + step, shards_n)
        shard = place if sending else lax.rem(place - step + shards_n, shards_n)
        some = pl.ds(j * TILE, TILE)
        source = shared.at[pl.ds(pl.multiple_of(to * local, local), local), some]
        if step == 0:
            return pltpu.make_async_copy(source, sum_out.at[place, :, some], sum_sem.at[0, j, 0])
        return remote(source, sum_out.at[shard, :, some], sum_sem, (j, step), {"shard": to})

    def tile(j):
        for copy in tile_loads(j):
            copy.wait()
        if j + 1 < width // TILE:
            for copy in tile_loads(j + 1):
                copy.start()
        lanes = pl.ds(j * TILE, TILE)
        owner, begin = divmod(j * TILE, cols)
        theirs_at = slice(begin, begin + TILE)

        def block(i, totals):
            some = pl.ds(pl.multiple_of(i * local, local), local)
            normed = (tile_x[j % 2, some, :].astype(jnp.float32) - stats_ref[0, some, :]) * stats_ref[
                1, some, :
            ]
            mlp = sum(
                dot_cols(pre[k, some, :], tile_up[j % 2, :, k * cols : (k + 1) * cols])
                for k in range(hiddens)
            )
            attn = sum(dot_cols(joined[p, some, :], tile_qkv[j % 2, p]) for p in range(3))
            shared[some, lanes] = (
                attn * small_ref[owner, 0:1, theirs_at].astype(jnp.float32)
                + mlp * small_ref[owner, 3:4, theirs_at].astype(jnp.float32)
            ).astype(jnp.bfloat16)
            found = (attn * normed, attn, mlp * normed, mlp)
            return tuple(t + jnp.sum(f, 0, keepdims=True) for t, f in zip(totals, found))

        zero = jnp.zeros((1, TILE), jnp.float32)
        totals = lax.fori_loop(0, shards_n, block, (zero,) * 4)
        for number, total in enumerate(totals):
            put(number * width + j * TILE, total)
        for step in range(shards_n):
            sum_part(j, step, True).start()

    def stage(k, number):
        if number == 0:
            compute(k)
        elif number == 1:
            to_core(k).wait()
            add(k, mine, half, 0, cols, lambda g: from_core[k % RING, g])
            for path in range(2):
                to_far(k, 0, path).start()
        elif number <= 1 + far:
            level = number - 2
            for path in range(2):
                to_far(k, level, path).wait()
                size = half >> (level + 1)
                add(
                    k,
                    starts[path][level + 1],
                    size,
                    path * side,
                    side,
                    lambda g: from_far[level][k % RING, path, g],
                )
                if level + 1 < far:
                    to_far(k, level + 1, path).start()
                else:
                    if k >= natives:
                        for step in range(1, shards_n):
                            turned(k, path, step, True).start()
                    settle(k, path).start()
        elif number == 2 + far:
            for path in range(2):
                settle(k, path).wait()
                if k >= natives:
                    for step in range(1, shards_n):
                        turned(k, path, step, False).wait_recv()
                spread(k, path, 0).start()
            if k >= natives:
                for path in range(2):
                    for step in range(1, shards_n):
                        turned(k, path, step, True).wait_send()
        elif number <= 2 + 2 * far:
            level = number - 3 - far
            for path in range(2):
                spread(k, path, level).wait()
                if level + 1 < far:
                    spread(k, path, level + 1).start()
            if level + 1 == far:
                spread_core(k).start()
        else:
            spread_core(k).wait()

    stages = 4 + 2 * far
    n_heads, n_tiles = cols // HEAD, width // TILE
    extras = {0: [grad_mixed, partial(grad_pre, 0)]}
    for k in range(1, hiddens):
        extras.setdefault(k, []).append(partial(grad_pre, k))
    for head in range(n_heads):
        extras.setdefault(1 + head, []).append(partial(attention, head))
    extras[hiddens] = [big_load(2).start]
    tile_at = hiddens + 1
    for j in range(n_tiles):
        extras.setdefault(tile_at + j, []).append(partial(tile, j))
    vec_at = max(extras) + 1

    for copy in [narrow_load(0), big_load(0), proj_load()] + pre_loads(0):
        copy.start()
    slope_load(1).start()
    for copy in [heads_load(), big_load(1)] + tile_loads(0):
        copy.start()
    vec_sum[...] = jnp.zeros_like(vec_sum)
    greet(rep, place, replicas, shards_n)
    peers = [{"replica": flip(rep, bit)} for bit in range(bits)]
    peers += [{"shard": flip(place, bit)} for bit in range(shards_n.bit_length() - 1)]

    def vec_copy(number):
        return remote(vec_sum, vec_got.at[number], vec_sem, (number,), peers[number])

    for tick in range(max(chunks + stages - 1, vec_at + len(peers) + 1)):
        for number in reversed(range(stages)):
            if 0 <= tick - number < chunks:
                stage(tick - number, number)
        if tick == 0:
            heads_load().wait()
        for extra in extras.get(tick, []):
            extra()
        turn_of = tick - vec_at
        if 0 < turn_of <= len(peers):
            vec_copy(turn_of - 1).wait()
            vec_sum[...] = vec_sum[...] + vec_got[turn_of - 1]
        if 0 <= turn_of < len(peers):
            vec_copy(turn_of).start()
    vec_out[...] = vec_sum[...]
    for j in range(n_tiles):
        for step in range(shards_n):
            sum_part(j, step, False).wait()


def summed_grads(*operands):
    act, up, mixed, mlp_in = operands[:4]
    replicas, count = lax.axis_size("replica"), lax.axis_size("shard")
    bits = replicas.bit_length() - 1
    far = bits - 1
    tokens, width = up.shape
    cols = width // count
    hidden = act.shape[1]
    hiddens = hidden // cols
    natives = hiddens + 1
    chunks = natives + hiddens + 3
    peers = bits + count.bit_length() - 1
    slots = 2 + far
    vector = ((8 * width + count * hidden) // 128, 128)
    any_spec = pl.BlockSpec(memory_space=pl.ANY)
    vmem_spec = pl.BlockSpec(memory_space=pltpu.VMEM)
    low = lambda *shape: pltpu.VMEM(shape, jnp.bfloat16)
    full = lambda *shape: pltpu.VMEM(shape, jnp.float32)
    dma = lambda *shape: pltpu.SemaphoreType.DMA(shape)
    return pl.pallas_call(
        partial(grads_kernel, replicas, count),
        out_shape=(
            jax.ShapeDtypeStruct((chunks, count, cols, cols), jnp.bfloat16),
            jax.ShapeDtypeStruct(vector, jnp.float32),
            jax.ShapeDtypeStruct((count, tokens // count, width), jnp.bfloat16),
        ),
        in_specs=[any_spec] * 12 + [vmem_spec] * 4,
        out_specs=(any_spec, vmem_spec, any_spec),
        scratch_shapes=[
            low(slots, count, cols, cols),
            low(RING, count, cols // 2, cols),
        ]
        + [low(RING, 2, count, cols >> (level + 2), cols // 2) for level in range(far)]
        + [
            low(2, tokens, width),
            low(2, tokens, cols),
            low(hiddens, tokens, cols),
            low(3, tokens, cols),
            low(2, cols, width),
            low(2, tokens, cols),
            low(4, tokens, cols),
            full(tokens, HEAD),
            full(tokens, HEAD),
            low(2, tokens, TILE),
            low(2, TILE, hidden),
            low(2, 3, TILE, cols),
            low(tokens, width),
            full(peers, *vector),
            full(*vector),
            dma(16),
            dma(2, 2, chunks),
            dma(2, chunks, far, 2),
            dma(2, chunks - natives, 2, count - 1),
            dma(2, 2),
            dma(2, chunks, far, 2),
            dma(2, peers),
            dma(2, width // TILE, count),
        ],
        compiler_params=pltpu.CompilerParams(
            collective_id=1, has_side_effects=True, vmem_limit_bytes=60 * 2**20
        ),
        cost_estimate=pl.CostEstimate(
            flops=4 * tokens * chunks * count * cols * cols,
            bytes_accessed=600_000_000,
            transcendentals=0,
        ),
    )(*operands)


def last_kernel(
    up_blocks,
    down_blocks,
    out_blocks,
    qkv_blocks,
    parts_ref,
    branch_ref,
    x_ref,
    g_ref,
    small_ref,
    layer_out,
    input_out,
    up_out,
    down_out,
    out_out,
    qkv_out,
):
    number, count, _, cols = up_blocks.shape
    for g in range(count):
        lanes = slice(g * cols, (g + 1) * cols)
        for k in range(number):
            at = (g * number + k) * cols
            up_out[:, at : at + cols] = up_blocks[k, g].astype(jnp.float32)
        for k in range(3):
            at = (k * count + g) * cols
            qkv_out[:, at : at + cols] = qkv_blocks[k, g].astype(jnp.float32)
        down_out[:, lanes] = down_blocks[0, g].astype(jnp.float32)
        out_out[:, lanes] = out_blocks[0, g].astype(jnp.float32)
    rows = x_ref[...].astype(jnp.float32)
    normed, inverse_std = normalize(rows)
    grad = sum(parts_ref[g].astype(jnp.float32) for g in range(count))
    input_out[...] = g_ref[...].astype(jnp.float32) + norm_backward(grad, normed, inverse_std)
    for g in range(count):
        lanes = slice(g * cols, (g + 1) * cols)
        bias = small_ref[g, 2:3, :].astype(jnp.float32) + small_ref[g, 5:6, :].astype(jnp.float32)
        layer_out[:, lanes] = (
            rows[:, lanes] + branch_ref[:, lanes].astype(jnp.float32) + bias
        ).astype(jnp.bfloat16)


def last(blocks, parts, branch, x, g, small):
    count, rows, cols = blocks.shape[1:]
    number = (blocks.shape[0] - 4) // 2
    local, width = x.shape
    steps = local // 16
    some, tall = rows // steps, number * rows // steps
    turns = rows // tall
    whole = lambda i: (i, 0)
    return pl.pallas_call(
        last_kernel,
        out_shape=(
            jax.ShapeDtypeStruct((local, width), jnp.bfloat16),
            jax.ShapeDtypeStruct((local, width), jnp.float32),
            jax.ShapeDtypeStruct((rows, number * width), jnp.float32),
            jax.ShapeDtypeStruct((number * rows, width), jnp.float32),
            jax.ShapeDtypeStruct((rows, width), jnp.float32),
            jax.ShapeDtypeStruct((rows, 3 * width), jnp.float32),
        ),
        grid=(steps,),
        in_specs=[
            pl.BlockSpec((number, count, some, cols), lambda i: (0, 0, i, 0)),
            pl.BlockSpec((1, count, tall, cols), lambda i: (number + i // turns, 0, i % turns, 0)),
            pl.BlockSpec((1, count, some, cols), lambda i: (2 * number, 0, i, 0)),
            pl.BlockSpec((3, count, some, cols), lambda i: ((2 * number + 1) // 3, 0, i, 0)),
            pl.BlockSpec((count, 16, width), lambda i: (0, i, 0)),
            pl.BlockSpec((16, width), whole),
            pl.BlockSpec((16, width), whole),
            pl.BlockSpec((16, width), whole),
            pl.BlockSpec(small.shape, lambda i: (0, 0, 0)),
        ],
        out_specs=(
            pl.BlockSpec((16, width), whole),
            pl.BlockSpec((16, width), whole),
            pl.BlockSpec((some, number * width), whole),
            pl.BlockSpec((tall, width), whole),
            pl.BlockSpec((some, width), whole),
            pl.BlockSpec((some, 3 * width), whole),
        ),
        compiler_params=pltpu.CompilerParams(vmem_limit_bytes=62 * 2**20),
    )(blocks, blocks, blocks, blocks, parts, branch, x, g, small)


def shards(
    layer_input,
    attn_gain,
    attn_shift,
    qkv_weight,
    qkv_bias,
    out_weight,
    out_bias,
    mlp_gain,
    mlp_shift,
    up_weight,
    up_bias,
    down_weight,
    down_bias,
    seq_lengths,
    upstream,
):
    local_rows = layer_input.shape[0]
    count = lax.axis_size("shard")
    group_rows = local_rows * count
    place = lax.axis_index("shard")
    part = D // count
    hidden = up_bias.shape[0]

    params = [attn_gain, attn_shift, out_bias, mlp_gain, mlp_shift, down_bias]
    params += [qkv_bias[i * part : (i + 1) * part] for i in range(3)]
    row = lax.broadcasted_iota(jnp.int32, (16, part), 0)
    small = jnp.zeros((16, part), jnp.bfloat16)
    for i, param in enumerate(params):
        small = jnp.where(row == i, param[None], small)

    frequency = np.power(np.float32(ROPE_BASE), -np.arange(ROT // 2, dtype=np.float32) * np.float32(2.0 / ROT))
    known = forward(
        small,
        up_weight,
        qkv_weight,
        layer_input,
        upstream,
        down_weight,
        out_weight,
        up_bias.astype(jnp.float32)[None],
        jnp.asarray(np.tile(frequency, 128 // (ROT // 2))[None]),
        seq_lengths,
    )
    branch_own = lax.psum_scatter(known["branch"], "shard", scatter_dimension=0, tiled=True)
    grads, vector, normed_parts = summed_grads(
        known["act"],
        known["g"],
        known["mixed"],
        known["mlp_in"],
        known["attn_in"],
        known["slope"],
        down_weight,
        out_weight,
        known["heads"],
        known["x"],
        known["up_cols"],
        known["qkv_cols"],
        known["tables"],
        known["first"],
        known["stats"],
        known["small"],
    )
    grads, branch_own = lax.optimization_barrier((grads, branch_own))
    vector = vector.reshape(-1)
    layer_output, input_grad, up_grad, down_grad, out_grad, qkv_grad = last(
        grads, normed_parts, branch_own, layer_input, upstream, known["small"]
    )
    own = lambda i: lax.dynamic_slice_in_dim(vector, i * D + place * part, part, 0)
    bias_grad = own(4)
    qkv_bias_grad = lax.dynamic_slice_in_dim(vector, 5 * D + place * 3 * part, 3 * part, 0)
    up_bias_grad = lax.dynamic_slice_in_dim(vector, 8 * D + place * hidden, hidden, 0)
    return (
        layer_output,
        input_grad,
        own(0),
        own(1),
        qkv_grad,
        qkv_bias_grad,
        out_grad,
        bias_grad,
        own(2),
        own(3),
        up_grad,
        up_bias_grad,
        down_grad,
        bias_grad,
    )


def solution(mesh):
    in_specs = (
        P(("replica", "shard"), None),
        P("shard"),
        P("shard"),
        P("shard", None),
        P("shard"),
        P("shard", None),
        P("shard"),
        P("shard"),
        P("shard"),
        P("shard", None),
        P("shard"),
        P("shard", None),
        P("shard"),
        P("replica", None),
        P(("replica", "shard"), None),
    )
    out_specs = (
        P(("replica", "shard"), None),
        P(("replica", "shard"), None),
        P("shard"),
        P("shard"),
        P("shard", None),
        P("shard"),
        P("shard", None),
        P("shard"),
        P("shard"),
        P("shard"),
        P("shard", None),
        P("shard"),
        P("shard", None),
        P("shard"),
    )
    return jax.shard_map(shards, mesh=mesh, in_specs=in_specs, out_specs=out_specs, check_vma=False)
```

```python
from functools import partial
import math

import jax
import jax.numpy as jnp
import numpy as np
from jax import lax
from jax.experimental import pallas as pl
from jax.experimental.pallas import tpu as pltpu
from jax.sharding import PartitionSpec as P

D = 2048
HEADS = 8
HEAD = 256
ROT = 64


EPSILON = 1e-05
ROPE_BASE = 10000.0
NEG_LARGE = -1e30
MESH = pl.DeviceIdType.MESH
CONTRACT_ROWS = (((0,), (0,)), ((), ()))
CONTRACT_COLS = (((1,), (1,)), ((), ()))


def normalize(layer_rows):
    centered = layer_rows - jnp.mean(layer_rows, -1, keepdims=True)
    variance = jnp.mean(centered * centered, -1, keepdims=True)
    inverse_std = lax.rsqrt(variance + EPSILON)
    return (centered * inverse_std, inverse_std)


def norm_backward(grad_normed, normed, inverse_std):
    mean_grad = jnp.mean(grad_normed, -1, keepdims=True)
    mean_cross = jnp.mean(grad_normed * normed, -1, keepdims=True)
    return (grad_normed - mean_grad - normed * mean_cross) * inverse_std


def dot(left, right):
    return jnp.dot(left, right, preferred_element_type=jnp.float32)


def dot_rows(left, right):
    return lax.dot_general(left, right, CONTRACT_ROWS, preferred_element_type=jnp.float32)


def dot_cols(left, right):
    return lax.dot_general(left, right, CONTRACT_COLS, preferred_element_type=jnp.float32)


def bit_of(index, bit):
    return lax.rem(lax.div(index, 1 << bit), 2)


def flip(index, bit):
    return index + (1 << bit) * (1 - 2 * bit_of(index, bit))


def plane_orders(replicas):
    far = list(range(1, replicas.bit_length() - 1))
    return far, far[1:] + far[:1]


def remote(src, dst, sems, at, device):
    return pltpu.make_async_remote_copy(
        src_ref=src,
        dst_ref=dst,
        send_sem=sems.at[(0,) + at],
        recv_sem=sems.at[(1,) + at],
        device_id=device,
        device_id_type=MESH,
    )


def greet(rep, place, replicas, shards_n):
    barrier = pltpu.get_barrier_semaphore()
    bits = replicas.bit_length() - 1
    for bit in range(bits):
        pl.semaphore_signal(
            barrier, inc=1, device_id={"replica": flip(rep, bit)}, device_id_type=MESH
        )
    for step in range(1, shards_n):
        pl.semaphore_signal(
            barrier,
            inc=1,
            device_id={"shard": lax.rem(place + step, shards_n)},
            device_id_type=MESH,
        )
    pl.semaphore_wait(barrier, bits + shards_n - 1)


TILE = 256
TALL = 512


def causal_probs(query, key, first, row):
    shape = (query.shape[0], key.shape[0])
    scores = dot_cols(query, key) * (1.0 / math.sqrt(HEAD))
    at = lax.broadcasted_iota(jnp.int32, shape, 1)
    upto = lax.broadcasted_iota(jnp.int32, shape, 0) + row
    scores = jnp.where((at >= first) & (at <= upto), scores, NEG_LARGE)
    shifted = jnp.exp(scores - jnp.max(scores, -1, keepdims=True))
    return shifted / jnp.sum(shifted, -1, keepdims=True)


def forward_kernel(
    replicas,
    shards_n,
    small_ref,
    up_ref,
    qkv_ref,
    x_ref,
    g_ref,
    down_ref,
    proj_ref,
    bias_ref,
    frequency_ref,
    lengths_ref,
    small_out,
    up_out,
    qkv_out,
    x_out,
    g_out,
    mlp_out,
    attn_out,
    act_out,
    slope_out,
    heads_out,
    mixed_out,
    branch_out,
    stats_out,
    tables_out,
    first_out,
    small_low,
    small,
    x_rows,
    mlp,
    attn,
    up,
    qkv,
    act,
    slope,
    heads,
    mixed,
    down,
    proj,
    branch,
    own_sem,
    load_sem,
    keep_sem,
    small_sem,
    turn_sem,
    plane_sem,
    hop_sem,
    g_sem,
):
    rep, place = lax.axis_index("replica"), lax.axis_index("shard")
    bits = replicas.bit_length() - 1
    width, hidden = up_out.shape
    part = width // shards_n
    wide = qkv_out.shape[2]
    rows = part // replicas
    tokens = x_out.shape[0]
    local = tokens // shards_n
    cols = down.shape[2]
    orders = [order + [0] for order in plane_orders(replicas)]
    starts = []
    for order in orders:
        start = 0
        for level, bit in enumerate(order):
            start = start + bit_of(rep, bit) * (rows << level)
        starts.append(start)

    items = [(thing, step) for thing in range(2) for step in range(1, shards_n)]

    def source(third, shard, path):
        some = pl.ds(pl.multiple_of(starts[path], rows), rows)
        if third is None:
            at = shard * hidden + path * (hidden // 2)
            return up_ref.at[some, pl.ds(pl.multiple_of(at, 128), hidden // 2)]
        at = third * width + shard * wide + path * (wide // 2)
        return qkv_ref.at[some, pl.ds(pl.multiple_of(at, 128), wide // 2)]

    def target(third, shard, start, count, path):
        some = pl.ds(pl.multiple_of(shard * part + start, rows), count)
        if third is None:
            return up_out.at[some, pl.ds(path * (hidden // 2), hidden // 2)]
        return qkv_out.at[third, some, pl.ds(path * (wide // 2), wide // 2)]

    def turned(item, path, sending):
        thing, step = items[item]
        to = lax.rem(place + step, shards_n)
        shard = place if sending else lax.rem(place - step + shards_n, shards_n)
        return [
            remote(
                source(third, to, path),
                target(third, shard, starts[path], rows, path),
                turn_sem,
                (item, path, third or 0),
                {"shard": to},
            )
            for third in (range(3) if thing else (None,))
        ]

    def spread(item, path, level):
        thing, step = items[item]
        shard = lax.rem(place - step + shards_n, shards_n)
        order = orders[path]
        start = 0
        for above in range(level, bits):
            start = start + bit_of(rep, order[above]) * (rows << above)
        here = target(pl.ds(0, 3) if thing else None, shard, start, rows << level, path)
        return remote(
            here, here, plane_sem, (item, path, level), {"replica": flip(rep, order[level])}
        )

    def small_copy(step, sending):
        to = lax.rem(place + step, shards_n)
        shard = place if sending else lax.rem(place - step + shards_n, shards_n)
        return remote(small_ref, small_out.at[shard], small_sem, (step,), {"shard": to})

    def column_tick(tick):
        for level in reversed(range(bits + 1)):
            item = tick - level
            if not 0 <= item < len(items):
                continue
            for path in range(2):
                if level == 0:
                    for copy in turned(item, path, False):
                        copy.wait_recv()
                else:
                    spread(item, path, level - 1).wait_recv()
                if level < bits:
                    spread(item, path, level).start()

    def block_rows(block):
        return pl.ds(pl.multiple_of(block * local, local), local)

    def hop(way, step, sending):
        sign = 1 - 2 * way
        block = place - sign * (step if sending else step + 1)
        there = x_out.at[block_rows(block), :]
        return remote(
            x_ref if sending and step == 0 else there,
            there,
            hop_sem,
            (way, step),
            {"shard": lax.rem(place + sign + shards_n, shards_n)},
        )

    def upstream_copy(step, sending):
        to = lax.rem(place + step, shards_n)
        shard = place if sending else lax.rem(place - step + shards_n, shards_n)
        return remote(g_ref, g_out.at[block_rows(shard), :], g_sem, (step,), {"shard": to})

    def holds(way, step):
        return place >= step if way == 0 else place + step < shards_n

    def goes(way, step):
        onward = place + 1 < shards_n if way == 0 else place >= 1
        return holds(way, step) & onward

    def send_hop(step):
        for way in range(2):

            @pl.when(goes(way, step))
            def _():
                hop(way, step, True).start()

    def pass_on(step):
        for way in range(2):

            @pl.when(holds(way, step))
            def _():
                hop(way, step - 1, False).wait_recv()

        if step + 1 < shards_n:
            send_hop(step)

    def load(number, src, dst):
        return pltpu.make_async_copy(src, dst, load_sem.at[number])

    def keep(number, src, dst):
        return pltpu.make_async_copy(src, dst, keep_sem.at[number])

    def norm(block, from_ref, slot):
        copy = load(slot, from_ref, x_rows.at[slot])
        copy.start()
        copy.wait()

        def some_rows(i, carry):
            here = pl.ds(pl.multiple_of(i * 32, 32), 32)
            there = pl.ds(pl.multiple_of(block * local + i * 32, 32), 32)
            values = x_rows[slot, here, :].astype(jnp.float32)
            mean = jnp.mean(values, -1, keepdims=True)
            centered = values - mean
            scale = lax.rsqrt(jnp.mean(centered * centered, -1, keepdims=True) + EPSILON)
            stats_out[0, there, :] = mean
            stats_out[1, there, :] = scale
            normed = centered * scale
            for z in range(shards_n):
                lanes = slice(z * part, (z + 1) * part)
                some = normed[:, lanes]
                attn[there, lanes] = (some * small[z, 0:1, :] + small[z, 1:2, :]).astype(jnp.bfloat16)
                mlp[there, lanes] = (some * small[z, 3:4, :] + small[z, 4:5, :]).astype(jnp.bfloat16)
            return carry

        lax.fori_loop(0, local // 32, some_rows, 0)

    def hidden_units(block):
        here = block_rows(block)

        def some_cols(k, carry):
            lanes = pl.ds(pl.multiple_of(k * cols, cols), cols)
            found = dot(mlp[here, :], up[:, lanes]) + bias_ref[0:1, lanes]
            cdf = 0.5 * (1.0 + lax.erf(found * math.sqrt(0.5)))
            act[here, lanes] = (found * cdf).astype(jnp.bfloat16)
            bell = jnp.exp(-0.5 * found * found) * (1.0 / math.sqrt(2.0 * math.pi))
            slope[here, lanes] = (cdf + found * bell).astype(jnp.bfloat16)
            return carry

        lax.fori_loop(0, hidden // cols, some_cols, 0)

    def tables(i, carry):
        some = local // 2
        here = pl.ds(pl.multiple_of(i * some, some), some)
        token = lax.broadcasted_iota(jnp.int32, (some, 128), 0) + i * some
        lane = lax.broadcasted_iota(jnp.int32, (some, 128), 1)
        first, end = jnp.zeros((some, 128), jnp.int32), 0
        for j in range(lengths_ref.shape[1]):
            length = lengths_ref[0, j]
            end = end + length
            first = first + jnp.where(token >= end, length, 0)
        first_out[here, :] = first[:, :1]
        angles = (token - first).astype(jnp.float32) * frequency_ref[0:1, :]
        sine = jnp.sin(angles)
        tables_out[0, here, :] = jnp.where(lane < ROT, jnp.cos(angles), 1.0)
        tables_out[1, here, :] = jnp.where(lane < ROT // 2, sine, 0.0)
        tables_out[2, here, :] = jnp.where((lane >= ROT // 2) & (lane < ROT), sine, 0.0)
        return carry

    def on_step(step, todo):
        for way in range(2):
            if step == 0 and way == 1:
                continue
            block = place - (1 - 2 * way) * step

            @pl.when(holds(way, step))
            def _():
                todo(block, way)

    def project(third):
        number = third * shards_n + place
        bias = small[lax.div(number, 3), pl.ds(6 + lax.rem(number, 3), 1), :]

        def some_rows(i, carry):
            here = pl.ds(pl.multiple_of(i * TALL, TALL), TALL)
            found = dot(attn[here, :], qkv[third]) + bias
            for head in range(wide // HEAD):
                mine = found[:, head * HEAD : (head + 1) * HEAD]
                if third < 2:
                    lead = mine[:, :128]
                    lead = (
                        lead * tables_out[0, here, :]
                        - pltpu.roll(lead, 96, 1) * tables_out[1, here, :]
                        + pltpu.roll(lead, 32, 1) * tables_out[2, here, :]
                    )
                    mine = jnp.concatenate([lead, mine[:, 128:]], 1)
                heads[third, here, head * HEAD : (head + 1) * HEAD] = mine.astype(jnp.bfloat16)
            return carry

        lax.fori_loop(0, tokens // TALL, some_rows, 0)

    def attend(head):
        lanes = slice(head * HEAD, (head + 1) * HEAD)
        for i in range(tokens // TILE):
            here, keys = slice(i * TILE, (i + 1) * TILE), slice(0, (i + 1) * TILE)
            probs = causal_probs(heads[0, here, lanes], heads[1, keys, lanes], first_out[here, :], i * TILE)
            mixed[here, lanes] = dot(probs.astype(jnp.bfloat16), heads[2, keys, lanes]).astype(jnp.bfloat16)

    def down_load(j):
        return load(4 + j % 2, down_ref.at[:, pl.ds(j * cols, cols)], down.at[j % 2])

    def branch_keep(j):
        return keep(6 + j, branch.at[j % 2], branch_out.at[:, pl.ds(j * cols, cols)])

    def branch_cols(j):
        down_load(j).wait()
        if j >= 2:
            branch_keep(j - 2).wait()

        def some_rows(i, carry):
            here = pl.ds(pl.multiple_of(i * TALL, TALL), TALL)
            found = dot(act[here, :], down[j % 2]) + dot(mixed[here, :], proj[:, j * cols : (j + 1) * cols])
            branch[j % 2, here, :] = found.astype(jnp.bfloat16)
            return carry

        lax.fori_loop(0, tokens // TALL, some_rows, 0)
        branch_keep(j).start()
        if j + 2 < width // cols:
            down_load(j + 2).start()

    greet(rep, place, replicas, shards_n)
    for step in range(1, shards_n):
        small_copy(step, True).start()
    for item in range(shards_n - 1):
        for path in range(2):
            for copy in turned(item, path, True):
                copy.start()
    send_hop(0)
    own = [
        (small_ref, small_out.at[place]),
        (
            up_ref.at[:, pl.ds(pl.multiple_of(place * hidden, 128), hidden)],
            up_out.at[pl.ds(pl.multiple_of(place * part, part), part), :],
        ),
        (x_ref, x_out.at[block_rows(place), :]),
        (g_ref, g_out.at[block_rows(place), :]),
    ] + [
        (
            qkv_ref.at[:, pl.ds(pl.multiple_of(third * width + place * wide, 128), wide)],
            qkv_out.at[third, pl.ds(pl.multiple_of(place * part, part), part), :],
        )
        for third in range(3)
    ]
    own = [pltpu.make_async_copy(src, dst, own_sem.at[i]) for i, (src, dst) in enumerate(own)]
    for copy in own:
        copy.start()
    down_load(0).start()
    down_load(1).start()
    load_proj = load(6, proj_ref, proj)
    load_proj.start()

    lax.fori_loop(0, 2 * shards_n, tables, 0)
    for step in range(1, shards_n):
        small_copy(step, False).wait()
    own[0].wait()
    load_small = load(0, small_out, small_low)
    load_small.start()
    load_small.wait()
    small[...] = small_low[...].astype(jnp.float32)
    on_step(0, lambda block, way: norm(block, x_ref, way))

    load_up = load(2, up_out, up)
    load_qkv = load(3, qkv_out, qkv)
    ticks = list(range(len(items) + bits))

    def some_ticks(number):
        for tick in ticks[:number]:
            column_tick(tick)
        del ticks[:number]

    def send_upstream(to_ends):
        for other in range(1, shards_n):
            to = lax.rem(place + other, shards_n)
            at_end = (to == 0) | (to == shards_n - 1)

            @pl.when(at_end if to_ends else jnp.logical_not(at_end))
            def _():
                upstream_copy(other, True).start()

    def arrive(step):
        pass_on(step)
        if step == 1:
            for item in range(shards_n - 1, len(items)):
                for path in range(2):
                    for copy in turned(item, path, True):
                        copy.start()
        if step == shards_n - 2:
            send_upstream(False)
        on_step(step, lambda block, way: norm(block, x_out.at[block_rows(block), :], way))

    some_ticks(3)
    arrive(1)
    some_ticks(shards_n - 1 + bits - 3)
    own[1].wait()
    load_up.start()
    load_up.wait()
    on_step(0, lambda block, way: hidden_units(block))
    for step in range(2, shards_n - 1):
        arrive(step)
    some_ticks(1)
    on_step(1, lambda block, way: hidden_units(block))
    some_ticks(1)
    for way in range(2):

        @pl.when(goes(way, shards_n - 2))
        def _():
            hop(way, shards_n - 2, True).wait_send()

    send_upstream(True)
    some_ticks(len(ticks))
    arrive(shards_n - 1)
    keeps = [keep(0, mlp, mlp_out), keep(1, attn, attn_out)]
    keeps[0].start()
    keeps[1].start()
    for copy in own[4:]:
        copy.wait()
    load_qkv.start()
    for step in range(2, shards_n):
        on_step(step, lambda block, way: hidden_units(block))
    keeps += [keep(2, act, act_out), keep(3, slope, slope_out)]
    keeps[2].start()
    keeps[3].start()
    load_qkv.wait()
    for third in range(3):
        project(third)
    keeps.append(keep(4, heads, heads_out))
    keeps[4].start()
    for head in range(wide // HEAD):
        attend(head)
    keeps.append(keep(5, mixed, mixed_out))
    keeps[5].start()
    load_proj.wait()
    for j in range(width // cols):
        branch_cols(j)
    for step in range(1, shards_n):
        upstream_copy(step, False).wait()
    for j in range(max(width // cols - 2, 0), width // cols):
        branch_keep(j).wait()
    for copy in keeps:
        copy.wait()
    for item in range(len(items)):
        for path in range(2):
            for copy in turned(item, path, True):
                copy.wait_send()
            for level in range(bits):
                spread(item, path, level).wait_send()
    for step in range(shards_n - 2):
        for way in range(2):

            @pl.when(goes(way, step))
            def _():
                hop(way, step, True).wait_send()

    for copy in own[2:4]:
        copy.wait()


def forward(small, up_weight, qkv_weight, x, g, down_weight, proj_weight, bias, frequency, lengths):
    replicas, count = lax.axis_size("replica"), lax.axis_size("shard")
    bits = replicas.bit_length() - 1
    local, width = x.shape
    tokens = local * count
    hidden, wide = up_weight.shape[1] // count, width // count
    cols = wide
    items = 2 * (count - 1)
    any_spec = pl.BlockSpec(memory_space=pl.ANY)
    vmem_spec = pl.BlockSpec(memory_space=pltpu.VMEM)
    shapes = dict(
        small=(count,) + small.shape,
        up_cols=(width, hidden),
        qkv_cols=(3, width, wide),
        x=(tokens, width),
        g=(tokens, width),
        mlp_in=(tokens, width),
        attn_in=(tokens, width),
        act=(tokens, hidden),
        slope=(tokens, hidden),
        heads=(3, tokens, wide),
        mixed=(tokens, wide),
        branch=(tokens, width),
    )
    low = lambda *shape: pltpu.VMEM(shape, jnp.bfloat16)
    dma = lambda *shape: pltpu.SemaphoreType.DMA(shape)
    found = pl.pallas_call(
        partial(forward_kernel, replicas, count),
        out_shape=tuple(jax.ShapeDtypeStruct(shape, jnp.bfloat16) for shape in shapes.values())
        + (
            jax.ShapeDtypeStruct((2, tokens, 1), jnp.float32),
            jax.ShapeDtypeStruct((3, tokens, 128), jnp.float32),
            jax.ShapeDtypeStruct((tokens, 1), jnp.int32),
        ),
        in_specs=[any_spec] * 7 + [vmem_spec] * 2 + [pl.BlockSpec(memory_space=pltpu.SMEM)],
        out_specs=(any_spec,) * len(shapes) + (vmem_spec,) * 3,
        scratch_shapes=[
            low(*shapes["small"]),
            pltpu.VMEM(shapes["small"], jnp.float32),
            low(2, local, width),
            low(tokens, width),
            low(tokens, width),
            low(width, hidden),
            low(3, width, wide),
            low(tokens, hidden),
            low(tokens, hidden),
            low(3, tokens, wide),
            low(tokens, wide),
            low(2, hidden, cols),
            low(wide, width),
            low(2, tokens, cols),
            dma(7),
            dma(7),
            dma(6 + width // cols),
            dma(2, count),
            dma(2, items, 2, 3),
            dma(2, items, 2, bits),
            dma(2, 2, count - 1),
            dma(2, count),
        ],
        compiler_params=pltpu.CompilerParams(
            collective_id=0, has_side_effects=True, vmem_limit_bytes=58 * 2**20
        ),
        cost_estimate=pl.CostEstimate(
            flops=2 * tokens * width * (hidden * 2 + wide * 4),
            bytes_accessed=500_000_000,
            transcendentals=0,
        ),
    )(small, up_weight, qkv_weight, x, g, down_weight, proj_weight, bias, frequency, lengths)
    return dict(zip(list(shapes) + ["stats", "tables", "first"], found))


RING = 3


def grads_kernel(
    replicas,
    shards_n,
    act_ref,
    up_ref,
    mixed_ref,
    mlp_ref,
    attn_ref,
    slope_ref,
    down_ref,
    proj_ref,
    heads_ref,
    rows_ref,
    cols_up_ref,
    cols_qkv_ref,
    tables_ref,
    first_ref,
    stats_ref,
    small_ref,
    out_ref,
    vec_out,
    sum_out,
    work,
    from_core,
    *rest,
):
    rep, place = lax.axis_index("replica"), lax.axis_index("shard")
    bits = replicas.bit_length() - 1
    far = bits - 1
    from_far = rest[:far]
    (
        big,
        narrow,
        pre,
        joined,
        wide_rows,
        slope,
        heads,
        key_sum,
        value_sum,
        tile_x,
        tile_up,
        tile_qkv,
        shared,
        vec_got,
        vec_sum,
        load_sem,
        core_sem,
        far_sem,
        turn_sem,
        own_sem,
        plane_sem,
        vec_sem,
        sum_sem,
    ) = rest[far:]
    chunks, _, rows, cols = out_ref.shape
    slots = work.shape[0]
    half, side = rows // 2, cols // 2
    piece = rows // replicas
    orders = plane_orders(replicas)
    core = bit_of(rep, 0)
    tokens, width = up_ref.shape
    local = tokens // shards_n
    hiddens = pre.shape[1] // cols
    natives = hiddens + 1
    mine = pl.multiple_of(core * half, half)
    theirs = pl.multiple_of((1 - core) * half, half)

    starts = []
    for order in orders:
        line, size = [core * half], half
        for bit in order:
            size //= 2
            line.append(line[-1] + bit_of(rep, bit) * size)
        starts.append(line)

    def spot(k):
        if k < natives:
            return k + hiddens
        return k - natives if k < natives + hiddens else k

    def load(source, target, number):
        return pltpu.make_async_copy(source, target, load_sem.at[number])

    def narrow_load(k):
        source = act_ref.at[:, pl.ds(k * cols, cols)] if k < hiddens else mixed_ref
        return load(source, narrow.at[k % 2], k % 2)

    def big_load(which):
        return load((up_ref, mlp_ref, attn_ref)[which], big.at[which % 2], 2 + which)

    def down_load(k):
        return load(down_ref.at[pl.ds(k * cols, cols), :], wide_rows.at[k % 2], 5 + k % 2)

    def slope_load(k):
        return load(slope_ref.at[:, pl.ds(k * cols, cols)], slope.at[k % 2], 7 + k % 2)

    def pre_loads(k):
        return [down_load(k), slope_load(k)]

    def proj_load():
        return load(proj_ref, wide_rows.at[1], 6)

    def heads_load():
        return load(heads_ref, heads.at[pl.ds(0, 3)], 9)

    def tile_loads(j):
        some = pl.ds(j * TILE, TILE)
        return [
            load(rows_ref.at[:, some], tile_x.at[j % 2], 10 + j % 2),
            load(cols_up_ref.at[some, :], tile_up.at[j % 2], 12 + j % 2),
        ] + [
            load(
                cols_qkv_ref.at[third, some, :],
                tile_qkv.at[j % 2, :, pl.ds(third * cols, cols)],
                14 + 2 * third + j % 2,
            )
            for third in range(3)
        ]

    def to_core(k):
        return remote(
            work.at[k % slots, :, pl.ds(theirs, half), :],
            from_core.at[k % RING],
            core_sem,
            (0, k),
            {"replica": flip(rep, 0)},
        )

    def to_far(k, level, path):
        size = half >> (level + 1)
        bit = orders[path][level]
        start = starts[path][level] + (1 - bit_of(rep, bit)) * size
        return remote(
            work.at[k % slots, :, pl.ds(pl.multiple_of(start, size), size), pl.ds(path * side, side)],
            from_far[level].at[k % RING, path],
            far_sem,
            (k, level, path),
            {"replica": flip(rep, bit)},
        )

    def own_piece(k, path, block):
        return work.at[
            k % slots,
            block,
            pl.ds(pl.multiple_of(starts[path][far], piece), piece),
            pl.ds(path * side, side),
        ]

    def place_piece(k, path, block):
        return out_ref.at[
            spot(k),
            block,
            pl.ds(pl.multiple_of(starts[path][far], piece), piece),
            pl.ds(path * side, side),
        ]

    def settle(k, path):
        block = pl.ds(0, shards_n) if k < natives else place
        return pltpu.make_async_copy(
            own_piece(k, path, block), place_piece(k, path, block), own_sem.at[k % 2, path]
        )

    def turned(k, path, step, sending):
        to = lax.rem(place + step, shards_n)
        shard = place if sending else lax.rem(place - step + shards_n, shards_n)
        return remote(
            own_piece(k, path, to),
            place_piece(k, path, shard),
            turn_sem,
            (k - natives, path, step - 1),
            {"shard": to},
        )

    def spread(k, path, level):
        size = piece << level
        bit = orders[path][far - 1 - level]
        here = out_ref.at[
            spot(k),
            :,
            pl.ds(pl.multiple_of(starts[path][far - level], size), size),
            pl.ds(path * side, side),
        ]
        return remote(here, here, plane_sem, (k, level, path), {"replica": flip(rep, bit)})

    def spread_core(k):
        here = out_ref.at[spot(k), :, pl.ds(mine, half), :]
        return remote(here, here, core_sem, (1, k), {"replica": flip(rep, 0)})

    def put(offset, sums):
        for i in range(sums.shape[1] // 128):
            vec_sum[pl.ds(offset // 128 + i, 1), :] = sums[:, i * 128 : (i + 1) * 128]

    def compute(k):
        if k < natives:
            narrow_load(k).wait()
            if k + 1 < natives:
                narrow_load(k + 1).start()
        if k == 0:
            big_load(0).wait()
        if k == natives:
            big_load(1).wait()
        if k == natives + hiddens:
            big_load(2).wait()
        slot = k % slots
        which = 1 if natives <= k < natives + hiddens else 0

        def block(g, carry):
            if k < natives:
                left = narrow[k % 2]
                right = big[which, :, pl.ds(pl.multiple_of(g * cols, cols), cols)]
            else:
                left = big[which, :, pl.ds(pl.multiple_of(g * rows, rows), rows)]
                if k < natives + hiddens:
                    right = pre[:, (k - natives) * cols : (k - natives + 1) * cols]
                else:
                    third = k - natives - hiddens
                    right = joined[:, third * cols : (third + 1) * cols]
            work[slot, g] = dot_rows(left, right).astype(jnp.bfloat16)
            return carry

        lax.fori_loop(0, shards_n, block, 0)
        to_core(k).start()

    def add(k, start, size, left, width, got):
        def block(g, carry):
            where = (k % slots, g, pl.ds(pl.multiple_of(start, size), size), pl.ds(left, width))
            work[where] = (
                work[where].astype(jnp.float32) + got(g).astype(jnp.float32)
            ).astype(jnp.bfloat16)
            return carry

        lax.fori_loop(0, shards_n, block, 0)

    def grad_mixed():
        proj_load().wait()

        def block(i, carry):
            some = pl.ds(pl.multiple_of(i * TALL, TALL), TALL)
            heads[3, some, :] = dot_cols(big[0, some, :], wide_rows[1]).astype(jnp.bfloat16)
            return carry

        lax.fori_loop(0, tokens // TALL, block, 0)
        down_load(1).start()
        own = pl.ds(pl.multiple_of(place * cols, cols), cols)
        put(4 * width + place * cols, jnp.sum(big[0, :, own].astype(jnp.float32), 0, keepdims=True))

    def grad_pre(k):
        for copy in pre_loads(k):
            copy.wait()

        def block(i, total):
            some = pl.ds(pl.multiple_of(i * TALL, TALL), TALL)
            found = dot_cols(big[0, some, :], wide_rows[k % 2]) * slope[k % 2, some, :].astype(
                jnp.float32
            )
            low = found.astype(jnp.bfloat16)
            pre[some, k * cols : (k + 1) * cols] = low
            return total + jnp.sum(low.astype(jnp.float32), 0, keepdims=True)

        total = lax.fori_loop(0, tokens // TALL, block, jnp.zeros((1, cols), jnp.float32))
        put(8 * width + (place * hiddens + k) * cols, total)
        if k + 2 < hiddens:
            for copy in pre_loads(k + 2):
                copy.start()

    def turn_rows(found, some):
        lead = found[:, :128]
        lead = (
            lead * tables_ref[0, some, :]
            + pltpu.roll(lead, 96, 1) * tables_ref[1, some, :]
            - pltpu.roll(lead, 32, 1) * tables_ref[2, some, :]
        )
        return jnp.concatenate([lead, found[:, 128:]], 1)

    def attention(head):
        lanes = pl.ds(head * HEAD, HEAD)
        scale = 1.0 / math.sqrt(HEAD)
        key_sum[...] = jnp.zeros_like(key_sum)
        value_sum[...] = jnp.zeros_like(value_sum)
        sums = [jnp.zeros((1, HEAD), jnp.float32)] * 3
        for i in range(tokens // TILE):
            some, keys = pl.ds(i * TILE, TILE), pl.ds(0, (i + 1) * TILE)
            query = heads[0, some, lanes]
            key = heads[1, keys, lanes]
            probs = causal_probs(query, key, first_ref[some, :], i * TILE)
            grad = heads[3, some, lanes]
            grad_probs = dot_cols(grad, heads[2, keys, lanes])
            delta = jnp.sum(probs * grad_probs, -1, keepdims=True)
            low = (probs * (grad_probs - delta)).astype(jnp.bfloat16)
            found = turn_rows(dot(low, key) * scale, some).astype(jnp.bfloat16)
            joined[some, pl.ds(head * HEAD, HEAD)] = found
            sums[0] = sums[0] + jnp.sum(found.astype(jnp.float32), 0, keepdims=True)
            key_sum[keys, :] = key_sum[keys, :] + dot_rows(low, query)
            value_sum[keys, :] = value_sum[keys, :] + dot_rows(probs.astype(jnp.bfloat16), grad)
        for i in range(tokens // TILE):
            some = pl.ds(i * TILE, TILE)
            for third, found in (
                (1, turn_rows(key_sum[some, :] * scale, some)),
                (2, value_sum[some, :]),
            ):
                low = found.astype(jnp.bfloat16)
                joined[some, pl.ds(third * cols + head * HEAD, HEAD)] = low
                sums[third] = sums[third] + jnp.sum(low.astype(jnp.float32), 0, keepdims=True)
        for third in range(3):
            put(5 * width + third * width + place * cols + head * HEAD, sums[third])

    def sum_part(j, step, sending):
        to = lax.rem(place + step, shards_n)
        shard = place if sending else lax.rem(place - step + shards_n, shards_n)
        some = pl.ds(j * TILE, TILE)
        source = shared.at[pl.ds(pl.multiple_of(to * local, local), local), some]
        if step == 0:
            return pltpu.make_async_copy(source, sum_out.at[place, :, some], sum_sem.at[0, j, 0])
        return remote(source, sum_out.at[shard, :, some], sum_sem, (j, step), {"shard": to})

    def tile(j):
        for copy in tile_loads(j):
            copy.wait()
        if j + 1 < width // TILE:
            for copy in tile_loads(j + 1):
                copy.start()
        lanes = pl.ds(j * TILE, TILE)
        owner, begin = divmod(j * TILE, cols)
        theirs_at = slice(begin, begin + TILE)

        def block(i, totals):
            some = pl.ds(pl.multiple_of(i * TALL, TALL), TALL)
            normed = (tile_x[j % 2, some, :].astype(jnp.float32) - stats_ref[0, some, :]) * stats_ref[
                1, some, :
            ]
            mlp = dot_cols(pre[some, :], tile_up[j % 2])
            attn = dot_cols(joined[some, :], tile_qkv[j % 2])
            shared[some, lanes] = (
                attn * small_ref[owner, 0:1, theirs_at].astype(jnp.float32)
                + mlp * small_ref[owner, 3:4, theirs_at].astype(jnp.float32)
            ).astype(jnp.bfloat16)
            found = (attn * normed, attn, mlp * normed, mlp)
            return tuple(t + jnp.sum(f, 0, keepdims=True) for t, f in zip(totals, found))

        zero = jnp.zeros((1, TILE), jnp.float32)
        totals = lax.fori_loop(0, tokens // TALL, block, (zero,) * 4)
        for number, total in enumerate(totals):
            put(number * width + j * TILE, total)
        for step in range(shards_n):
            sum_part(j, step, True).start()

    def stage(k, number):
        if number == 0:
            compute(k)
        elif number == 1:
            to_core(k).wait()
            add(k, mine, half, 0, cols, lambda g: from_core[k % RING, g])
            for path in range(2):
                to_far(k, 0, path).start()
        elif number <= 1 + far:
            level = number - 2
            for path in range(2):
                to_far(k, level, path).wait()
                size = half >> (level + 1)
                add(
                    k,
                    starts[path][level + 1],
                    size,
                    path * side,
                    side,
                    lambda g: from_far[level][k % RING, path, g],
                )
                if level + 1 < far:
                    to_far(k, level + 1, path).start()
                else:
                    if k >= natives:
                        for step in range(1, shards_n):
                            turned(k, path, step, True).start()
                    settle(k, path).start()
        elif number == 2 + far:
            for path in range(2):
                settle(k, path).wait()
                if k >= natives:
                    for step in range(1, shards_n):
                        turned(k, path, step, False).wait_recv()
                spread(k, path, 0).start()
            if k >= natives:
                for path in range(2):
                    for step in range(1, shards_n):
                        turned(k, path, step, True).wait_send()
        elif number <= 2 + 2 * far:
            level = number - 3 - far
            for path in range(2):
                spread(k, path, level).wait()
                if level + 1 < far:
                    spread(k, path, level + 1).start()
            if level + 1 == far:
                spread_core(k).start()
        else:
            spread_core(k).wait()

    stages = 4 + 2 * far
    n_heads, n_tiles = cols // HEAD, width // TILE
    extras = {0: [grad_mixed, partial(grad_pre, 0)]}
    for k in range(1, hiddens):
        extras.setdefault(k, []).append(partial(grad_pre, k))
    for head in range(n_heads):
        extras.setdefault(1 + head, []).append(partial(attention, head))
    extras[hiddens] = [big_load(2).start]
    tile_at = hiddens + 1
    for j in range(n_tiles):
        extras.setdefault(tile_at + j, []).append(partial(tile, j))
    vec_at = max(extras) + 1

    for copy in [narrow_load(0), big_load(0), proj_load()] + pre_loads(0):
        copy.start()
    slope_load(1).start()
    for copy in [heads_load(), big_load(1)] + tile_loads(0):
        copy.start()
    vec_sum[...] = jnp.zeros_like(vec_sum)
    greet(rep, place, replicas, shards_n)
    peers = [{"replica": flip(rep, bit)} for bit in range(bits)]
    peers += [{"shard": flip(place, bit)} for bit in range(shards_n.bit_length() - 1)]

    def vec_copy(number):
        return remote(vec_sum, vec_got.at[number], vec_sem, (number,), peers[number])

    for tick in range(max(chunks + stages - 1, vec_at + len(peers) + 1)):
        for number in reversed(range(stages)):
            if 0 <= tick - number < chunks:
                stage(tick - number, number)
        if tick == 0:
            heads_load().wait()
        for extra in extras.get(tick, []):
            extra()
        turn_of = tick - vec_at
        if 0 < turn_of <= len(peers):
            vec_copy(turn_of - 1).wait()
            vec_sum[...] = vec_sum[...] + vec_got[turn_of - 1]
        if 0 <= turn_of < len(peers):
            vec_copy(turn_of).start()
    vec_out[...] = vec_sum[...]
    for j in range(n_tiles):
        for step in range(shards_n):
            sum_part(j, step, False).wait()


def summed_grads(*operands):
    act, up, mixed, mlp_in = operands[:4]
    replicas, count = lax.axis_size("replica"), lax.axis_size("shard")
    bits = replicas.bit_length() - 1
    far = bits - 1
    tokens, width = up.shape
    cols = width // count
    hidden = act.shape[1]
    hiddens = hidden // cols
    natives = hiddens + 1
    chunks = natives + hiddens + 3
    peers = bits + count.bit_length() - 1
    slots = 2 + far
    vector = ((8 * width + count * hidden) // 128, 128)
    any_spec = pl.BlockSpec(memory_space=pl.ANY)
    vmem_spec = pl.BlockSpec(memory_space=pltpu.VMEM)
    low = lambda *shape: pltpu.VMEM(shape, jnp.bfloat16)
    full = lambda *shape: pltpu.VMEM(shape, jnp.float32)
    dma = lambda *shape: pltpu.SemaphoreType.DMA(shape)
    return pl.pallas_call(
        partial(grads_kernel, replicas, count),
        out_shape=(
            jax.ShapeDtypeStruct((chunks, count, cols, cols), jnp.bfloat16),
            jax.ShapeDtypeStruct(vector, jnp.float32),
            jax.ShapeDtypeStruct((count, tokens // count, width), jnp.bfloat16),
        ),
        in_specs=[any_spec] * 12 + [vmem_spec] * 4,
        out_specs=(any_spec, vmem_spec, any_spec),
        scratch_shapes=[
            low(slots, count, cols, cols),
            low(RING, count, cols // 2, cols),
        ]
        + [low(RING, 2, count, cols >> (level + 2), cols // 2) for level in range(far)]
        + [
            low(2, tokens, width),
            low(2, tokens, cols),
            low(tokens, hidden),
            low(tokens, 3 * cols),
            low(2, cols, width),
            low(2, tokens, cols),
            low(4, tokens, cols),
            full(tokens, HEAD),
            full(tokens, HEAD),
            low(2, tokens, TILE),
            low(2, TILE, hidden),
            low(2, TILE, 3 * cols),
            low(tokens, width),
            full(peers, *vector),
            full(*vector),
            dma(20),
            dma(2, 2, chunks),
            dma(2, chunks, far, 2),
            dma(2, chunks - natives, 2, count - 1),
            dma(2, 2),
            dma(2, chunks, far, 2),
            dma(2, peers),
            dma(2, width // TILE, count),
        ],
        compiler_params=pltpu.CompilerParams(
            collective_id=1, has_side_effects=True, vmem_limit_bytes=60 * 2**20
        ),
        cost_estimate=pl.CostEstimate(
            flops=4 * tokens * chunks * count * cols * cols,
            bytes_accessed=600_000_000,
            transcendentals=0,
        ),
    )(*operands)


def last_kernel(
    up_blocks,
    down_blocks,
    out_blocks,
    qkv_blocks,
    parts_ref,
    branch_ref,
    x_ref,
    g_ref,
    small_ref,
    layer_out,
    input_out,
    up_out,
    down_out,
    out_out,
    qkv_out,
):
    number, count, _, cols = up_blocks.shape
    for g in range(count):
        lanes = slice(g * cols, (g + 1) * cols)
        for k in range(number):
            at = (g * number + k) * cols
            up_out[:, at : at + cols] = up_blocks[k, g].astype(jnp.float32)
        for k in range(3):
            at = (k * count + g) * cols
            qkv_out[:, at : at + cols] = qkv_blocks[k, g].astype(jnp.float32)
        down_out[:, lanes] = down_blocks[0, g].astype(jnp.float32)
        out_out[:, lanes] = out_blocks[0, g].astype(jnp.float32)
    rows = x_ref[...].astype(jnp.float32)
    normed, inverse_std = normalize(rows)
    grad = sum(parts_ref[g].astype(jnp.float32) for g in range(count))
    input_out[...] = g_ref[...].astype(jnp.float32) + norm_backward(grad, normed, inverse_std)
    for g in range(count):
        lanes = slice(g * cols, (g + 1) * cols)
        bias = small_ref[g, 2:3, :].astype(jnp.float32) + small_ref[g, 5:6, :].astype(jnp.float32)
        layer_out[:, lanes] = (
            rows[:, lanes] + branch_ref[:, lanes].astype(jnp.float32) + bias
        ).astype(jnp.bfloat16)


def last(blocks, parts, branch, x, g, small):
    count, rows, cols = blocks.shape[1:]
    number = (blocks.shape[0] - 4) // 2
    local, width = x.shape
    steps = local // 16
    some, tall = rows // steps, number * rows // steps
    turns = rows // tall
    whole = lambda i: (i, 0)
    return pl.pallas_call(
        last_kernel,
        out_shape=(
            jax.ShapeDtypeStruct((local, width), jnp.bfloat16),
            jax.ShapeDtypeStruct((local, width), jnp.float32),
            jax.ShapeDtypeStruct((rows, number * width), jnp.float32),
            jax.ShapeDtypeStruct((number * rows, width), jnp.float32),
            jax.ShapeDtypeStruct((rows, width), jnp.float32),
            jax.ShapeDtypeStruct((rows, 3 * width), jnp.float32),
        ),
        grid=(steps,),
        in_specs=[
            pl.BlockSpec((number, count, some, cols), lambda i: (0, 0, i, 0)),
            pl.BlockSpec((1, count, tall, cols), lambda i: (number + i // turns, 0, i % turns, 0)),
            pl.BlockSpec((1, count, some, cols), lambda i: (2 * number, 0, i, 0)),
            pl.BlockSpec((3, count, some, cols), lambda i: ((2 * number + 1) // 3, 0, i, 0)),
            pl.BlockSpec((count, 16, width), lambda i: (0, i, 0)),
            pl.BlockSpec((16, width), whole),
            pl.BlockSpec((16, width), whole),
            pl.BlockSpec((16, width), whole),
            pl.BlockSpec(small.shape, lambda i: (0, 0, 0)),
        ],
        out_specs=(
            pl.BlockSpec((16, width), whole),
            pl.BlockSpec((16, width), whole),
            pl.BlockSpec((some, number * width), whole),
            pl.BlockSpec((tall, width), whole),
            pl.BlockSpec((some, width), whole),
            pl.BlockSpec((some, 3 * width), whole),
        ),
        compiler_params=pltpu.CompilerParams(vmem_limit_bytes=62 * 2**20),
    )(blocks, blocks, blocks, blocks, parts, branch, x, g, small)


def shards(
    layer_input,
    attn_gain,
    attn_shift,
    qkv_weight,
    qkv_bias,
    out_weight,
    out_bias,
    mlp_gain,
    mlp_shift,
    up_weight,
    up_bias,
    down_weight,
    down_bias,
    seq_lengths,
    upstream,
):
    local_rows = layer_input.shape[0]
    count = lax.axis_size("shard")
    group_rows = local_rows * count
    place = lax.axis_index("shard")
    part = D // count
    hidden = up_bias.shape[0]

    params = [attn_gain, attn_shift, out_bias, mlp_gain, mlp_shift, down_bias]
    params += [qkv_bias[i * part : (i + 1) * part] for i in range(3)]
    row = lax.broadcasted_iota(jnp.int32, (16, part), 0)
    small = jnp.zeros((16, part), jnp.bfloat16)
    for i, param in enumerate(params):
        small = jnp.where(row == i, param[None], small)

    frequency = np.power(np.float32(ROPE_BASE), -np.arange(ROT // 2, dtype=np.float32) * np.float32(2.0 / ROT))
    known = forward(
        small,
        up_weight,
        qkv_weight,
        layer_input,
        upstream,
        down_weight,
        out_weight,
        up_bias.astype(jnp.float32)[None],
        jnp.asarray(np.tile(frequency, 128 // (ROT // 2))[None]),
        seq_lengths,
    )
    branch_own = lax.psum_scatter(known["branch"], "shard", scatter_dimension=0, tiled=True)
    grads, vector, normed_parts = summed_grads(
        known["act"],
        known["g"],
        known["mixed"],
        known["mlp_in"],
        known["attn_in"],
        known["slope"],
        down_weight,
        out_weight,
        known["heads"],
        known["x"],
        known["up_cols"],
        known["qkv_cols"],
        known["tables"],
        known["first"],
        known["stats"],
        known["small"],
    )
    grads, branch_own = lax.optimization_barrier((grads, branch_own))
    vector = vector.reshape(-1)
    layer_output, input_grad, up_grad, down_grad, out_grad, qkv_grad = last(
        grads, normed_parts, branch_own, layer_input, upstream, known["small"]
    )
    own = lambda i: lax.dynamic_slice_in_dim(vector, i * D + place * part, part, 0)
    bias_grad = own(4)
    qkv_bias_grad = lax.dynamic_slice_in_dim(vector, 5 * D + place * 3 * part, 3 * part, 0)
    up_bias_grad = lax.dynamic_slice_in_dim(vector, 8 * D + place * hidden, hidden, 0)
    return (
        layer_output,
        input_grad,
        own(0),
        own(1),
        qkv_grad,
        qkv_bias_grad,
        out_grad,
        bias_grad,
        own(2),
        own(3),
        up_grad,
        up_bias_grad,
        down_grad,
        bias_grad,
    )


def solution(mesh):
    in_specs = (
        P(("replica", "shard"), None),
        P("shard"),
        P("shard"),
        P("shard", None),
        P("shard"),
        P("shard", None),
        P("shard"),
        P("shard"),
        P("shard"),
        P("shard", None),
        P("shard"),
        P("shard", None),
        P("shard"),
        P("replica", None),
        P(("replica", "shard"), None),
    )
    out_specs = (
        P(("replica", "shard"), None),
        P(("replica", "shard"), None),
        P("shard"),
        P("shard"),
        P("shard", None),
        P("shard"),
        P("shard", None),
        P("shard"),
        P("shard"),
        P("shard"),
        P("shard", None),
        P("shard"),
        P("shard", None),
        P("shard"),
    )
    return jax.shard_map(shards, mesh=mesh, in_specs=in_specs, out_specs=out_specs, check_vma=False)
```

```python
from functools import partial
import math

import jax
import jax.numpy as jnp
import numpy as np
from jax import lax
from jax.experimental import pallas as pl
from jax.experimental.pallas import tpu as pltpu
from jax.sharding import PartitionSpec as P

D = 2048
HEADS = 8
HEAD = 256
ROT = 64


EPSILON = 1e-05
ROPE_BASE = 10000.0
NEG_LARGE = -1e30
MESH = pl.DeviceIdType.MESH
CONTRACT_ROWS = (((0,), (0,)), ((), ()))
CONTRACT_COLS = (((1,), (1,)), ((), ()))


def normalize(layer_rows):
    centered = layer_rows - jnp.mean(layer_rows, -1, keepdims=True)
    variance = jnp.mean(centered * centered, -1, keepdims=True)
    inverse_std = lax.rsqrt(variance + EPSILON)
    return (centered * inverse_std, inverse_std)


def norm_backward(grad_normed, normed, inverse_std):
    mean_grad = jnp.mean(grad_normed, -1, keepdims=True)
    mean_cross = jnp.mean(grad_normed * normed, -1, keepdims=True)
    return (grad_normed - mean_grad - normed * mean_cross) * inverse_std


def dot(left, right):
    return jnp.dot(left, right, preferred_element_type=jnp.float32)


def dot_rows(left, right):
    return lax.dot_general(left, right, CONTRACT_ROWS, preferred_element_type=jnp.float32)


def dot_cols(left, right):
    return lax.dot_general(left, right, CONTRACT_COLS, preferred_element_type=jnp.float32)


def bit_of(index, bit):
    return lax.rem(lax.div(index, 1 << bit), 2)


def flip(index, bit):
    return index + (1 << bit) * (1 - 2 * bit_of(index, bit))


def plane_orders(replicas):
    far = list(range(1, replicas.bit_length() - 1))
    return far, far[1:] + far[:1]


def remote(src, dst, sems, at, device):
    return pltpu.make_async_remote_copy(
        src_ref=src,
        dst_ref=dst,
        send_sem=sems.at[(0,) + at],
        recv_sem=sems.at[(1,) + at],
        device_id=device,
        device_id_type=MESH,
    )


def greet(rep, place, replicas, shards_n):
    barrier = pltpu.get_barrier_semaphore()
    bits = replicas.bit_length() - 1
    for bit in range(bits):
        pl.semaphore_signal(
            barrier, inc=1, device_id={"replica": flip(rep, bit)}, device_id_type=MESH
        )
    for step in range(1, shards_n):
        pl.semaphore_signal(
            barrier,
            inc=1,
            device_id={"shard": lax.rem(place + step, shards_n)},
            device_id_type=MESH,
        )
    pl.semaphore_wait(barrier, bits + shards_n - 1)


TILE = 256
TALL = 512


def causal_probs(query, key, first, row):
    count = query.shape[0]
    scores = dot_cols(query, key) * (1.0 / math.sqrt(HEAD))
    at = lax.broadcasted_iota(jnp.int32, scores.shape, 1)
    scores = jnp.where(at >= first, scores, NEG_LARGE)
    ahead = lax.broadcasted_iota(jnp.int32, (count, count), 1) > lax.broadcasted_iota(
        jnp.int32, (count, count), 0
    )
    diagonal = jnp.where(ahead, NEG_LARGE, scores[:, row:])
    scores = jnp.concatenate([scores[:, :row], diagonal], 1) if row else diagonal
    shifted = jnp.exp(scores - jnp.max(scores, -1, keepdims=True))
    return shifted * (1.0 / jnp.sum(shifted, -1, keepdims=True))


ERF_AT = 0.3275911
ERF_TERMS = (0.254829592, -0.284496736, 1.421413741, -1.453152027, 1.061405429)


def gelu_and_slope(found):
    bell = jnp.exp(-0.5 * found * found)
    t = 1.0 / (1.0 + (ERF_AT * math.sqrt(0.5)) * jnp.abs(found))
    series = ERF_TERMS[4]
    for term in ERF_TERMS[3::-1]:
        series = term + t * series
    outside = 0.5 * t * series * bell
    cdf = jnp.where(found >= 0.0, 1.0 - outside, outside)
    return found * cdf, cdf + found * bell * (1.0 / math.sqrt(2.0 * math.pi))


def forward_kernel(
    replicas,
    shards_n,
    small_ref,
    up_ref,
    qkv_ref,
    x_ref,
    g_ref,
    down_ref,
    proj_ref,
    bias_ref,
    frequency_ref,
    lengths_ref,
    small_out,
    up_out,
    qkv_out,
    x_out,
    g_out,
    mlp_out,
    attn_out,
    act_out,
    slope_out,
    heads_out,
    mixed_out,
    branch_out,
    stats_out,
    tables_out,
    first_out,
    small_low,
    small,
    x_rows,
    mlp,
    attn,
    up,
    qkv,
    act,
    slope,
    heads,
    mixed,
    down,
    proj,
    branch,
    own_sem,
    load_sem,
    keep_sem,
    small_sem,
    turn_sem,
    plane_sem,
    hop_sem,
    g_sem,
):
    rep, place = lax.axis_index("replica"), lax.axis_index("shard")
    bits = replicas.bit_length() - 1
    width, hidden = up_out.shape
    part = width // shards_n
    wide = qkv_out.shape[2]
    rows = part // replicas
    tokens = x_out.shape[0]
    local = tokens // shards_n
    cols = down.shape[2]
    orders = [order + [0] for order in plane_orders(replicas)]
    starts = []
    for order in orders:
        start = 0
        for level, bit in enumerate(order):
            start = start + bit_of(rep, bit) * (rows << level)
        starts.append(start)

    items = [(thing, step) for thing in range(2) for step in range(1, shards_n)]

    def source(third, shard, path):
        some = pl.ds(pl.multiple_of(starts[path], rows), rows)
        if third is None:
            at = shard * hidden + path * (hidden // 2)
            return up_ref.at[some, pl.ds(pl.multiple_of(at, 128), hidden // 2)]
        at = third * width + shard * wide + path * (wide // 2)
        return qkv_ref.at[some, pl.ds(pl.multiple_of(at, 128), wide // 2)]

    def target(third, shard, start, count, path):
        some = pl.ds(pl.multiple_of(shard * part + start, rows), count)
        if third is None:
            return up_out.at[some, pl.ds(path * (hidden // 2), hidden // 2)]
        return qkv_out.at[third, some, pl.ds(path * (wide // 2), wide // 2)]

    def turned(item, path, sending):
        thing, step = items[item]
        to = lax.rem(place + step, shards_n)
        shard = place if sending else lax.rem(place - step + shards_n, shards_n)
        return [
            remote(
                source(third, to, path),
                target(third, shard, starts[path], rows, path),
                turn_sem,
                (item, path, third or 0),
                {"shard": to},
            )
            for third in (range(3) if thing else (None,))
        ]

    def spread(item, path, level):
        thing, step = items[item]
        shard = lax.rem(place - step + shards_n, shards_n)
        order = orders[path]
        start = 0
        for above in range(level, bits):
            start = start + bit_of(rep, order[above]) * (rows << above)
        here = target(pl.ds(0, 3) if thing else None, shard, start, rows << level, path)
        return remote(
            here, here, plane_sem, (item, path, level), {"replica": flip(rep, order[level])}
        )

    def small_copy(step, sending):
        to = lax.rem(place + step, shards_n)
        shard = place if sending else lax.rem(place - step + shards_n, shards_n)
        return remote(small_ref, small_out.at[shard], small_sem, (step,), {"shard": to})

    def column_tick(tick):
        for level in reversed(range(bits + 1)):
            item = tick - level
            if not 0 <= item < len(items):
                continue
            for path in range(2):
                if level == 0:
                    for copy in turned(item, path, False):
                        copy.wait_recv()
                else:
                    spread(item, path, level - 1).wait_recv()
                if level < bits:
                    spread(item, path, level).start()

    def block_rows(block):
        return pl.ds(pl.multiple_of(block * local, local), local)

    def hop(way, step, sending):
        sign = 1 - 2 * way
        block = place - sign * (step if sending else step + 1)
        there = x_out.at[block_rows(block), :]
        return remote(
            x_ref if sending and step == 0 else there,
            there,
            hop_sem,
            (way, step),
            {"shard": lax.rem(place + sign + shards_n, shards_n)},
        )

    def upstream_copy(step, sending):
        to = lax.rem(place + step, shards_n)
        shard = place if sending else lax.rem(place - step + shards_n, shards_n)
        return remote(g_ref, g_out.at[block_rows(shard), :], g_sem, (step,), {"shard": to})

    def holds(way, step):
        return place >= step if way == 0 else place + step < shards_n

    def goes(way, step):
        onward = place + 1 < shards_n if way == 0 else place >= 1
        return holds(way, step) & onward

    def send_hop(step):
        for way in range(2):

            @pl.when(goes(way, step))
            def _():
                hop(way, step, True).start()

    def pass_on(step):
        for way in range(2):

            @pl.when(holds(way, step))
            def _():
                hop(way, step - 1, False).wait_recv()

        if step + 1 < shards_n:
            send_hop(step)

    def load(number, src, dst):
        return pltpu.make_async_copy(src, dst, load_sem.at[number])

    def keep(number, src, dst):
        return pltpu.make_async_copy(src, dst, keep_sem.at[number])

    def norm(block, from_ref, slot):
        copy = load(slot, from_ref, x_rows.at[slot])
        copy.start()
        copy.wait()

        def some_rows(i, carry):
            here = pl.ds(pl.multiple_of(i * 64, 64), 64)
            there = pl.ds(pl.multiple_of(block * local + i * 64, 64), 64)
            values = x_rows[slot, here, :].astype(jnp.float32)
            mean = jnp.mean(values, -1, keepdims=True)
            centered = values - mean
            scale = lax.rsqrt(jnp.mean(centered * centered, -1, keepdims=True) + EPSILON)
            stats_out[0, there, :] = mean
            stats_out[1, there, :] = scale
            normed = centered * scale
            for z in range(shards_n):
                lanes = slice(z * part, (z + 1) * part)
                some = normed[:, lanes]
                attn[there, lanes] = (some * small[z, 0:1, :] + small[z, 1:2, :]).astype(jnp.bfloat16)
                mlp[there, lanes] = (some * small[z, 3:4, :] + small[z, 4:5, :]).astype(jnp.bfloat16)
            return carry

        lax.fori_loop(0, local // 64, some_rows, 0)

    broad = hidden // 2

    def hidden_units(block):
        here = block_rows(block)

        def some_cols(k, carry):
            lanes = pl.ds(pl.multiple_of(k * broad, broad), broad)
            found = dot(mlp[here, :], up[:, lanes]) + bias_ref[0:1, lanes]
            value, rise = gelu_and_slope(found)
            act[here, lanes] = value.astype(jnp.bfloat16)
            slope[here, lanes] = rise.astype(jnp.bfloat16)
            return carry

        lax.fori_loop(0, hidden // broad, some_cols, 0)

    def tables(i, carry):
        some = local // 2
        here = pl.ds(pl.multiple_of(i * some, some), some)
        token = lax.broadcasted_iota(jnp.int32, (some, 128), 0) + i * some
        lane = lax.broadcasted_iota(jnp.int32, (some, 128), 1)
        first, end = jnp.zeros((some, 128), jnp.int32), 0
        for j in range(lengths_ref.shape[1]):
            length = lengths_ref[0, j]
            end = end + length
            first = first + jnp.where(token >= end, length, 0)
        first_out[here, :] = first[:, :1]
        angles = (token - first).astype(jnp.float32) * frequency_ref[0:1, :]
        sine = jnp.sin(angles)
        tables_out[0, here, :] = jnp.where(lane < ROT, jnp.cos(angles), 1.0)
        tables_out[1, here, :] = jnp.where(lane < ROT // 2, sine, 0.0)
        tables_out[2, here, :] = jnp.where((lane >= ROT // 2) & (lane < ROT), sine, 0.0)
        return carry

    def on_step(step, todo):
        for way in range(2):
            if step == 0 and way == 1:
                continue
            block = place - (1 - 2 * way) * step

            @pl.when(holds(way, step))
            def _():
                todo(block, way)

    def project(third):
        number = third * shards_n + place
        bias = small[lax.div(number, 3), pl.ds(6 + lax.rem(number, 3), 1), :]

        def some_rows(i, carry):
            here = pl.ds(pl.multiple_of(i * TALL, TALL), TALL)
            found = dot(attn[here, :], qkv[third]) + bias
            for head in range(wide // HEAD):
                mine = found[:, head * HEAD : (head + 1) * HEAD]
                if third < 2:
                    lead = mine[:, :128]
                    lead = (
                        lead * tables_out[0, here, :]
                        - pltpu.roll(lead, 96, 1) * tables_out[1, here, :]
                        + pltpu.roll(lead, 32, 1) * tables_out[2, here, :]
                    )
                    mine = jnp.concatenate([lead, mine[:, 128:]], 1)
                heads[third, here, head * HEAD : (head + 1) * HEAD] = mine.astype(jnp.bfloat16)
            return carry

        lax.fori_loop(0, tokens // TALL, some_rows, 0)

    def attend(head):
        lanes = slice(head * HEAD, (head + 1) * HEAD)
        for i in range(tokens // TILE):
            here, keys = slice(i * TILE, (i + 1) * TILE), slice(0, (i + 1) * TILE)
            probs = causal_probs(heads[0, here, lanes], heads[1, keys, lanes], first_out[here, :], i * TILE)
            mixed[here, lanes] = dot(probs.astype(jnp.bfloat16), heads[2, keys, lanes]).astype(jnp.bfloat16)

    def down_load(j):
        return load(4 + j % 2, down_ref.at[:, pl.ds(j * cols, cols)], down.at[j % 2])

    def branch_keep(j):
        return keep(6 + j, branch.at[j % 2], branch_out.at[:, pl.ds(j * cols, cols)])

    def branch_cols(j):
        down_load(j).wait()
        if j >= 2:
            branch_keep(j - 2).wait()

        def some_rows(i, carry):
            here = pl.ds(pl.multiple_of(i * TALL, TALL), TALL)
            found = dot(act[here, :], down[j % 2]) + dot(mixed[here, :], proj[:, j * cols : (j + 1) * cols])
            branch[j % 2, here, :] = found.astype(jnp.bfloat16)
            return carry

        lax.fori_loop(0, tokens // TALL, some_rows, 0)
        branch_keep(j).start()
        if j + 2 < width // cols:
            down_load(j + 2).start()

    greet(rep, place, replicas, shards_n)
    for step in range(1, shards_n):
        small_copy(step, True).start()
    for item in range(shards_n - 1):
        for path in range(2):
            for copy in turned(item, path, True):
                copy.start()
    send_hop(0)
    own = [
        (small_ref, small_out.at[place]),
        (
            up_ref.at[:, pl.ds(pl.multiple_of(place * hidden, 128), hidden)],
            up_out.at[pl.ds(pl.multiple_of(place * part, part), part), :],
        ),
        (x_ref, x_out.at[block_rows(place), :]),
        (g_ref, g_out.at[block_rows(place), :]),
    ] + [
        (
            qkv_ref.at[:, pl.ds(pl.multiple_of(third * width + place * wide, 128), wide)],
            qkv_out.at[third, pl.ds(pl.multiple_of(place * part, part), part), :],
        )
        for third in range(3)
    ]
    own = [pltpu.make_async_copy(src, dst, own_sem.at[i]) for i, (src, dst) in enumerate(own)]
    for copy in own:
        copy.start()
    down_load(0).start()
    down_load(1).start()
    load_proj = load(6, proj_ref, proj)
    load_proj.start()

    lax.fori_loop(0, 2 * shards_n, tables, 0)
    for step in range(1, shards_n):
        small_copy(step, False).wait()
    own[0].wait()
    load_small = load(0, small_out, small_low)
    load_small.start()
    load_small.wait()
    small[...] = small_low[...].astype(jnp.float32)
    on_step(0, lambda block, way: norm(block, x_ref, way))

    load_up = load(2, up_out, up)
    load_qkv = load(3, qkv_out, qkv)
    ticks = list(range(len(items) + bits))

    def some_ticks(number):
        for tick in ticks[:number]:
            column_tick(tick)
        del ticks[:number]

    def send_upstream(to_ends):
        for other in range(1, shards_n):
            to = lax.rem(place + other, shards_n)
            at_end = (to == 0) | (to == shards_n - 1)

            @pl.when(at_end if to_ends else jnp.logical_not(at_end))
            def _():
                upstream_copy(other, True).start()

    def arrive(step):
        pass_on(step)
        if step == 1:
            for item in range(shards_n - 1, len(items)):
                for path in range(2):
                    for copy in turned(item, path, True):
                        copy.start()
        if step == shards_n - 2:
            send_upstream(False)
        on_step(step, lambda block, way: norm(block, x_out.at[block_rows(block), :], way))

    some_ticks(3)
    arrive(1)
    some_ticks(shards_n - 1 + bits - 3)
    own[1].wait()
    load_up.start()
    load_up.wait()
    on_step(0, lambda block, way: hidden_units(block))
    for step in range(2, shards_n - 1):
        arrive(step)
    some_ticks(1)
    on_step(1, lambda block, way: hidden_units(block))
    some_ticks(1)
    for way in range(2):

        @pl.when(goes(way, shards_n - 2))
        def _():
            hop(way, shards_n - 2, True).wait_send()

    send_upstream(True)
    some_ticks(len(ticks))
    arrive(shards_n - 1)
    keeps = [keep(0, mlp, mlp_out), keep(1, attn, attn_out)]
    keeps[0].start()
    keeps[1].start()
    for copy in own[4:]:
        copy.wait()
    load_qkv.start()
    for step in range(2, shards_n):
        on_step(step, lambda block, way: hidden_units(block))
    keeps += [keep(2, act, act_out), keep(3, slope, slope_out)]
    keeps[2].start()
    keeps[3].start()
    load_qkv.wait()
    for third in range(3):
        project(third)
    keeps.append(keep(4, heads, heads_out))
    keeps[4].start()
    for head in range(wide // HEAD):
        attend(head)
    keeps.append(keep(5, mixed, mixed_out))
    keeps[5].start()
    load_proj.wait()
    for j in range(width // cols):
        branch_cols(j)
    for step in range(1, shards_n):
        upstream_copy(step, False).wait()
    for j in range(max(width // cols - 2, 0), width // cols):
        branch_keep(j).wait()
    for copy in keeps:
        copy.wait()
    for item in range(len(items)):
        for path in range(2):
            for copy in turned(item, path, True):
                copy.wait_send()
            for level in range(bits):
                spread(item, path, level).wait_send()
    for step in range(shards_n - 2):
        for way in range(2):

            @pl.when(goes(way, step))
            def _():
                hop(way, step, True).wait_send()

    for copy in own[2:4]:
        copy.wait()


def forward(small, up_weight, qkv_weight, x, g, down_weight, proj_weight, bias, frequency, lengths):
    replicas, count = lax.axis_size("replica"), lax.axis_size("shard")
    bits = replicas.bit_length() - 1
    local, width = x.shape
    tokens = local * count
    hidden, wide = up_weight.shape[1] // count, width // count
    cols = wide
    items = 2 * (count - 1)
    any_spec = pl.BlockSpec(memory_space=pl.ANY)
    vmem_spec = pl.BlockSpec(memory_space=pltpu.VMEM)
    shapes = dict(
        small=(count,) + small.shape,
        up_cols=(width, hidden),
        qkv_cols=(3, width, wide),
        x=(tokens, width),
        g=(tokens, width),
        mlp_in=(tokens, width),
        attn_in=(tokens, width),
        act=(tokens, hidden),
        slope=(tokens, hidden),
        heads=(3, tokens, wide),
        mixed=(tokens, wide),
        branch=(tokens, width),
    )
    low = lambda *shape: pltpu.VMEM(shape, jnp.bfloat16)
    dma = lambda *shape: pltpu.SemaphoreType.DMA(shape)
    found = pl.pallas_call(
        partial(forward_kernel, replicas, count),
        out_shape=tuple(jax.ShapeDtypeStruct(shape, jnp.bfloat16) for shape in shapes.values())
        + (
            jax.ShapeDtypeStruct((2, tokens, 1), jnp.float32),
            jax.ShapeDtypeStruct((3, tokens, 128), jnp.float32),
            jax.ShapeDtypeStruct((tokens, 1), jnp.int32),
        ),
        in_specs=[any_spec] * 7 + [vmem_spec] * 2 + [pl.BlockSpec(memory_space=pltpu.SMEM)],
        out_specs=(any_spec,) * len(shapes) + (vmem_spec,) * 3,
        scratch_shapes=[
            low(*shapes["small"]),
            pltpu.VMEM(shapes["small"], jnp.float32),
            low(2, local, width),
            low(tokens, width),
            low(tokens, width),
            low(width, hidden),
            low(3, width, wide),
            low(tokens, hidden),
            low(tokens, hidden),
            low(3, tokens, wide),
            low(tokens, wide),
            low(2, hidden, cols),
            low(wide, width),
            low(2, tokens, cols),
            dma(7),
            dma(7),
            dma(6 + width // cols),
            dma(2, count),
            dma(2, items, 2, 3),
            dma(2, items, 2, bits),
            dma(2, 2, count - 1),
            dma(2, count),
        ],
        compiler_params=pltpu.CompilerParams(
            collective_id=0, has_side_effects=True, vmem_limit_bytes=58 * 2**20
        ),
        cost_estimate=pl.CostEstimate(
            flops=2 * tokens * width * (hidden * 2 + wide * 4),
            bytes_accessed=500_000_000,
            transcendentals=0,
        ),
    )(small, up_weight, qkv_weight, x, g, down_weight, proj_weight, bias, frequency, lengths)
    return dict(zip(list(shapes) + ["stats", "tables", "first"], found))


RING = 3


def grads_kernel(
    replicas,
    shards_n,
    act_ref,
    up_ref,
    mixed_ref,
    mlp_ref,
    attn_ref,
    slope_ref,
    down_ref,
    proj_ref,
    heads_ref,
    rows_ref,
    cols_up_ref,
    cols_qkv_ref,
    tables_ref,
    first_ref,
    stats_ref,
    small_ref,
    out_ref,
    vec_out,
    sum_out,
    work,
    from_core,
    *rest,
):
    rep, place = lax.axis_index("replica"), lax.axis_index("shard")
    bits = replicas.bit_length() - 1
    far = bits - 1
    from_far = rest[:far]
    (
        big,
        narrow,
        pre,
        joined,
        wide_rows,
        slope,
        heads,
        key_sum,
        value_sum,
        tile_x,
        tile_up,
        tile_qkv,
        shared,
        vec_got,
        vec_sum,
        load_sem,
        core_sem,
        far_sem,
        turn_sem,
        own_sem,
        plane_sem,
        vec_sem,
        sum_sem,
    ) = rest[far:]
    chunks, _, rows, cols = out_ref.shape
    slots = work.shape[0]
    half, side = rows // 2, cols // 2
    piece = rows // replicas
    orders = plane_orders(replicas)
    core = bit_of(rep, 0)
    tokens, width = up_ref.shape
    local = tokens // shards_n
    hiddens = pre.shape[1] // cols
    natives = hiddens + 1
    mine = pl.multiple_of(core * half, half)
    theirs = pl.multiple_of((1 - core) * half, half)

    starts = []
    for order in orders:
        line, size = [core * half], half
        for bit in order:
            size //= 2
            line.append(line[-1] + bit_of(rep, bit) * size)
        starts.append(line)

    def spot(k):
        if k < natives:
            return k + hiddens
        return k - natives if k < natives + hiddens else k

    def load(source, target, number):
        return pltpu.make_async_copy(source, target, load_sem.at[number])

    def narrow_load(k):
        source = act_ref.at[:, pl.ds(k * cols, cols)] if k < hiddens else mixed_ref
        return load(source, narrow.at[k % 2], k % 2)

    def big_load(which):
        return load((up_ref, mlp_ref, attn_ref)[which], big.at[which % 2], 2 + which)

    def down_load(k):
        return load(down_ref.at[pl.ds(k * cols, cols), :], wide_rows.at[k % 2], 5 + k % 2)

    def slope_load(k):
        return load(slope_ref.at[:, pl.ds(k * cols, cols)], slope.at[k % 2], 7 + k % 2)

    def pre_loads(k):
        return [down_load(k), slope_load(k)]

    def proj_load():
        return load(proj_ref, wide_rows.at[1], 6)

    def heads_load():
        return load(heads_ref, heads.at[pl.ds(0, 3)], 9)

    def tile_loads(j):
        some = pl.ds(j * TILE, TILE)
        return [
            load(rows_ref.at[:, some], tile_x.at[j % 2], 10 + j % 2),
            load(cols_up_ref.at[some, :], tile_up.at[j % 2], 12 + j % 2),
        ] + [
            load(
                cols_qkv_ref.at[third, some, :],
                tile_qkv.at[j % 2, :, pl.ds(third * cols, cols)],
                14 + 2 * third + j % 2,
            )
            for third in range(3)
        ]

    def to_core(k):
        return remote(
            work.at[k % slots, :, pl.ds(theirs, half), :],
            from_core.at[k % RING],
            core_sem,
            (0, k),
            {"replica": flip(rep, 0)},
        )

    def to_far(k, level, path):
        size = half >> (level + 1)
        bit = orders[path][level]
        start = starts[path][level] + (1 - bit_of(rep, bit)) * size
        return remote(
            work.at[k % slots, :, pl.ds(pl.multiple_of(start, size), size), pl.ds(path * side, side)],
            from_far[level].at[k % RING, path],
            far_sem,
            (k, level, path),
            {"replica": flip(rep, bit)},
        )

    def own_piece(k, path, block):
        return work.at[
            k % slots,
            block,
            pl.ds(pl.multiple_of(starts[path][far], piece), piece),
            pl.ds(path * side, side),
        ]

    def place_piece(k, path, block):
        return out_ref.at[
            spot(k),
            block,
            pl.ds(pl.multiple_of(starts[path][far], piece), piece),
            pl.ds(path * side, side),
        ]

    def settle(k, path):
        block = pl.ds(0, shards_n) if k < natives else place
        return pltpu.make_async_copy(
            own_piece(k, path, block), place_piece(k, path, block), own_sem.at[k % 2, path]
        )

    def turned(k, path, step, sending):
        to = lax.rem(place + step, shards_n)
        shard = place if sending else lax.rem(place - step + shards_n, shards_n)
        return remote(
            own_piece(k, path, to),
            place_piece(k, path, shard),
            turn_sem,
            (k - natives, path, step - 1),
            {"shard": to},
        )

    def spread(k, path, level):
        size = piece << level
        bit = orders[path][far - 1 - level]
        here = out_ref.at[
            spot(k),
            :,
            pl.ds(pl.multiple_of(starts[path][far - level], size), size),
            pl.ds(path * side, side),
        ]
        return remote(here, here, plane_sem, (k, level, path), {"replica": flip(rep, bit)})

    def spread_core(k):
        here = out_ref.at[spot(k), :, pl.ds(mine, half), :]
        return remote(here, here, core_sem, (1, k), {"replica": flip(rep, 0)})

    def put(offset, sums):
        for i in range(sums.shape[1] // 128):
            vec_sum[pl.ds(offset // 128 + i, 1), :] = sums[:, i * 128 : (i + 1) * 128]

    def compute(k):
        if k < natives:
            narrow_load(k).wait()
            if k + 1 < natives:
                narrow_load(k + 1).start()
        if k == 0:
            big_load(0).wait()
        if k == natives:
            big_load(1).wait()
        if k == natives + hiddens:
            big_load(2).wait()
        slot = k % slots
        which = 1 if natives <= k < natives + hiddens else 0

        def block(g, carry):
            if k < natives:
                left = narrow[k % 2]
                right = big[which, :, pl.ds(pl.multiple_of(g * cols, cols), cols)]
            else:
                left = big[which, :, pl.ds(pl.multiple_of(g * rows, rows), rows)]
                if k < natives + hiddens:
                    right = pre[:, (k - natives) * cols : (k - natives + 1) * cols]
                else:
                    third = k - natives - hiddens
                    right = joined[:, third * cols : (third + 1) * cols]
            work[slot, g] = dot_rows(left, right).astype(jnp.bfloat16)
            return carry

        lax.fori_loop(0, shards_n, block, 0)
        to_core(k).start()

    def add(k, start, size, left, width, got):
        def block(g, carry):
            where = (k % slots, g, pl.ds(pl.multiple_of(start, size), size), pl.ds(left, width))
            work[where] = (
                work[where].astype(jnp.float32) + got(g).astype(jnp.float32)
            ).astype(jnp.bfloat16)
            return carry

        lax.fori_loop(0, shards_n, block, 0)

    def grad_mixed():
        proj_load().wait()

        def block(i, carry):
            some = pl.ds(pl.multiple_of(i * TALL, TALL), TALL)
            heads[3, some, :] = dot_cols(big[0, some, :], wide_rows[1]).astype(jnp.bfloat16)
            return carry

        lax.fori_loop(0, tokens // TALL, block, 0)
        down_load(1).start()
        own = pl.ds(pl.multiple_of(place * cols, cols), cols)
        put(4 * width + place * cols, jnp.sum(big[0, :, own].astype(jnp.float32), 0, keepdims=True))

    def grad_pre(k):
        for copy in pre_loads(k):
            copy.wait()

        def block(i, total):
            some = pl.ds(pl.multiple_of(i * TALL, TALL), TALL)
            found = dot_cols(big[0, some, :], wide_rows[k % 2]) * slope[k % 2, some, :].astype(
                jnp.float32
            )
            low = found.astype(jnp.bfloat16)
            pre[some, k * cols : (k + 1) * cols] = low
            return total + jnp.sum(low.astype(jnp.float32), 0, keepdims=True)

        total = lax.fori_loop(0, tokens // TALL, block, jnp.zeros((1, cols), jnp.float32))
        put(8 * width + (place * hiddens + k) * cols, total)
        if k + 2 < hiddens:
            for copy in pre_loads(k + 2):
                copy.start()

    def turn_rows(found, some):
        lead = found[:, :128]
        lead = (
            lead * tables_ref[0, some, :]
            + pltpu.roll(lead, 96, 1) * tables_ref[1, some, :]
            - pltpu.roll(lead, 32, 1) * tables_ref[2, some, :]
        )
        return jnp.concatenate([lead, found[:, 128:]], 1)

    def attention(head):
        lanes = pl.ds(head * HEAD, HEAD)
        scale = 1.0 / math.sqrt(HEAD)
        key_sum[...] = jnp.zeros_like(key_sum)
        value_sum[...] = jnp.zeros_like(value_sum)
        sums = [jnp.zeros((1, HEAD), jnp.float32)] * 3
        for i in range(tokens // TILE):
            some, keys = pl.ds(i * TILE, TILE), pl.ds(0, (i + 1) * TILE)
            query = heads[0, some, lanes]
            key = heads[1, keys, lanes]
            probs = causal_probs(query, key, first_ref[some, :], i * TILE)
            grad = heads[3, some, lanes]
            grad_probs = dot_cols(grad, heads[2, keys, lanes])
            delta = jnp.sum(probs * grad_probs, -1, keepdims=True)
            low = (probs * (grad_probs - delta)).astype(jnp.bfloat16)
            found = turn_rows(dot(low, key) * scale, some).astype(jnp.bfloat16)
            joined[some, pl.ds(head * HEAD, HEAD)] = found
            sums[0] = sums[0] + jnp.sum(found.astype(jnp.float32), 0, keepdims=True)
            key_sum[keys, :] = key_sum[keys, :] + dot_rows(low, query)
            value_sum[keys, :] = value_sum[keys, :] + dot_rows(probs.astype(jnp.bfloat16), grad)
        for i in range(tokens // TILE):
            some = pl.ds(i * TILE, TILE)
            for third, found in (
                (1, turn_rows(key_sum[some, :] * scale, some)),
                (2, value_sum[some, :]),
            ):
                low = found.astype(jnp.bfloat16)
                joined[some, pl.ds(third * cols + head * HEAD, HEAD)] = low
                sums[third] = sums[third] + jnp.sum(low.astype(jnp.float32), 0, keepdims=True)
        for third in range(3):
            put(5 * width + third * width + place * cols + head * HEAD, sums[third])

    def sum_part(j, step, sending):
        to = lax.rem(place + step, shards_n)
        shard = place if sending else lax.rem(place - step + shards_n, shards_n)
        some = pl.ds(j * TILE, TILE)
        source = shared.at[pl.ds(pl.multiple_of(to * local, local), local), some]
        if step == 0:
            return pltpu.make_async_copy(source, sum_out.at[place, :, some], sum_sem.at[0, j, 0])
        return remote(source, sum_out.at[shard, :, some], sum_sem, (j, step), {"shard": to})

    def tile(j):
        for copy in tile_loads(j):
            copy.wait()
        if j + 1 < width // TILE:
            for copy in tile_loads(j + 1):
                copy.start()
        lanes = pl.ds(j * TILE, TILE)
        owner, begin = divmod(j * TILE, cols)
        theirs_at = slice(begin, begin + TILE)

        def block(i, totals):
            some = pl.ds(pl.multiple_of(i * TALL, TALL), TALL)
            normed = (tile_x[j % 2, some, :].astype(jnp.float32) - stats_ref[0, some, :]) * stats_ref[
                1, some, :
            ]
            mlp = dot_cols(pre[some, :], tile_up[j % 2])
            attn = dot_cols(joined[some, :], tile_qkv[j % 2])
            shared[some, lanes] = (
                attn * small_ref[owner, 0:1, theirs_at].astype(jnp.float32)
                + mlp * small_ref[owner, 3:4, theirs_at].astype(jnp.float32)
            ).astype(jnp.bfloat16)
            found = (attn * normed, attn, mlp * normed, mlp)
            return tuple(t + jnp.sum(f, 0, keepdims=True) for t, f in zip(totals, found))

        zero = jnp.zeros((1, TILE), jnp.float32)
        totals = lax.fori_loop(0, tokens // TALL, block, (zero,) * 4)
        for number, total in enumerate(totals):
            put(number * width + j * TILE, total)
        for step in range(shards_n):
            sum_part(j, step, True).start()

    def stage(k, number):
        if number == 0:
            compute(k)
        elif number == 1:
            to_core(k).wait()
            add(k, mine, half, 0, cols, lambda g: from_core[k % RING, g])
            for path in range(2):
                to_far(k, 0, path).start()
        elif number <= 1 + far:
            level = number - 2
            for path in range(2):
                to_far(k, level, path).wait()
                size = half >> (level + 1)
                add(
                    k,
                    starts[path][level + 1],
                    size,
                    path * side,
                    side,
                    lambda g: from_far[level][k % RING, path, g],
                )
                if level + 1 < far:
                    to_far(k, level + 1, path).start()
                else:
                    if k >= natives:
                        for step in range(1, shards_n):
                            turned(k, path, step, True).start()
                    settle(k, path).start()
        elif number == 2 + far:
            for path in range(2):
                settle(k, path).wait()
                if k >= natives:
                    for step in range(1, shards_n):
                        turned(k, path, step, False).wait_recv()
                spread(k, path, 0).start()
            if k >= natives:
                for path in range(2):
                    for step in range(1, shards_n):
                        turned(k, path, step, True).wait_send()
        elif number <= 2 + 2 * far:
            level = number - 3 - far
            for path in range(2):
                spread(k, path, level).wait()
                if level + 1 < far:
                    spread(k, path, level + 1).start()
            if level + 1 == far:
                spread_core(k).start()
        else:
            spread_core(k).wait()

    stages = 4 + 2 * far
    n_heads, n_tiles = cols // HEAD, width // TILE
    extras = {0: [grad_mixed, partial(grad_pre, 0)]}
    for k in range(1, hiddens):
        extras.setdefault(k, []).append(partial(grad_pre, k))
    for head in range(n_heads):
        extras.setdefault(1 + head, []).append(partial(attention, head))
    extras[hiddens] = [big_load(2).start]
    tile_at = hiddens + 1
    for j in range(n_tiles):
        extras.setdefault(tile_at + j, []).append(partial(tile, j))
    vec_at = max(extras) + 1

    for copy in [narrow_load(0), big_load(0), proj_load()] + pre_loads(0):
        copy.start()
    slope_load(1).start()
    for copy in [heads_load(), big_load(1)] + tile_loads(0):
        copy.start()
    vec_sum[...] = jnp.zeros_like(vec_sum)
    greet(rep, place, replicas, shards_n)
    peers = [{"replica": flip(rep, bit)} for bit in range(bits)]
    peers += [{"shard": flip(place, bit)} for bit in range(shards_n.bit_length() - 1)]

    def vec_copy(number):
        return remote(vec_sum, vec_got.at[number], vec_sem, (number,), peers[number])

    for tick in range(max(chunks + stages - 1, vec_at + len(peers) + 1)):
        for number in reversed(range(stages)):
            if 0 <= tick - number < chunks:
                stage(tick - number, number)
        if tick == 0:
            heads_load().wait()
        for extra in extras.get(tick, []):
            extra()
        turn_of = tick - vec_at
        if 0 < turn_of <= len(peers):
            vec_copy(turn_of - 1).wait()
            vec_sum[...] = vec_sum[...] + vec_got[turn_of - 1]
        if 0 <= turn_of < len(peers):
            vec_copy(turn_of).start()
    vec_out[...] = vec_sum[...]
    for j in range(n_tiles):
        for step in range(shards_n):
            sum_part(j, step, False).wait()


def summed_grads(*operands):
    act, up, mixed, mlp_in = operands[:4]
    replicas, count = lax.axis_size("replica"), lax.axis_size("shard")
    bits = replicas.bit_length() - 1
    far = bits - 1
    tokens, width = up.shape
    cols = width // count
    hidden = act.shape[1]
    hiddens = hidden // cols
    natives = hiddens + 1
    chunks = natives + hiddens + 3
    peers = bits + count.bit_length() - 1
    slots = 2 + far
    vector = ((8 * width + count * hidden) // 128, 128)
    any_spec = pl.BlockSpec(memory_space=pl.ANY)
    vmem_spec = pl.BlockSpec(memory_space=pltpu.VMEM)
    low = lambda *shape: pltpu.VMEM(shape, jnp.bfloat16)
    full = lambda *shape: pltpu.VMEM(shape, jnp.float32)
    dma = lambda *shape: pltpu.SemaphoreType.DMA(shape)
    return pl.pallas_call(
        partial(grads_kernel, replicas, count),
        out_shape=(
            jax.ShapeDtypeStruct((chunks, count, cols, cols), jnp.bfloat16),
            jax.ShapeDtypeStruct(vector, jnp.float32),
            jax.ShapeDtypeStruct((count, tokens // count, width), jnp.bfloat16),
        ),
        in_specs=[any_spec] * 12 + [vmem_spec] * 4,
        out_specs=(any_spec, vmem_spec, any_spec),
        scratch_shapes=[
            low(slots, count, cols, cols),
            low(RING, count, cols // 2, cols),
        ]
        + [low(RING, 2, count, cols >> (level + 2), cols // 2) for level in range(far)]
        + [
            low(2, tokens, width),
            low(2, tokens, cols),
            low(tokens, hidden),
            low(tokens, 3 * cols),
            low(2, cols, width),
            low(2, tokens, cols),
            low(4, tokens, cols),
            full(tokens, HEAD),
            full(tokens, HEAD),
            low(2, tokens, TILE),
            low(2, TILE, hidden),
            low(2, TILE, 3 * cols),
            low(tokens, width),
            full(peers, *vector),
            full(*vector),
            dma(20),
            dma(2, 2, chunks),
            dma(2, chunks, far, 2),
            dma(2, chunks - natives, 2, count - 1),
            dma(2, 2),
            dma(2, chunks, far, 2),
            dma(2, peers),
            dma(2, width // TILE, count),
        ],
        compiler_params=pltpu.CompilerParams(
            collective_id=1, has_side_effects=True, vmem_limit_bytes=60 * 2**20
        ),
        cost_estimate=pl.CostEstimate(
            flops=4 * tokens * chunks * count * cols * cols,
            bytes_accessed=600_000_000,
            transcendentals=0,
        ),
    )(*operands)


def last_kernel(
    up_blocks,
    down_blocks,
    out_blocks,
    qkv_blocks,
    parts_ref,
    branch_ref,
    x_ref,
    g_ref,
    small_ref,
    vec_ref,
    layer_out,
    input_out,
    up_out,
    down_out,
    out_out,
    qkv_out,
    *thin_outs,
):
    number, count, _, cols = up_blocks.shape
    for g in range(count):
        lanes = slice(g * cols, (g + 1) * cols)
        for k in range(number):
            at = (g * number + k) * cols
            up_out[:, at : at + cols] = up_blocks[k, g].astype(jnp.float32)
        for k in range(3):
            at = (k * count + g) * cols
            qkv_out[:, at : at + cols] = qkv_blocks[k, g].astype(jnp.float32)
        down_out[:, lanes] = down_blocks[0, g].astype(jnp.float32)
        out_out[:, lanes] = out_blocks[0, g].astype(jnp.float32)
    rows = x_ref[...].astype(jnp.float32)
    normed, inverse_std = normalize(rows)
    grad = sum(parts_ref[g].astype(jnp.float32) for g in range(count))
    input_out[...] = g_ref[...].astype(jnp.float32) + norm_backward(grad, normed, inverse_std)
    for g in range(count):
        lanes = slice(g * cols, (g + 1) * cols)
        bias = small_ref[g, 2:3, :].astype(jnp.float32) + small_ref[g, 5:6, :].astype(jnp.float32)
        layer_out[:, lanes] = (
            rows[:, lanes] + branch_ref[:, lanes].astype(jnp.float32) + bias
        ).astype(jnp.bfloat16)

    @pl.when(pl.program_id(0) == 0)
    def _():
        place = lax.axis_index("shard")
        width = count * cols
        for thin, start in zip(thin_outs, (0, 1, 4, 4, 2, 3, 5, 8)):
            length = thin.shape[0]
            first = (start * width + place * length) // 128
            for i in range(length // 128):
                thin[i * 128 : (i + 1) * 128] = vec_ref[first + i, :]


def last(blocks, parts, branch, x, g, small, vector):
    count, rows, cols = blocks.shape[1:]
    number = (blocks.shape[0] - 4) // 2
    local, width = x.shape
    steps = local // 16
    some, tall = rows // steps, number * rows // steps
    turns = rows // tall
    whole = lambda i: (i, 0)
    thin = [rows] * 6 + [3 * rows, number * rows]
    return pl.pallas_call(
        last_kernel,
        out_shape=(
            jax.ShapeDtypeStruct((local, width), jnp.bfloat16),
            jax.ShapeDtypeStruct((local, width), jnp.float32),
            jax.ShapeDtypeStruct((rows, number * width), jnp.float32),
            jax.ShapeDtypeStruct((number * rows, width), jnp.float32),
            jax.ShapeDtypeStruct((rows, width), jnp.float32),
            jax.ShapeDtypeStruct((rows, 3 * width), jnp.float32),
        )
        + tuple(jax.ShapeDtypeStruct((length,), jnp.float32) for length in thin),
        grid=(steps,),
        in_specs=[
            pl.BlockSpec((number, count, some, cols), lambda i: (0, 0, i, 0)),
            pl.BlockSpec((1, count, tall, cols), lambda i: (number + i // turns, 0, i % turns, 0)),
            pl.BlockSpec((1, count, some, cols), lambda i: (2 * number, 0, i, 0)),
            pl.BlockSpec((3, count, some, cols), lambda i: ((2 * number + 1) // 3, 0, i, 0)),
            pl.BlockSpec((count, 16, width), lambda i: (0, i, 0)),
            pl.BlockSpec((16, width), whole),
            pl.BlockSpec((16, width), whole),
            pl.BlockSpec((16, width), whole),
            pl.BlockSpec(small.shape, lambda i: (0, 0, 0)),
            pl.BlockSpec(vector.shape, lambda i: (0, 0)),
        ],
        out_specs=(
            pl.BlockSpec((16, width), whole),
            pl.BlockSpec((16, width), whole),
            pl.BlockSpec((some, number * width), whole),
            pl.BlockSpec((tall, width), whole),
            pl.BlockSpec((some, width), whole),
            pl.BlockSpec((some, 3 * width), whole),
        )
        + tuple(pl.BlockSpec((length,), lambda i: (0,)) for length in thin),
        compiler_params=pltpu.CompilerParams(vmem_limit_bytes=62 * 2**20),
    )(blocks, blocks, blocks, blocks, parts, branch, x, g, small, vector)


def shards(
    layer_input,
    attn_gain,
    attn_shift,
    qkv_weight,
    qkv_bias,
    out_weight,
    out_bias,
    mlp_gain,
    mlp_shift,
    up_weight,
    up_bias,
    down_weight,
    down_bias,
    seq_lengths,
    upstream,
):
    local_rows = layer_input.shape[0]
    count = lax.axis_size("shard")
    group_rows = local_rows * count
    place = lax.axis_index("shard")
    part = D // count
    hidden = up_bias.shape[0]

    params = [attn_gain, attn_shift, out_bias, mlp_gain, mlp_shift, down_bias]
    params += [qkv_bias[i * part : (i + 1) * part] for i in range(3)]
    row = lax.broadcasted_iota(jnp.int32, (16, part), 0)
    small = jnp.zeros((16, part), jnp.bfloat16)
    for i, param in enumerate(params):
        small = jnp.where(row == i, param[None], small)

    frequency = np.power(np.float32(ROPE_BASE), -np.arange(ROT // 2, dtype=np.float32) * np.float32(2.0 / ROT))
    known = forward(
        small,
        up_weight,
        qkv_weight,
        layer_input,
        upstream,
        down_weight,
        out_weight,
        up_bias.astype(jnp.float32)[None],
        jnp.asarray(np.tile(frequency, 128 // (ROT // 2))[None]),
        seq_lengths,
    )
    branch_own = lax.psum_scatter(known["branch"], "shard", scatter_dimension=0, tiled=True)
    grads, vector, normed_parts = summed_grads(
        known["act"],
        known["g"],
        known["mixed"],
        known["mlp_in"],
        known["attn_in"],
        known["slope"],
        down_weight,
        out_weight,
        known["heads"],
        known["x"],
        known["up_cols"],
        known["qkv_cols"],
        known["tables"],
        known["first"],
        known["stats"],
        known["small"],
    )
    grads, branch_own = lax.optimization_barrier((grads, branch_own))
    layer_output, input_grad, up_grad, down_grad, out_grad, qkv_grad, *thin = last(
        grads, normed_parts, branch_own, layer_input, upstream, known["small"], vector
    )
    return (
        layer_output,
        input_grad,
        thin[0],
        thin[1],
        qkv_grad,
        thin[6],
        out_grad,
        thin[2],
        thin[4],
        thin[5],
        up_grad,
        thin[7],
        down_grad,
        thin[3],
    )


def solution(mesh):
    in_specs = (
        P(("replica", "shard"), None),
        P("shard"),
        P("shard"),
        P("shard", None),
        P("shard"),
        P("shard", None),
        P("shard"),
        P("shard"),
        P("shard"),
        P("shard", None),
        P("shard"),
        P("shard", None),
        P("shard"),
        P("replica", None),
        P(("replica", "shard"), None),
    )
    out_specs = (
        P(("replica", "shard"), None),
        P(("replica", "shard"), None),
        P("shard"),
        P("shard"),
        P("shard", None),
        P("shard"),
        P("shard", None),
        P("shard"),
        P("shard"),
        P("shard"),
        P("shard", None),
        P("shard"),
        P("shard", None),
        P("shard"),
    )
    return jax.shard_map(shards, mesh=mesh, in_specs=in_specs, out_specs=out_specs, check_vma=False)
```

```python
from functools import partial
import math

import jax
import jax.numpy as jnp
import numpy as np
from jax import lax
from jax.experimental import pallas as pl
from jax.experimental.pallas import tpu as pltpu
from jax.sharding import PartitionSpec as P

D = 2048
HEADS = 8
HEAD = 256
ROT = 64


EPSILON = 1e-05
ROPE_BASE = 10000.0
NEG_LARGE = -1e30
MESH = pl.DeviceIdType.MESH
CONTRACT_ROWS = (((0,), (0,)), ((), ()))
CONTRACT_COLS = (((1,), (1,)), ((), ()))


def normalize(layer_rows):
    centered = layer_rows - jnp.mean(layer_rows, -1, keepdims=True)
    variance = jnp.mean(centered * centered, -1, keepdims=True)
    inverse_std = lax.rsqrt(variance + EPSILON)
    return (centered * inverse_std, inverse_std)


def norm_backward(grad_normed, normed, inverse_std):
    mean_grad = jnp.mean(grad_normed, -1, keepdims=True)
    mean_cross = jnp.mean(grad_normed * normed, -1, keepdims=True)
    return (grad_normed - mean_grad - normed * mean_cross) * inverse_std


def dot(left, right):
    return jnp.dot(left, right, preferred_element_type=jnp.float32)


def dot_rows(left, right):
    return lax.dot_general(left, right, CONTRACT_ROWS, preferred_element_type=jnp.float32)


def dot_cols(left, right):
    return lax.dot_general(left, right, CONTRACT_COLS, preferred_element_type=jnp.float32)


def bit_of(index, bit):
    return lax.rem(lax.div(index, 1 << bit), 2)


def flip(index, bit):
    return index + (1 << bit) * (1 - 2 * bit_of(index, bit))


def plane_orders(replicas):
    far = list(range(1, replicas.bit_length() - 1))
    return far, far[1:] + far[:1]


def remote(src, dst, sems, at, device):
    return pltpu.make_async_remote_copy(
        src_ref=src,
        dst_ref=dst,
        send_sem=sems.at[(0,) + at],
        recv_sem=sems.at[(1,) + at],
        device_id=device,
        device_id_type=MESH,
    )


def greet(rep, place, replicas, shards_n):
    barrier = pltpu.get_barrier_semaphore()
    bits = replicas.bit_length() - 1
    for bit in range(bits):
        pl.semaphore_signal(
            barrier, inc=1, device_id={"replica": flip(rep, bit)}, device_id_type=MESH
        )
    for step in range(1, shards_n):
        pl.semaphore_signal(
            barrier,
            inc=1,
            device_id={"shard": lax.rem(place + step, shards_n)},
            device_id_type=MESH,
        )
    pl.semaphore_wait(barrier, bits + shards_n - 1)


TILE = 256
TALL = 512


def causal_probs(query, key, first, row):
    shape = (query.shape[0], key.shape[0])
    scores = dot_cols(query, key) * (1.0 / math.sqrt(HEAD))
    at = lax.broadcasted_iota(jnp.int32, shape, 1)
    upto = lax.broadcasted_iota(jnp.int32, shape, 0) + row
    scores = jnp.where((at >= first) & (at <= upto), scores, NEG_LARGE)
    shifted = jnp.exp(scores - jnp.max(scores, -1, keepdims=True))
    return shifted / jnp.sum(shifted, -1, keepdims=True)


def forward_kernel(
    replicas,
    shards_n,
    small_ref,
    up_ref,
    qkv_ref,
    x_ref,
    g_ref,
    down_ref,
    proj_ref,
    bias_ref,
    frequency_ref,
    lengths_ref,
    small_out,
    up_out,
    qkv_out,
    x_out,
    g_out,
    mlp_out,
    attn_out,
    act_out,
    slope_out,
    heads_out,
    mixed_out,
    branch_out,
    stats_out,
    tables_out,
    first_out,
    small_low,
    small,
    x_rows,
    mlp,
    attn,
    up,
    qkv,
    act,
    slope,
    heads,
    mixed,
    down,
    proj,
    branch,
    own_sem,
    load_sem,
    keep_sem,
    small_sem,
    turn_sem,
    plane_sem,
    hop_sem,
    g_sem,
):
    rep, place = lax.axis_index("replica"), lax.axis_index("shard")
    bits = replicas.bit_length() - 1
    width, hidden = up_out.shape
    part = width // shards_n
    wide = qkv_out.shape[2]
    rows = part // replicas
    tokens = x_out.shape[0]
    local = tokens // shards_n
    cols = down.shape[2]
    orders = [order + [0] for order in plane_orders(replicas)]
    starts = []
    for order in orders:
        start = 0
        for level, bit in enumerate(order):
            start = start + bit_of(rep, bit) * (rows << level)
        starts.append(start)

    items = [(thing, step) for thing in range(2) for step in range(1, shards_n)]

    def source(third, shard, path):
        some = pl.ds(pl.multiple_of(starts[path], rows), rows)
        if third is None:
            at = shard * hidden + path * (hidden // 2)
            return up_ref.at[some, pl.ds(pl.multiple_of(at, 128), hidden // 2)]
        at = third * width + shard * wide + path * (wide // 2)
        return qkv_ref.at[some, pl.ds(pl.multiple_of(at, 128), wide // 2)]

    def target(third, shard, start, count, path):
        some = pl.ds(pl.multiple_of(shard * part + start, rows), count)
        if third is None:
            return up_out.at[some, pl.ds(path * (hidden // 2), hidden // 2)]
        return qkv_out.at[third, some, pl.ds(path * (wide // 2), wide // 2)]

    def turned(item, path, sending):
        thing, step = items[item]
        to = lax.rem(place + step, shards_n)
        shard = place if sending else lax.rem(place - step + shards_n, shards_n)
        return [
            remote(
                source(third, to, path),
                target(third, shard, starts[path], rows, path),
                turn_sem,
                (item, path, third or 0),
                {"shard": to},
            )
            for third in (range(3) if thing else (None,))
        ]

    def spread(item, path, level):
        thing, step = items[item]
        shard = lax.rem(place - step + shards_n, shards_n)
        order = orders[path]
        start = 0
        for above in range(level, bits):
            start = start + bit_of(rep, order[above]) * (rows << above)
        here = target(pl.ds(0, 3) if thing else None, shard, start, rows << level, path)
        return remote(
            here, here, plane_sem, (item, path, level), {"replica": flip(rep, order[level])}
        )

    def small_copy(step, sending):
        to = lax.rem(place + step, shards_n)
        shard = place if sending else lax.rem(place - step + shards_n, shards_n)
        return remote(small_ref, small_out.at[shard], small_sem, (step,), {"shard": to})

    def column_tick(tick):
        for level in reversed(range(bits + 1)):
            item = tick - level
            if not 0 <= item < len(items):
                continue
            for path in range(2):
                if level == 0:
                    for copy in turned(item, path, False):
                        copy.wait_recv()
                else:
                    spread(item, path, level - 1).wait_recv()
                if level < bits:
                    spread(item, path, level).start()

    def block_rows(block):
        return pl.ds(pl.multiple_of(block * local, local), local)

    def hop(way, step, sending):
        sign = 1 - 2 * way
        block = place - sign * (step if sending else step + 1)
        there = x_out.at[block_rows(block), :]
        return remote(
            x_ref if sending and step == 0 else there,
            there,
            hop_sem,
            (way, step),
            {"shard": lax.rem(place + sign + shards_n, shards_n)},
        )

    def upstream_copy(step, sending):
        to = lax.rem(place + step, shards_n)
        shard = place if sending else lax.rem(place - step + shards_n, shards_n)
        return remote(g_ref, g_out.at[block_rows(shard), :], g_sem, (0, step), {"shard": to})

    def to_end(block, end):
        there = g_out.at[block_rows(block), :]
        return remote(there, there, g_sem, (1, block), {"shard": end})

    ends = [(0, 1), (shards_n - 1, shards_n - 2)]
    passed = [list(range(2, shards_n)), list(range(shards_n - 3, -1, -1))]

    def pass_upstream(number):
        for (end, beside), blocks in zip(ends, passed):

            @pl.when(place == beside)
            def _():
                block = blocks[number]
                upstream_copy((beside - block) % shards_n, False).wait_recv()
                to_end(block, end).start()

    def holds(way, step):
        return place >= step if way == 0 else place + step < shards_n

    def goes(way, step):
        onward = place + 1 < shards_n if way == 0 else place >= 1
        return holds(way, step) & onward

    def send_hop(step):
        for way in range(2):

            @pl.when(goes(way, step))
            def _():
                hop(way, step, True).start()

    def pass_on(step):
        for way in range(2):

            @pl.when(holds(way, step))
            def _():
                hop(way, step - 1, False).wait_recv()

        if step + 1 < shards_n:
            send_hop(step)

    def load(number, src, dst):
        return pltpu.make_async_copy(src, dst, load_sem.at[number])

    def keep(number, src, dst):
        return pltpu.make_async_copy(src, dst, keep_sem.at[number])

    def norm(block, from_ref, slot):
        copy = load(slot, from_ref, x_rows.at[slot])
        copy.start()
        copy.wait()

        def some_rows(i, carry):
            here = pl.ds(pl.multiple_of(i * 32, 32), 32)
            there = pl.ds(pl.multiple_of(block * local + i * 32, 32), 32)
            values = x_rows[slot, here, :].astype(jnp.float32)
            mean = jnp.mean(values, -1, keepdims=True)
            centered = values - mean
            scale = lax.rsqrt(jnp.mean(centered * centered, -1, keepdims=True) + EPSILON)
            stats_out[0, there, :] = mean
            stats_out[1, there, :] = scale
            normed = centered * scale
            for z in range(shards_n):
                lanes = slice(z * part, (z + 1) * part)
                some = normed[:, lanes]
                attn[there, lanes] = (some * small[z, 0:1, :] + small[z, 1:2, :]).astype(jnp.bfloat16)
                mlp[there, lanes] = (some * small[z, 3:4, :] + small[z, 4:5, :]).astype(jnp.bfloat16)
            return carry

        lax.fori_loop(0, local // 32, some_rows, 0)

    def hidden_units(block):
        here = block_rows(block)

        def some_cols(k, carry):
            lanes = pl.ds(pl.multiple_of(k * cols, cols), cols)
            found = dot(mlp[here, :], up[:, lanes]) + bias_ref[0:1, lanes]
            cdf = 0.5 * (1.0 + lax.erf(found * math.sqrt(0.5)))
            act[here, lanes] = (found * cdf).astype(jnp.bfloat16)
            bell = jnp.exp(-0.5 * found * found) * (1.0 / math.sqrt(2.0 * math.pi))
            slope[here, lanes] = (cdf + found * bell).astype(jnp.bfloat16)
            return carry

        lax.fori_loop(0, hidden // cols, some_cols, 0)

    def tables(i, carry):
        some = local // 2
        here = pl.ds(pl.multiple_of(i * some, some), some)
        token = lax.broadcasted_iota(jnp.int32, (some, 128), 0) + i * some
        lane = lax.broadcasted_iota(jnp.int32, (some, 128), 1)
        first, end = jnp.zeros((some, 128), jnp.int32), 0
        for j in range(lengths_ref.shape[1]):
            length = lengths_ref[0, j]
            end = end + length
            first = first + jnp.where(token >= end, length, 0)
        first_out[here, :] = first[:, :1]
        angles = (token - first).astype(jnp.float32) * frequency_ref[0:1, :]
        sine = jnp.sin(angles)
        tables_out[0, here, :] = jnp.where(lane < ROT, jnp.cos(angles), 1.0)
        tables_out[1, here, :] = jnp.where(lane < ROT // 2, sine, 0.0)
        tables_out[2, here, :] = jnp.where((lane >= ROT // 2) & (lane < ROT), sine, 0.0)
        return carry

    def on_step(step, todo):
        for way in range(2):
            if step == 0 and way == 1:
                continue
            block = place - (1 - 2 * way) * step

            @pl.when(holds(way, step))
            def _():
                todo(block, way)

    def project(third):
        number = third * shards_n + place
        bias = small[lax.div(number, 3), pl.ds(6 + lax.rem(number, 3), 1), :]

        def some_rows(i, carry):
            here = pl.ds(pl.multiple_of(i * TALL, TALL), TALL)
            found = dot(attn[here, :], qkv[third]) + bias
            for head in range(wide // HEAD):
                mine = found[:, head * HEAD : (head + 1) * HEAD]
                if third < 2:
                    lead = mine[:, :128]
                    lead = (
                        lead * tables_out[0, here, :]
                        - pltpu.roll(lead, 96, 1) * tables_out[1, here, :]
                        + pltpu.roll(lead, 32, 1) * tables_out[2, here, :]
                    )
                    mine = jnp.concatenate([lead, mine[:, 128:]], 1)
                heads[third, here, head * HEAD : (head + 1) * HEAD] = mine.astype(jnp.bfloat16)
            return carry

        lax.fori_loop(0, tokens // TALL, some_rows, 0)

    def attend(head):
        lanes = slice(head * HEAD, (head + 1) * HEAD)
        for i in range(tokens // TILE):
            here, keys = slice(i * TILE, (i + 1) * TILE), slice(0, (i + 1) * TILE)
            probs = causal_probs(heads[0, here, lanes], heads[1, keys, lanes], first_out[here, :], i * TILE)
            mixed[here, lanes] = dot(probs.astype(jnp.bfloat16), heads[2, keys, lanes]).astype(jnp.bfloat16)

    def down_load(j):
        return load(4 + j % 2, down_ref.at[:, pl.ds(j * cols, cols)], down.at[j % 2])

    def branch_keep(j):
        return keep(6 + j, branch.at[j % 2], branch_out.at[:, pl.ds(j * cols, cols)])

    def branch_cols(j):
        down_load(j).wait()
        if j >= 2:
            branch_keep(j - 2).wait()

        def some_rows(i, carry):
            here = pl.ds(pl.multiple_of(i * TALL, TALL), TALL)
            found = dot(act[here, :], down[j % 2]) + dot(mixed[here, :], proj[:, j * cols : (j + 1) * cols])
            branch[j % 2, here, :] = found.astype(jnp.bfloat16)
            return carry

        lax.fori_loop(0, tokens // TALL, some_rows, 0)
        branch_keep(j).start()
        if j + 2 < width // cols:
            down_load(j + 2).start()

    greet(rep, place, replicas, shards_n)
    for step in range(1, shards_n):
        small_copy(step, True).start()
    for item in range(shards_n - 1):
        for path in range(2):
            for copy in turned(item, path, True):
                copy.start()
    send_hop(0)
    own = [
        (small_ref, small_out.at[place]),
        (
            up_ref.at[:, pl.ds(pl.multiple_of(place * hidden, 128), hidden)],
            up_out.at[pl.ds(pl.multiple_of(place * part, part), part), :],
        ),
        (x_ref, x_out.at[block_rows(place), :]),
        (g_ref, g_out.at[block_rows(place), :]),
    ] + [
        (
            qkv_ref.at[:, pl.ds(pl.multiple_of(third * width + place * wide, 128), wide)],
            qkv_out.at[third, pl.ds(pl.multiple_of(place * part, part), part), :],
        )
        for third in range(3)
    ]
    own = [pltpu.make_async_copy(src, dst, own_sem.at[i]) for i, (src, dst) in enumerate(own)]
    for copy in own:
        copy.start()
    down_load(0).start()
    down_load(1).start()
    load_proj = load(6, proj_ref, proj)
    load_proj.start()

    lax.fori_loop(0, 2 * shards_n, tables, 0)
    for step in range(1, shards_n):
        small_copy(step, False).wait()
    own[0].wait()
    load_small = load(0, small_out, small_low)
    load_small.start()
    load_small.wait()
    small[...] = small_low[...].astype(jnp.float32)
    on_step(0, lambda block, way: norm(block, x_ref, way))

    load_up = load(2, up_out, up)
    load_qkv = load(3, qkv_out, qkv)
    ticks = list(range(len(items) + bits))

    def some_ticks(number):
        for tick in ticks[:number]:
            column_tick(tick)
        del ticks[:number]

    def send_upstream(to_ends):
        for other in range(1, shards_n):
            to = lax.rem(place + other, shards_n)
            at_end = (to == 0) | (to == shards_n - 1)
            beside = ((to == 0) & (place == 1)) | ((to == shards_n - 1) & (place == shards_n - 2))

            @pl.when(beside if to_ends else jnp.logical_not(at_end))
            def _():
                upstream_copy(other, True).start()

    def arrive(step):
        pass_on(step)
        if step == 1:
            for item in range(shards_n - 1, len(items)):
                for path in range(2):
                    for copy in turned(item, path, True):
                        copy.start()
        if step == shards_n - 2:
            send_upstream(False)
        on_step(step, lambda block, way: norm(block, x_out.at[block_rows(block), :], way))

    some_ticks(3)
    arrive(1)
    some_ticks(shards_n - 1 + bits - 3)
    own[1].wait()
    load_up.start()
    load_up.wait()
    on_step(0, lambda block, way: hidden_units(block))
    for step in range(2, shards_n - 1):
        arrive(step)
    some_ticks(1)
    on_step(1, lambda block, way: hidden_units(block))
    some_ticks(1)
    for way in range(2):

        @pl.when(goes(way, shards_n - 2))
        def _():
            hop(way, shards_n - 2, True).wait_send()

    send_upstream(True)
    some_ticks(len(ticks))
    arrive(shards_n - 1)
    keeps = [keep(0, mlp, mlp_out), keep(1, attn, attn_out)]
    keeps[0].start()
    keeps[1].start()
    for copy in own[4:]:
        copy.wait()
    load_qkv.start()
    for step in range(2, shards_n):
        on_step(step, lambda block, way: hidden_units(block))
    pass_upstream(0)
    keeps += [keep(2, act, act_out), keep(3, slope, slope_out)]
    keeps[2].start()
    keeps[3].start()
    load_qkv.wait()
    for third in range(3):
        project(third)
    for number in range(1, shards_n - 2):
        pass_upstream(number)
    keeps.append(keep(4, heads, heads_out))
    keeps[4].start()
    for head in range(wide // HEAD):
        attend(head)
    keeps.append(keep(5, mixed, mixed_out))
    keeps[5].start()
    load_proj.wait()
    for j in range(width // cols):
        branch_cols(j)
    for step in range(1, shards_n):
        origin, onto = lax.rem(place - step + shards_n, shards_n), lax.rem(place + step, shards_n)
        inner = (place > 0) & (place < shards_n - 1)
        for end, beside in ends:

            @pl.when((place == end) & (origin == beside))
            def _():
                upstream_copy(step, False).wait_recv()

            @pl.when((place == end) & (origin != beside))
            def _():
                to_end(origin, end).wait_recv()

            @pl.when((onto == end) & (place == beside))
            def _():
                upstream_copy(step, True).wait_send()

        waited = False
        for (end, beside), blocks in zip(ends, passed):
            waited = waited | ((place == beside) & (origin != end))

        @pl.when(inner & jnp.logical_not(waited))
        def _():
            upstream_copy(step, False).wait_recv()

        @pl.when((onto > 0) & (onto < shards_n - 1))
        def _():
            upstream_copy(step, True).wait_send()

    for (end, beside), blocks in zip(ends, passed):
        for block in blocks:

            @pl.when(place == beside)
            def _():
                to_end(block, end).wait_send()

    for j in range(max(width // cols - 2, 0), width // cols):
        branch_keep(j).wait()
    for copy in keeps:
        copy.wait()
    for item in range(len(items)):
        for path in range(2):
            for copy in turned(item, path, True):
                copy.wait_send()
            for level in range(bits):
                spread(item, path, level).wait_send()
    for step in range(shards_n - 2):
        for way in range(2):

            @pl.when(goes(way, step))
            def _():
                hop(way, step, True).wait_send()

    for copy in own[2:4]:
        copy.wait()


def forward(small, up_weight, qkv_weight, x, g, down_weight, proj_weight, bias, frequency, lengths):
    replicas, count = lax.axis_size("replica"), lax.axis_size("shard")
    bits = replicas.bit_length() - 1
    local, width = x.shape
    tokens = local * count
    hidden, wide = up_weight.shape[1] // count, width // count
    cols = wide
    items = 2 * (count - 1)
    any_spec = pl.BlockSpec(memory_space=pl.ANY)
    vmem_spec = pl.BlockSpec(memory_space=pltpu.VMEM)
    shapes = dict(
        small=(count,) + small.shape,
        up_cols=(width, hidden),
        qkv_cols=(3, width, wide),
        x=(tokens, width),
        g=(tokens, width),
        mlp_in=(tokens, width),
        attn_in=(tokens, width),
        act=(tokens, hidden),
        slope=(tokens, hidden),
        heads=(3, tokens, wide),
        mixed=(tokens, wide),
        branch=(tokens, width),
    )
    low = lambda *shape: pltpu.VMEM(shape, jnp.bfloat16)
    dma = lambda *shape: pltpu.SemaphoreType.DMA(shape)
    found = pl.pallas_call(
        partial(forward_kernel, replicas, count),
        out_shape=tuple(jax.ShapeDtypeStruct(shape, jnp.bfloat16) for shape in shapes.values())
        + (
            jax.ShapeDtypeStruct((2, tokens, 1), jnp.float32),
            jax.ShapeDtypeStruct((3, tokens, 128), jnp.float32),
            jax.ShapeDtypeStruct((tokens, 1), jnp.int32),
        ),
        in_specs=[any_spec] * 7 + [vmem_spec] * 2 + [pl.BlockSpec(memory_space=pltpu.SMEM)],
        out_specs=(any_spec,) * len(shapes) + (vmem_spec,) * 3,
        scratch_shapes=[
            low(*shapes["small"]),
            pltpu.VMEM(shapes["small"], jnp.float32),
            low(2, local, width),
            low(tokens, width),
            low(tokens, width),
            low(width, hidden),
            low(3, width, wide),
            low(tokens, hidden),
            low(tokens, hidden),
            low(3, tokens, wide),
            low(tokens, wide),
            low(2, hidden, cols),
            low(wide, width),
            low(2, tokens, cols),
            dma(7),
            dma(7),
            dma(6 + width // cols),
            dma(2, count),
            dma(2, items, 2, 3),
            dma(2, items, 2, bits),
            dma(2, 2, count - 1),
            dma(2, 2, count),
        ],
        compiler_params=pltpu.CompilerParams(
            collective_id=0, has_side_effects=True, vmem_limit_bytes=58 * 2**20
        ),
        cost_estimate=pl.CostEstimate(
            flops=2 * tokens * width * (hidden * 2 + wide * 4),
            bytes_accessed=500_000_000,
            transcendentals=0,
        ),
    )(small, up_weight, qkv_weight, x, g, down_weight, proj_weight, bias, frequency, lengths)
    return dict(zip(list(shapes) + ["stats", "tables", "first"], found))


RING = 3


def grads_kernel(
    replicas,
    shards_n,
    act_ref,
    up_ref,
    mixed_ref,
    mlp_ref,
    attn_ref,
    slope_ref,
    down_ref,
    proj_ref,
    heads_ref,
    rows_ref,
    cols_up_ref,
    cols_qkv_ref,
    tables_ref,
    first_ref,
    stats_ref,
    small_ref,
    out_ref,
    vec_out,
    sum_out,
    work,
    from_core,
    *rest,
):
    rep, place = lax.axis_index("replica"), lax.axis_index("shard")
    bits = replicas.bit_length() - 1
    far = bits - 1
    from_far = rest[:far]
    (
        big,
        narrow,
        pre,
        joined,
        wide_rows,
        slope,
        heads,
        key_sum,
        value_sum,
        tile_x,
        tile_up,
        tile_qkv,
        shared,
        vec_got,
        vec_sum,
        load_sem,
        core_sem,
        far_sem,
        turn_sem,
        own_sem,
        plane_sem,
        vec_sem,
        sum_sem,
    ) = rest[far:]
    chunks, _, rows, cols = out_ref.shape
    slots = work.shape[0]
    half, side = rows // 2, cols // 2
    piece = rows // replicas
    orders = plane_orders(replicas)
    core = bit_of(rep, 0)
    tokens, width = up_ref.shape
    local = tokens // shards_n
    hiddens = pre.shape[1] // cols
    natives = hiddens + 1
    mine = pl.multiple_of(core * half, half)
    theirs = pl.multiple_of((1 - core) * half, half)

    starts = []
    for order in orders:
        line, size = [core * half], half
        for bit in order:
            size //= 2
            line.append(line[-1] + bit_of(rep, bit) * size)
        starts.append(line)

    def spot(k):
        if k < natives:
            return k + hiddens
        return k - natives if k < natives + hiddens else k

    def load(source, target, number):
        return pltpu.make_async_copy(source, target, load_sem.at[number])

    def narrow_load(k):
        source = act_ref.at[:, pl.ds(k * cols, cols)] if k < hiddens else mixed_ref
        return load(source, narrow.at[k % 2], k % 2)

    def big_load(which):
        return load((up_ref, mlp_ref, attn_ref)[which], big.at[which % 2], 2 + which)

    def down_load(k):
        return load(down_ref.at[pl.ds(k * cols, cols), :], wide_rows.at[k % 2], 5 + k % 2)

    def slope_load(k):
        return load(slope_ref.at[:, pl.ds(k * cols, cols)], slope.at[k % 2], 7 + k % 2)

    def pre_loads(k):
        return [down_load(k), slope_load(k)]

    def proj_load():
        return load(proj_ref, wide_rows.at[1], 6)

    def heads_load():
        return load(heads_ref, heads.at[pl.ds(0, 3)], 9)

    def tile_loads(j):
        some = pl.ds(j * TILE, TILE)
        return [
            load(rows_ref.at[:, some], tile_x.at[j % 2], 10 + j % 2),
            load(cols_up_ref.at[some, :], tile_up.at[j % 2], 12 + j % 2),
        ] + [
            load(
                cols_qkv_ref.at[third, some, :],
                tile_qkv.at[j % 2, :, pl.ds(third * cols, cols)],
                14 + 2 * third + j % 2,
            )
            for third in range(3)
        ]

    def to_core(k):
        return remote(
            work.at[k % slots, :, pl.ds(theirs, half), :],
            from_core.at[k % RING],
            core_sem,
            (0, k),
            {"replica": flip(rep, 0)},
        )

    def to_far(k, level, path):
        size = half >> (level + 1)
        bit = orders[path][level]
        start = starts[path][level] + (1 - bit_of(rep, bit)) * size
        return remote(
            work.at[k % slots, :, pl.ds(pl.multiple_of(start, size), size), pl.ds(path * side, side)],
            from_far[level].at[k % RING, path],
            far_sem,
            (k, level, path),
            {"replica": flip(rep, bit)},
        )

    def own_piece(k, path, block):
        return work.at[
            k % slots,
            block,
            pl.ds(pl.multiple_of(starts[path][far], piece), piece),
            pl.ds(path * side, side),
        ]

    def place_piece(k, path, block):
        return out_ref.at[
            spot(k),
            block,
            pl.ds(pl.multiple_of(starts[path][far], piece), piece),
            pl.ds(path * side, side),
        ]

    def settle(k, path):
        block = pl.ds(0, shards_n) if k < natives else place
        return pltpu.make_async_copy(
            own_piece(k, path, block), place_piece(k, path, block), own_sem.at[k % 2, path]
        )

    def turned(k, path, step, sending):
        to = lax.rem(place + step, shards_n)
        shard = place if sending else lax.rem(place - step + shards_n, shards_n)
        return remote(
            own_piece(k, path, to),
            place_piece(k, path, shard),
            turn_sem,
            (k - natives, path, step - 1),
            {"shard": to},
        )

    def spread(k, path, level):
        size = piece << level
        bit = orders[path][far - 1 - level]
        here = out_ref.at[
            spot(k),
            :,
            pl.ds(pl.multiple_of(starts[path][far - level], size), size),
            pl.ds(path * side, side),
        ]
        return remote(here, here, plane_sem, (k, level, path), {"replica": flip(rep, bit)})

    def spread_core(k):
        here = out_ref.at[spot(k), :, pl.ds(mine, half), :]
        return remote(here, here, core_sem, (1, k), {"replica": flip(rep, 0)})

    def put(offset, sums):
        for i in range(sums.shape[1] // 128):
            vec_sum[pl.ds(offset // 128 + i, 1), :] = sums[:, i * 128 : (i + 1) * 128]

    def compute(k):
        if k < natives:
            narrow_load(k).wait()
            if k + 1 < natives:
                narrow_load(k + 1).start()
        if k == 0:
            big_load(0).wait()
        if k == natives:
            big_load(1).wait()
        if k == natives + hiddens:
            big_load(2).wait()
        slot = k % slots
        which = 1 if natives <= k < natives + hiddens else 0

        def block(g, carry):
            if k < natives:
                left = narrow[k % 2]
                right = big[which, :, pl.ds(pl.multiple_of(g * cols, cols), cols)]
            else:
                left = big[which, :, pl.ds(pl.multiple_of(g * rows, rows), rows)]
                if k < natives + hiddens:
                    right = pre[:, (k - natives) * cols : (k - natives + 1) * cols]
                else:
                    third = k - natives - hiddens
                    right = joined[:, third * cols : (third + 1) * cols]
            work[slot, g] = dot_rows(left, right).astype(jnp.bfloat16)
            return carry

        lax.fori_loop(0, shards_n, block, 0)
        to_core(k).start()

    def add(k, start, size, left, width, got):
        def block(g, carry):
            where = (k % slots, g, pl.ds(pl.multiple_of(start, size), size), pl.ds(left, width))
            work[where] = (
                work[where].astype(jnp.float32) + got(g).astype(jnp.float32)
            ).astype(jnp.bfloat16)
            return carry

        lax.fori_loop(0, shards_n, block, 0)

    def grad_mixed():
        proj_load().wait()

        def block(i, carry):
            some = pl.ds(pl.multiple_of(i * TALL, TALL), TALL)
            heads[3, some, :] = dot_cols(big[0, some, :], wide_rows[1]).astype(jnp.bfloat16)
            return carry

        lax.fori_loop(0, tokens // TALL, block, 0)
        down_load(1).start()
        own = pl.ds(pl.multiple_of(place * cols, cols), cols)
        put(4 * width + place * cols, jnp.sum(big[0, :, own].astype(jnp.float32), 0, keepdims=True))

    def grad_pre(k):
        for copy in pre_loads(k):
            copy.wait()

        def block(i, total):
            some = pl.ds(pl.multiple_of(i * TALL, TALL), TALL)
            found = dot_cols(big[0, some, :], wide_rows[k % 2]) * slope[k % 2, some, :].astype(
                jnp.float32
            )
            low = found.astype(jnp.bfloat16)
            pre[some, k * cols : (k + 1) * cols] = low
            return total + jnp.sum(low.astype(jnp.float32), 0, keepdims=True)

        total = lax.fori_loop(0, tokens // TALL, block, jnp.zeros((1, cols), jnp.float32))
        put(8 * width + (place * hiddens + k) * cols, total)
        if k + 2 < hiddens:
            for copy in pre_loads(k + 2):
                copy.start()

    def turn_rows(found, some):
        lead = found[:, :128]
        lead = (
            lead * tables_ref[0, some, :]
            + pltpu.roll(lead, 96, 1) * tables_ref[1, some, :]
            - pltpu.roll(lead, 32, 1) * tables_ref[2, some, :]
        )
        return jnp.concatenate([lead, found[:, 128:]], 1)

    def attention(head):
        lanes = pl.ds(head * HEAD, HEAD)
        scale = 1.0 / math.sqrt(HEAD)
        key_sum[...] = jnp.zeros_like(key_sum)
        value_sum[...] = jnp.zeros_like(value_sum)
        sums = [jnp.zeros((1, HEAD), jnp.float32)] * 3
        for i in range(tokens // TILE):
            some, keys = pl.ds(i * TILE, TILE), pl.ds(0, (i + 1) * TILE)
            query = heads[0, some, lanes]
            key = heads[1, keys, lanes]
            probs = causal_probs(query, key, first_ref[some, :], i * TILE)
            grad = heads[3, some, lanes]
            grad_probs = dot_cols(grad, heads[2, keys, lanes])
            delta = jnp.sum(probs * grad_probs, -1, keepdims=True)
            low = (probs * (grad_probs - delta)).astype(jnp.bfloat16)
            found = turn_rows(dot(low, key) * scale, some).astype(jnp.bfloat16)
            joined[some, pl.ds(head * HEAD, HEAD)] = found
            sums[0] = sums[0] + jnp.sum(found.astype(jnp.float32), 0, keepdims=True)
            key_sum[keys, :] = key_sum[keys, :] + dot_rows(low, query)
            value_sum[keys, :] = value_sum[keys, :] + dot_rows(probs.astype(jnp.bfloat16), grad)
        for i in range(tokens // TILE):
            some = pl.ds(i * TILE, TILE)
            for third, found in (
                (1, turn_rows(key_sum[some, :] * scale, some)),
                (2, value_sum[some, :]),
            ):
                low = found.astype(jnp.bfloat16)
                joined[some, pl.ds(third * cols + head * HEAD, HEAD)] = low
                sums[third] = sums[third] + jnp.sum(low.astype(jnp.float32), 0, keepdims=True)
        for third in range(3):
            put(5 * width + third * width + place * cols + head * HEAD, sums[third])

    def sum_part(j, step, sending):
        to = lax.rem(place + step, shards_n)
        shard = place if sending else lax.rem(place - step + shards_n, shards_n)
        some = pl.ds(j * TILE, TILE)
        source = shared.at[pl.ds(pl.multiple_of(to * local, local), local), some]
        if step == 0:
            return pltpu.make_async_copy(source, sum_out.at[place, :, some], sum_sem.at[0, j, 0])
        return remote(source, sum_out.at[shard, :, some], sum_sem, (j, step), {"shard": to})

    def tile(j):
        for copy in tile_loads(j):
            copy.wait()
        if j + 1 < width // TILE:
            for copy in tile_loads(j + 1):
                copy.start()
        lanes = pl.ds(j * TILE, TILE)
        owner, begin = divmod(j * TILE, cols)
        theirs_at = slice(begin, begin + TILE)

        def block(i, totals):
            some = pl.ds(pl.multiple_of(i * TALL, TALL), TALL)
            normed = (tile_x[j % 2, some, :].astype(jnp.float32) - stats_ref[0, some, :]) * stats_ref[
                1, some, :
            ]
            mlp = dot_cols(pre[some, :], tile_up[j % 2])
            attn = dot_cols(joined[some, :], tile_qkv[j % 2])
            shared[some, lanes] = (
                attn * small_ref[owner, 0:1, theirs_at].astype(jnp.float32)
                + mlp * small_ref[owner, 3:4, theirs_at].astype(jnp.float32)
            ).astype(jnp.bfloat16)
            found = (attn * normed, attn, mlp * normed, mlp)
            return tuple(t + jnp.sum(f, 0, keepdims=True) for t, f in zip(totals, found))

        zero = jnp.zeros((1, TILE), jnp.float32)
        totals = lax.fori_loop(0, tokens // TALL, block, (zero,) * 4)
        for number, total in enumerate(totals):
            put(number * width + j * TILE, total)
        for step in range(shards_n):
            sum_part(j, step, True).start()

    def stage(k, number):
        if number == 0:
            compute(k)
        elif number == 1:
            to_core(k).wait()
            add(k, mine, half, 0, cols, lambda g: from_core[k % RING, g])
            for path in range(2):
                to_far(k, 0, path).start()
        elif number <= 1 + far:
            level = number - 2
            for path in range(2):
                to_far(k, level, path).wait()
                size = half >> (level + 1)
                add(
                    k,
                    starts[path][level + 1],
                    size,
                    path * side,
                    side,
                    lambda g: from_far[level][k % RING, path, g],
                )
                if level + 1 < far:
                    to_far(k, level + 1, path).start()
                else:
                    if k >= natives:
                        for step in range(1, shards_n):
                            turned(k, path, step, True).start()
                    settle(k, path).start()
        elif number == 2 + far:
            for path in range(2):
                settle(k, path).wait()
                if k >= natives:
                    for step in range(1, shards_n):
                        turned(k, path, step, False).wait_recv()
                spread(k, path, 0).start()
            if k >= natives:
                for path in range(2):
                    for step in range(1, shards_n):
                        turned(k, path, step, True).wait_send()
        elif number <= 2 + 2 * far:
            level = number - 3 - far
            for path in range(2):
                spread(k, path, level).wait()
                if level + 1 < far:
                    spread(k, path, level + 1).start()
            if level + 1 == far:
                spread_core(k).start()
        else:
            spread_core(k).wait()

    stages = 4 + 2 * far
    n_heads, n_tiles = cols // HEAD, width // TILE
    extras = {0: [grad_mixed, partial(grad_pre, 0)]}
    for k in range(1, hiddens):
        extras.setdefault(k, []).append(partial(grad_pre, k))
    for head in range(n_heads):
        extras.setdefault(1 + head, []).append(partial(attention, head))
    extras[hiddens] = [big_load(2).start]
    tile_at = hiddens + 1
    for j in range(n_tiles):
        extras.setdefault(tile_at + j, []).append(partial(tile, j))
    vec_at = max(extras) + 1

    for copy in [narrow_load(0), big_load(0), proj_load()] + pre_loads(0):
        copy.start()
    slope_load(1).start()
    for copy in [heads_load(), big_load(1)] + tile_loads(0):
        copy.start()
    vec_sum[...] = jnp.zeros_like(vec_sum)
    greet(rep, place, replicas, shards_n)
    peers = [{"replica": flip(rep, bit)} for bit in range(bits)]
    peers += [{"shard": flip(place, bit)} for bit in range(shards_n.bit_length() - 1)]

    def vec_copy(number):
        return remote(vec_sum, vec_got.at[number], vec_sem, (number,), peers[number])

    for tick in range(max(chunks + stages - 1, vec_at + len(peers) + 1)):
        for number in reversed(range(stages)):
            if 0 <= tick - number < chunks:
                stage(tick - number, number)
        if tick == 0:
            heads_load().wait()
        for extra in extras.get(tick, []):
            extra()
        turn_of = tick - vec_at
        if 0 < turn_of <= len(peers):
            vec_copy(turn_of - 1).wait()
            vec_sum[...] = vec_sum[...] + vec_got[turn_of - 1]
        if 0 <= turn_of < len(peers):
            vec_copy(turn_of).start()
    vec_out[...] = vec_sum[...]
    for j in range(n_tiles):
        for step in range(shards_n):
            sum_part(j, step, False).wait()


def summed_grads(*operands):
    act, up, mixed, mlp_in = operands[:4]
    replicas, count = lax.axis_size("replica"), lax.axis_size("shard")
    bits = replicas.bit_length() - 1
    far = bits - 1
    tokens, width = up.shape
    cols = width // count
    hidden = act.shape[1]
    hiddens = hidden // cols
    natives = hiddens + 1
    chunks = natives + hiddens + 3
    peers = bits + count.bit_length() - 1
    slots = 2 + far
    vector = ((8 * width + count * hidden) // 128, 128)
    any_spec = pl.BlockSpec(memory_space=pl.ANY)
    vmem_spec = pl.BlockSpec(memory_space=pltpu.VMEM)
    low = lambda *shape: pltpu.VMEM(shape, jnp.bfloat16)
    full = lambda *shape: pltpu.VMEM(shape, jnp.float32)
    dma = lambda *shape: pltpu.SemaphoreType.DMA(shape)
    return pl.pallas_call(
        partial(grads_kernel, replicas, count),
        out_shape=(
            jax.ShapeDtypeStruct((chunks, count, cols, cols), jnp.bfloat16),
            jax.ShapeDtypeStruct(vector, jnp.float32),
            jax.ShapeDtypeStruct((count, tokens // count, width), jnp.bfloat16),
        ),
        in_specs=[any_spec] * 12 + [vmem_spec] * 4,
        out_specs=(any_spec, vmem_spec, any_spec),
        scratch_shapes=[
            low(slots, count, cols, cols),
            low(RING, count, cols // 2, cols),
        ]
        + [low(RING, 2, count, cols >> (level + 2), cols // 2) for level in range(far)]
        + [
            low(2, tokens, width),
            low(2, tokens, cols),
            low(tokens, hidden),
            low(tokens, 3 * cols),
            low(2, cols, width),
            low(2, tokens, cols),
            low(4, tokens, cols),
            full(tokens, HEAD),
            full(tokens, HEAD),
            low(2, tokens, TILE),
            low(2, TILE, hidden),
            low(2, TILE, 3 * cols),
            low(tokens, width),
            full(peers, *vector),
            full(*vector),
            dma(20),
            dma(2, 2, chunks),
            dma(2, chunks, far, 2),
            dma(2, chunks - natives, 2, count - 1),
            dma(2, 2),
            dma(2, chunks, far, 2),
            dma(2, peers),
            dma(2, width // TILE, count),
        ],
        compiler_params=pltpu.CompilerParams(
            collective_id=1, has_side_effects=True, vmem_limit_bytes=60 * 2**20
        ),
        cost_estimate=pl.CostEstimate(
            flops=4 * tokens * chunks * count * cols * cols,
            bytes_accessed=600_000_000,
            transcendentals=0,
        ),
    )(*operands)


def last_kernel(
    up_blocks,
    down_blocks,
    out_blocks,
    qkv_blocks,
    parts_ref,
    branch_ref,
    x_ref,
    g_ref,
    small_ref,
    vec_ref,
    layer_out,
    input_out,
    up_out,
    down_out,
    out_out,
    qkv_out,
    *thin_outs,
):
    number, count, _, cols = up_blocks.shape
    for g in range(count):
        lanes = slice(g * cols, (g + 1) * cols)
        for k in range(number):
            at = (g * number + k) * cols
            up_out[:, at : at + cols] = up_blocks[k, g].astype(jnp.float32)
        for k in range(3):
            at = (k * count + g) * cols
            qkv_out[:, at : at + cols] = qkv_blocks[k, g].astype(jnp.float32)
        down_out[:, lanes] = down_blocks[0, g].astype(jnp.float32)
        out_out[:, lanes] = out_blocks[0, g].astype(jnp.float32)
    rows = x_ref[...].astype(jnp.float32)
    normed, inverse_std = normalize(rows)
    grad = sum(parts_ref[g].astype(jnp.float32) for g in range(count))
    input_out[...] = g_ref[...].astype(jnp.float32) + norm_backward(grad, normed, inverse_std)
    for g in range(count):
        lanes = slice(g * cols, (g + 1) * cols)
        bias = small_ref[g, 2:3, :].astype(jnp.float32) + small_ref[g, 5:6, :].astype(jnp.float32)
        layer_out[:, lanes] = (
            rows[:, lanes] + branch_ref[:, lanes].astype(jnp.float32) + bias
        ).astype(jnp.bfloat16)

    @pl.when(pl.program_id(0) == 0)
    def _():
        place = lax.axis_index("shard")
        width = count * cols
        for thin, start in zip(thin_outs, (0, 1, 4, 4, 2, 3, 5, 8)):
            length = thin.shape[0]
            first = (start * width + place * length) // 128
            for i in range(length // 128):
                thin[i * 128 : (i + 1) * 128] = vec_ref[first + i, :]


def last(blocks, parts, branch, x, g, small, vector):
    count, rows, cols = blocks.shape[1:]
    number = (blocks.shape[0] - 4) // 2
    local, width = x.shape
    steps = local // 16
    some, tall = rows // steps, number * rows // steps
    turns = rows // tall
    whole = lambda i: (i, 0)
    thin = [rows] * 6 + [3 * rows, number * rows]
    return pl.pallas_call(
        last_kernel,
        out_shape=(
            jax.ShapeDtypeStruct((local, width), jnp.bfloat16),
            jax.ShapeDtypeStruct((local, width), jnp.float32),
            jax.ShapeDtypeStruct((rows, number * width), jnp.float32),
            jax.ShapeDtypeStruct((number * rows, width), jnp.float32),
            jax.ShapeDtypeStruct((rows, width), jnp.float32),
            jax.ShapeDtypeStruct((rows, 3 * width), jnp.float32),
        )
        + tuple(jax.ShapeDtypeStruct((length,), jnp.float32) for length in thin),
        grid=(steps,),
        in_specs=[
            pl.BlockSpec((number, count, some, cols), lambda i: (0, 0, i, 0)),
            pl.BlockSpec((1, count, tall, cols), lambda i: (number + i // turns, 0, i % turns, 0)),
            pl.BlockSpec((1, count, some, cols), lambda i: (2 * number, 0, i, 0)),
            pl.BlockSpec((3, count, some, cols), lambda i: ((2 * number + 1) // 3, 0, i, 0)),
            pl.BlockSpec((count, 16, width), lambda i: (0, i, 0)),
            pl.BlockSpec((16, width), whole),
            pl.BlockSpec((16, width), whole),
            pl.BlockSpec((16, width), whole),
            pl.BlockSpec(small.shape, lambda i: (0, 0, 0)),
            pl.BlockSpec(vector.shape, lambda i: (0, 0)),
        ],
        out_specs=(
            pl.BlockSpec((16, width), whole),
            pl.BlockSpec((16, width), whole),
            pl.BlockSpec((some, number * width), whole),
            pl.BlockSpec((tall, width), whole),
            pl.BlockSpec((some, width), whole),
            pl.BlockSpec((some, 3 * width), whole),
        )
        + tuple(pl.BlockSpec((length,), lambda i: (0,)) for length in thin),
        compiler_params=pltpu.CompilerParams(vmem_limit_bytes=62 * 2**20),
    )(blocks, blocks, blocks, blocks, parts, branch, x, g, small, vector)


def shards(
    layer_input,
    attn_gain,
    attn_shift,
    qkv_weight,
    qkv_bias,
    out_weight,
    out_bias,
    mlp_gain,
    mlp_shift,
    up_weight,
    up_bias,
    down_weight,
    down_bias,
    seq_lengths,
    upstream,
):
    local_rows = layer_input.shape[0]
    count = lax.axis_size("shard")
    group_rows = local_rows * count
    place = lax.axis_index("shard")
    part = D // count
    hidden = up_bias.shape[0]

    params = [attn_gain, attn_shift, out_bias, mlp_gain, mlp_shift, down_bias]
    params += [qkv_bias[i * part : (i + 1) * part] for i in range(3)]
    row = lax.broadcasted_iota(jnp.int32, (16, part), 0)
    small = jnp.zeros((16, part), jnp.bfloat16)
    for i, param in enumerate(params):
        small = jnp.where(row == i, param[None], small)

    frequency = np.power(np.float32(ROPE_BASE), -np.arange(ROT // 2, dtype=np.float32) * np.float32(2.0 / ROT))
    known = forward(
        small,
        up_weight,
        qkv_weight,
        layer_input,
        upstream,
        down_weight,
        out_weight,
        up_bias.astype(jnp.float32)[None],
        jnp.asarray(np.tile(frequency, 128 // (ROT // 2))[None]),
        seq_lengths,
    )
    branch_own = lax.psum_scatter(known["branch"], "shard", scatter_dimension=0, tiled=True)
    grads, vector, normed_parts = summed_grads(
        known["act"],
        known["g"],
        known["mixed"],
        known["mlp_in"],
        known["attn_in"],
        known["slope"],
        down_weight,
        out_weight,
        known["heads"],
        known["x"],
        known["up_cols"],
        known["qkv_cols"],
        known["tables"],
        known["first"],
        known["stats"],
        known["small"],
    )
    grads, branch_own = lax.optimization_barrier((grads, branch_own))
    layer_output, input_grad, up_grad, down_grad, out_grad, qkv_grad, *thin = last(
        grads, normed_parts, branch_own, layer_input, upstream, known["small"], vector
    )
    return (
        layer_output,
        input_grad,
        thin[0],
        thin[1],
        qkv_grad,
        thin[6],
        out_grad,
        thin[2],
        thin[4],
        thin[5],
        up_grad,
        thin[7],
        down_grad,
        thin[3],
    )


def solution(mesh):
    in_specs = (
        P(("replica", "shard"), None),
        P("shard"),
        P("shard"),
        P("shard", None),
        P("shard"),
        P("shard", None),
        P("shard"),
        P("shard"),
        P("shard"),
        P("shard", None),
        P("shard"),
        P("shard", None),
        P("shard"),
        P("replica", None),
        P(("replica", "shard"), None),
    )
    out_specs = (
        P(("replica", "shard"), None),
        P(("replica", "shard"), None),
        P("shard"),
        P("shard"),
        P("shard", None),
        P("shard"),
        P("shard", None),
        P("shard"),
        P("shard"),
        P("shard"),
        P("shard", None),
        P("shard"),
        P("shard", None),
        P("shard"),
    )
    return jax.shard_map(shards, mesh=mesh, in_specs=in_specs, out_specs=out_specs, check_vma=False)
```

```python
from functools import partial
import math

import jax
import jax.numpy as jnp
import numpy as np
from jax import lax
from jax.experimental import pallas as pl
from jax.experimental.pallas import tpu as pltpu
from jax.sharding import PartitionSpec as P

D = 2048
HEADS = 8
HEAD = 256
ROT = 64


EPSILON = 1e-05
ROPE_BASE = 10000.0
NEG_LARGE = -1e30
MESH = pl.DeviceIdType.MESH
CONTRACT_ROWS = (((0,), (0,)), ((), ()))
CONTRACT_COLS = (((1,), (1,)), ((), ()))


def normalize(layer_rows):
    centered = layer_rows - jnp.mean(layer_rows, -1, keepdims=True)
    variance = jnp.mean(centered * centered, -1, keepdims=True)
    inverse_std = lax.rsqrt(variance + EPSILON)
    return (centered * inverse_std, inverse_std)


def norm_backward(grad_normed, normed, inverse_std):
    mean_grad = jnp.mean(grad_normed, -1, keepdims=True)
    mean_cross = jnp.mean(grad_normed * normed, -1, keepdims=True)
    return (grad_normed - mean_grad - normed * mean_cross) * inverse_std


def dot(left, right):
    return jnp.dot(left, right, preferred_element_type=jnp.float32)


def dot_rows(left, right):
    return lax.dot_general(left, right, CONTRACT_ROWS, preferred_element_type=jnp.float32)


def dot_cols(left, right):
    return lax.dot_general(left, right, CONTRACT_COLS, preferred_element_type=jnp.float32)


def bit_of(index, bit):
    return lax.rem(lax.div(index, 1 << bit), 2)


def flip(index, bit):
    return index + (1 << bit) * (1 - 2 * bit_of(index, bit))


def plane_orders(replicas):
    far = list(range(1, replicas.bit_length() - 1))
    return far, far[1:] + far[:1]


def remote(src, dst, sems, at, device):
    return pltpu.make_async_remote_copy(
        src_ref=src,
        dst_ref=dst,
        send_sem=sems.at[(0,) + at],
        recv_sem=sems.at[(1,) + at],
        device_id=device,
        device_id_type=MESH,
    )


def greet(rep, place, replicas, shards_n):
    barrier = pltpu.get_barrier_semaphore()
    bits = replicas.bit_length() - 1
    for bit in range(bits):
        pl.semaphore_signal(
            barrier, inc=1, device_id={"replica": flip(rep, bit)}, device_id_type=MESH
        )
    for step in range(1, shards_n):
        pl.semaphore_signal(
            barrier,
            inc=1,
            device_id={"shard": lax.rem(place + step, shards_n)},
            device_id_type=MESH,
        )
    pl.semaphore_wait(barrier, bits + shards_n - 1)


TILE = 256
TALL = 512


def causal_probs(query, key, first, row):
    shape = (query.shape[0], key.shape[0])
    scores = dot_cols(query, key) * (1.0 / math.sqrt(HEAD))
    at = lax.broadcasted_iota(jnp.int32, shape, 1)
    upto = lax.broadcasted_iota(jnp.int32, shape, 0) + row
    scores = jnp.where((at >= first) & (at <= upto), scores, NEG_LARGE)
    shifted = jnp.exp(scores - jnp.max(scores, -1, keepdims=True))
    return shifted / jnp.sum(shifted, -1, keepdims=True)


def forward_kernel(
    replicas,
    shards_n,
    small_ref,
    up_ref,
    qkv_ref,
    x_ref,
    g_ref,
    down_ref,
    proj_ref,
    bias_ref,
    frequency_ref,
    lengths_ref,
    small_out,
    up_out,
    qkv_out,
    x_out,
    g_out,
    mlp_out,
    attn_out,
    act_out,
    slope_out,
    heads_out,
    mixed_out,
    branch_out,
    stats_out,
    tables_out,
    first_out,
    small_low,
    small,
    x_rows,
    mlp,
    attn,
    up,
    qkv,
    act,
    slope,
    heads,
    mixed,
    down,
    proj,
    branch,
    own_sem,
    load_sem,
    keep_sem,
    small_sem,
    turn_sem,
    plane_sem,
    hop_sem,
    g_sem,
):
    rep, place = lax.axis_index("replica"), lax.axis_index("shard")
    bits = replicas.bit_length() - 1
    width, hidden = up_out.shape
    part = width // shards_n
    wide = qkv_out.shape[2]
    rows = part // replicas
    tokens = x_out.shape[0]
    local = tokens // shards_n
    cols = down.shape[2]
    orders = [order + [0] for order in plane_orders(replicas)]
    starts = []
    for order in orders:
        start = 0
        for level, bit in enumerate(order):
            start = start + bit_of(rep, bit) * (rows << level)
        starts.append(start)

    items = [(thing, step) for thing in range(2) for step in range(1, shards_n)]

    def source(third, shard, path):
        some = pl.ds(pl.multiple_of(starts[path], rows), rows)
        if third is None:
            at = shard * hidden + path * (hidden // 2)
            return up_ref.at[some, pl.ds(pl.multiple_of(at, 128), hidden // 2)]
        at = third * width + shard * wide + path * (wide // 2)
        return qkv_ref.at[some, pl.ds(pl.multiple_of(at, 128), wide // 2)]

    def target(third, shard, start, count, path):
        some = pl.ds(pl.multiple_of(shard * part + start, rows), count)
        if third is None:
            return up_out.at[some, pl.ds(path * (hidden // 2), hidden // 2)]
        return qkv_out.at[third, some, pl.ds(path * (wide // 2), wide // 2)]

    def turned(item, path, sending):
        thing, step = items[item]
        to = lax.rem(place + step, shards_n)
        shard = place if sending else lax.rem(place - step + shards_n, shards_n)
        return [
            remote(
                source(third, to, path),
                target(third, shard, starts[path], rows, path),
                turn_sem,
                (item, path, third or 0),
                {"shard": to},
            )
            for third in (range(3) if thing else (None,))
        ]

    def spread(item, path, level):
        thing, step = items[item]
        shard = lax.rem(place - step + shards_n, shards_n)
        order = orders[path]
        start = 0
        for above in range(level, bits):
            start = start + bit_of(rep, order[above]) * (rows << above)
        here = target(pl.ds(0, 3) if thing else None, shard, start, rows << level, path)
        return remote(
            here, here, plane_sem, (item, path, level), {"replica": flip(rep, order[level])}
        )

    def small_copy(step, sending):
        to = lax.rem(place + step, shards_n)
        shard = place if sending else lax.rem(place - step + shards_n, shards_n)
        return remote(small_ref, small_out.at[shard], small_sem, (step,), {"shard": to})

    def column_tick(thing, tick):
        for level in reversed(range(bits + 1)):
            if not 0 <= tick - level < shards_n - 1:
                continue
            item = thing * (shards_n - 1) + tick - level
            for path in range(2):
                if level == 0:
                    for copy in turned(item, path, False):
                        copy.wait_recv()
                else:
                    spread(item, path, level - 1).wait_recv()
                if level < bits:
                    spread(item, path, level).start()

    def block_rows(block):
        return pl.ds(pl.multiple_of(block * local, local), local)

    def hop(way, step, sending):
        sign = 1 - 2 * way
        block = place - sign * (step if sending else step + 1)
        there = x_out.at[block_rows(block), :]
        return remote(
            x_ref if sending and step == 0 else there,
            there,
            hop_sem,
            (way, step),
            {"shard": lax.rem(place + sign + shards_n, shards_n)},
        )

    def upstream_copy(step, sending):
        to = lax.rem(place + step, shards_n)
        shard = place if sending else lax.rem(place - step + shards_n, shards_n)
        return remote(g_ref, g_out.at[block_rows(shard), :], g_sem, (step,), {"shard": to})

    def holds(way, step):
        return place >= step if way == 0 else place + step < shards_n

    def goes(way, step):
        onward = place + 1 < shards_n if way == 0 else place >= 1
        return holds(way, step) & onward

    def send_hop(step):
        for way in range(2):

            @pl.when(goes(way, step))
            def _():
                hop(way, step, True).start()

    def pass_on(step):
        for way in range(2):

            @pl.when(holds(way, step))
            def _():
                hop(way, step - 1, False).wait_recv()

        if step + 1 < shards_n:
            send_hop(step)

    def load(number, src, dst):
        return pltpu.make_async_copy(src, dst, load_sem.at[number])

    def keep(number, src, dst):
        return pltpu.make_async_copy(src, dst, keep_sem.at[number])

    def norm(block, from_ref, slot):
        copy = load(slot, from_ref, x_rows.at[slot])
        copy.start()
        copy.wait()

        def some_rows(i, carry):
            here = pl.ds(pl.multiple_of(i * 32, 32), 32)
            there = pl.ds(pl.multiple_of(block * local + i * 32, 32), 32)
            values = x_rows[slot, here, :].astype(jnp.float32)
            mean = jnp.mean(values, -1, keepdims=True)
            centered = values - mean
            scale = lax.rsqrt(jnp.mean(centered * centered, -1, keepdims=True) + EPSILON)
            stats_out[0, there, :] = mean
            stats_out[1, there, :] = scale
            normed = centered * scale
            for z in range(shards_n):
                lanes = slice(z * part, (z + 1) * part)
                some = normed[:, lanes]
                attn[there, lanes] = (some * small[z, 0:1, :] + small[z, 1:2, :]).astype(jnp.bfloat16)
                mlp[there, lanes] = (some * small[z, 3:4, :] + small[z, 4:5, :]).astype(jnp.bfloat16)
            return carry

        lax.fori_loop(0, local // 32, some_rows, 0)

    def hidden_units(block):
        here = block_rows(block)

        def some_cols(k, carry):
            lanes = pl.ds(pl.multiple_of(k * cols, cols), cols)
            found = dot(mlp[here, :], up[:, lanes]) + bias_ref[0:1, lanes]
            cdf = 0.5 * (1.0 + lax.erf(found * math.sqrt(0.5)))
            act[here, lanes] = (found * cdf).astype(jnp.bfloat16)
            bell = jnp.exp(-0.5 * found * found) * (1.0 / math.sqrt(2.0 * math.pi))
            slope[here, lanes] = (cdf + found * bell).astype(jnp.bfloat16)
            return carry

        lax.fori_loop(0, hidden // cols, some_cols, 0)

    def tables(i, carry):
        some = local // 2
        here = pl.ds(pl.multiple_of(i * some, some), some)
        token = lax.broadcasted_iota(jnp.int32, (some, 128), 0) + i * some
        lane = lax.broadcasted_iota(jnp.int32, (some, 128), 1)
        first, end = jnp.zeros((some, 128), jnp.int32), 0
        for j in range(lengths_ref.shape[1]):
            length = lengths_ref[0, j]
            end = end + length
            first = first + jnp.where(token >= end, length, 0)
        first_out[here, :] = first[:, :1]
        angles = (token - first).astype(jnp.float32) * frequency_ref[0:1, :]
        sine = jnp.sin(angles)
        tables_out[0, here, :] = jnp.where(lane < ROT, jnp.cos(angles), 1.0)
        tables_out[1, here, :] = jnp.where(lane < ROT // 2, sine, 0.0)
        tables_out[2, here, :] = jnp.where((lane >= ROT // 2) & (lane < ROT), sine, 0.0)
        return carry

    def on_step(step, todo):
        for way in range(2):
            if step == 0 and way == 1:
                continue
            block = place - (1 - 2 * way) * step

            @pl.when(holds(way, step))
            def _():
                todo(block, way)

    def project(third):
        number = third * shards_n + place
        bias = small[lax.div(number, 3), pl.ds(6 + lax.rem(number, 3), 1), :]

        def some_rows(i, carry):
            here = pl.ds(pl.multiple_of(i * TALL, TALL), TALL)
            found = dot(attn[here, :], qkv[third]) + bias
            for head in range(wide // HEAD):
                mine = found[:, head * HEAD : (head + 1) * HEAD]
                if third < 2:
                    lead = mine[:, :128]
                    lead = (
                        lead * tables_out[0, here, :]
                        - pltpu.roll(lead, 96, 1) * tables_out[1, here, :]
                        + pltpu.roll(lead, 32, 1) * tables_out[2, here, :]
                    )
                    mine = jnp.concatenate([lead, mine[:, 128:]], 1)
                heads[third, here, head * HEAD : (head + 1) * HEAD] = mine.astype(jnp.bfloat16)
            return carry

        lax.fori_loop(0, tokens // TALL, some_rows, 0)

    def attend(head):
        lanes = slice(head * HEAD, (head + 1) * HEAD)
        for i in range(tokens // TILE):
            here, keys = slice(i * TILE, (i + 1) * TILE), slice(0, (i + 1) * TILE)
            probs = causal_probs(heads[0, here, lanes], heads[1, keys, lanes], first_out[here, :], i * TILE)
            mixed[here, lanes] = dot(probs.astype(jnp.bfloat16), heads[2, keys, lanes]).astype(jnp.bfloat16)

    def down_load(j):
        return load(4 + j % 2, down_ref.at[:, pl.ds(j * cols, cols)], down.at[j % 2])

    def branch_keep(j):
        return keep(6 + j, branch.at[j % 2], branch_out.at[:, pl.ds(j * cols, cols)])

    def branch_cols(j):
        down_load(j).wait()
        if j >= 2:
            branch_keep(j - 2).wait()

        def some_rows(i, carry):
            here = pl.ds(pl.multiple_of(i * TALL, TALL), TALL)
            found = dot(act[here, :], down[j % 2]) + dot(mixed[here, :], proj[:, j * cols : (j + 1) * cols])
            branch[j % 2, here, :] = found.astype(jnp.bfloat16)
            return carry

        lax.fori_loop(0, tokens // TALL, some_rows, 0)
        branch_keep(j).start()
        if j + 2 < width // cols:
            down_load(j + 2).start()

    greet(rep, place, replicas, shards_n)
    for step in range(1, shards_n):
        small_copy(step, True).start()
    for item in range(shards_n - 1):
        for path in range(2):
            for copy in turned(item, path, True):
                copy.start()
    send_hop(0)
    own = [
        (small_ref, small_out.at[place]),
        (
            up_ref.at[:, pl.ds(pl.multiple_of(place * hidden, 128), hidden)],
            up_out.at[pl.ds(pl.multiple_of(place * part, part), part), :],
        ),
        (x_ref, x_out.at[block_rows(place), :]),
        (g_ref, g_out.at[block_rows(place), :]),
    ] + [
        (
            qkv_ref.at[:, pl.ds(pl.multiple_of(third * width + place * wide, 128), wide)],
            qkv_out.at[third, pl.ds(pl.multiple_of(place * part, part), part), :],
        )
        for third in range(3)
    ]
    own = [pltpu.make_async_copy(src, dst, own_sem.at[i]) for i, (src, dst) in enumerate(own)]
    for copy in own:
        copy.start()
    down_load(0).start()
    down_load(1).start()
    load_proj = load(6, proj_ref, proj)
    load_proj.start()

    lax.fori_loop(0, 2 * shards_n, tables, 0)
    for step in range(1, shards_n):
        small_copy(step, False).wait()
    own[0].wait()
    load_small = load(0, small_out, small_low)
    load_small.start()
    load_small.wait()
    small[...] = small_low[...].astype(jnp.float32)
    on_step(0, lambda block, way: norm(block, x_ref, way))

    load_up = load(2, up_out, up)
    load_qkv = load(3, qkv_out, qkv)
    ticks = [list(range(shards_n - 1 + bits)) for thing in range(2)]

    def some_ticks(thing, number):
        for tick in ticks[thing][:number]:
            column_tick(thing, tick)
        del ticks[thing][:number]

    def send_upstream(to_ends):
        for other in range(1, shards_n):
            to = lax.rem(place + other, shards_n)
            at_end = (to == 0) | (to == shards_n - 1)

            @pl.when(at_end if to_ends else jnp.logical_not(at_end))
            def _():
                upstream_copy(other, True).start()

    def norms(step):
        on_step(step, lambda block, way: norm(block, x_out.at[block_rows(block), :], way))

    def units(step):
        on_step(step, lambda block, way: hidden_units(block))

    some_ticks(0, 3)
    pass_on(1)
    norms(1)
    some_ticks(0, len(ticks[0]))
    own[1].wait()
    load_up.start()
    for step in range(2, shards_n - 1):
        pass_on(step)
    for item in range(shards_n - 1, len(items)):
        for path in range(2):
            for copy in turned(item, path, True):
                copy.start()
    send_upstream(False)
    load_up.wait()
    units(0)
    for step in range(2, shards_n - 1):
        norms(step)
    some_ticks(1, 1)
    units(1)
    some_ticks(1, 1)
    for way in range(2):

        @pl.when(goes(way, shards_n - 2))
        def _():
            hop(way, shards_n - 2, True).wait_send()

    send_upstream(True)
    pass_on(shards_n - 1)
    norms(shards_n - 1)
    some_ticks(1, 1)
    keeps = [keep(0, mlp, mlp_out), keep(1, attn, attn_out)]
    keeps[0].start()
    keeps[1].start()
    for step in range(2, shards_n):
        units(step)
        some_ticks(1, 1)
    some_ticks(1, len(ticks[1]))
    for copy in own[4:]:
        copy.wait()
    load_qkv.start()
    keeps += [keep(2, act, act_out), keep(3, slope, slope_out)]
    keeps[2].start()
    keeps[3].start()
    load_qkv.wait()
    for third in range(3):
        project(third)
    keeps.append(keep(4, heads, heads_out))
    keeps[4].start()
    for head in range(wide // HEAD):
        attend(head)
    keeps.append(keep(5, mixed, mixed_out))
    keeps[5].start()
    load_proj.wait()
    for j in range(width // cols):
        branch_cols(j)
    for step in range(1, shards_n):
        upstream_copy(step, False).wait()
    for j in range(max(width // cols - 2, 0), width // cols):
        branch_keep(j).wait()
    for copy in keeps:
        copy.wait()
    for item in range(len(items)):
        for path in range(2):
            for copy in turned(item, path, True):
                copy.wait_send()
            for level in range(bits):
                spread(item, path, level).wait_send()
    for step in range(shards_n - 2):
        for way in range(2):

            @pl.when(goes(way, step))
            def _():
                hop(way, step, True).wait_send()

    for copy in own[2:4]:
        copy.wait()


def forward(small, up_weight, qkv_weight, x, g, down_weight, proj_weight, bias, frequency, lengths):
    replicas, count = lax.axis_size("replica"), lax.axis_size("shard")
    bits = replicas.bit_length() - 1
    local, width = x.shape
    tokens = local * count
    hidden, wide = up_weight.shape[1] // count, width // count
    cols = wide
    items = 2 * (count - 1)
    any_spec = pl.BlockSpec(memory_space=pl.ANY)
    vmem_spec = pl.BlockSpec(memory_space=pltpu.VMEM)
    shapes = dict(
        small=(count,) + small.shape,
        up_cols=(width, hidden),
        qkv_cols=(3, width, wide),
        x=(tokens, width),
        g=(tokens, width),
        mlp_in=(tokens, width),
        attn_in=(tokens, width),
        act=(tokens, hidden),
        slope=(tokens, hidden),
        heads=(3, tokens, wide),
        mixed=(tokens, wide),
        branch=(tokens, width),
    )
    low = lambda *shape: pltpu.VMEM(shape, jnp.bfloat16)
    dma = lambda *shape: pltpu.SemaphoreType.DMA(shape)
    found = pl.pallas_call(
        partial(forward_kernel, replicas, count),
        out_shape=tuple(jax.ShapeDtypeStruct(shape, jnp.bfloat16) for shape in shapes.values())
        + (
            jax.ShapeDtypeStruct((2, tokens, 1), jnp.float32),
            jax.ShapeDtypeStruct((3, tokens, 128), jnp.float32),
            jax.ShapeDtypeStruct((tokens, 1), jnp.int32),
        ),
        in_specs=[any_spec] * 7 + [vmem_spec] * 2 + [pl.BlockSpec(memory_space=pltpu.SMEM)],
        out_specs=(any_spec,) * len(shapes) + (vmem_spec,) * 3,
        scratch_shapes=[
            low(*shapes["small"]),
            pltpu.VMEM(shapes["small"], jnp.float32),
            low(2, local, width),
            low(tokens, width),
            low(tokens, width),
            low(width, hidden),
            low(3, width, wide),
            low(tokens, hidden),
            low(tokens, hidden),
            low(3, tokens, wide),
            low(tokens, wide),
            low(2, hidden, cols),
            low(wide, width),
            low(2, tokens, cols),
            dma(7),
            dma(7),
            dma(6 + width // cols),
            dma(2, count),
            dma(2, items, 2, 3),
            dma(2, items, 2, bits),
            dma(2, 2, count - 1),
            dma(2, count),
        ],
        compiler_params=pltpu.CompilerParams(
            collective_id=0, has_side_effects=True, vmem_limit_bytes=58 * 2**20
        ),
        cost_estimate=pl.CostEstimate(
            flops=2 * tokens * width * (hidden * 2 + wide * 4),
            bytes_accessed=500_000_000,
            transcendentals=0,
        ),
    )(small, up_weight, qkv_weight, x, g, down_weight, proj_weight, bias, frequency, lengths)
    return dict(zip(list(shapes) + ["stats", "tables", "first"], found))


RING = 3


def grads_kernel(
    replicas,
    shards_n,
    act_ref,
    up_ref,
    mixed_ref,
    mlp_ref,
    attn_ref,
    slope_ref,
    down_ref,
    proj_ref,
    heads_ref,
    rows_ref,
    cols_up_ref,
    cols_qkv_ref,
    tables_ref,
    first_ref,
    stats_ref,
    small_ref,
    out_ref,
    vec_out,
    sum_out,
    work,
    from_core,
    *rest,
):
    rep, place = lax.axis_index("replica"), lax.axis_index("shard")
    bits = replicas.bit_length() - 1
    far = bits - 1
    from_far = rest[:far]
    (
        big,
        narrow,
        pre,
        joined,
        wide_rows,
        slope,
        heads,
        key_sum,
        value_sum,
        tile_x,
        tile_up,
        tile_qkv,
        shared,
        vec_got,
        vec_sum,
        load_sem,
        core_sem,
        far_sem,
        turn_sem,
        own_sem,
        plane_sem,
        vec_sem,
        sum_sem,
    ) = rest[far:]
    chunks, _, rows, cols = out_ref.shape
    slots = work.shape[0]
    half, side = rows // 2, cols // 2
    piece = rows // replicas
    orders = plane_orders(replicas)
    core = bit_of(rep, 0)
    tokens, width = up_ref.shape
    local = tokens // shards_n
    hiddens = pre.shape[1] // cols
    natives = hiddens + 1
    mine = pl.multiple_of(core * half, half)
    theirs = pl.multiple_of((1 - core) * half, half)

    starts = []
    for order in orders:
        line, size = [core * half], half
        for bit in order:
            size //= 2
            line.append(line[-1] + bit_of(rep, bit) * size)
        starts.append(line)

    def spot(k):
        if k < natives:
            return k + hiddens
        return k - natives if k < natives + hiddens else k

    def load(source, target, number):
        return pltpu.make_async_copy(source, target, load_sem.at[number])

    def narrow_load(k):
        source = act_ref.at[:, pl.ds(k * cols, cols)] if k < hiddens else mixed_ref
        return load(source, narrow.at[k % 2], k % 2)

    def big_load(which):
        return load((up_ref, mlp_ref, attn_ref)[which], big.at[which % 2], 2 + which)

    def down_load(k):
        return load(down_ref.at[pl.ds(k * cols, cols), :], wide_rows.at[k % 2], 5 + k % 2)

    def slope_load(k):
        return load(slope_ref.at[:, pl.ds(k * cols, cols)], slope.at[k % 2], 7 + k % 2)

    def pre_loads(k):
        return [down_load(k), slope_load(k)]

    def proj_load():
        return load(proj_ref, wide_rows.at[1], 6)

    def heads_load():
        return load(heads_ref, heads.at[pl.ds(0, 3)], 9)

    def tile_loads(j):
        some = pl.ds(j * TILE, TILE)
        return [
            load(rows_ref.at[:, some], tile_x.at[j % 2], 10 + j % 2),
            load(cols_up_ref.at[some, :], tile_up.at[j % 2], 12 + j % 2),
        ] + [
            load(
                cols_qkv_ref.at[third, some, :],
                tile_qkv.at[j % 2, :, pl.ds(third * cols, cols)],
                14 + 2 * third + j % 2,
            )
            for third in range(3)
        ]

    def to_core(k):
        return remote(
            work.at[k % slots, :, pl.ds(theirs, half), :],
            from_core.at[k % RING],
            core_sem,
            (0, k),
            {"replica": flip(rep, 0)},
        )

    def to_far(k, level, path):
        size = half >> (level + 1)
        bit = orders[path][level]
        start = starts[path][level] + (1 - bit_of(rep, bit)) * size
        return remote(
            work.at[k % slots, :, pl.ds(pl.multiple_of(start, size), size), pl.ds(path * side, side)],
            from_far[level].at[k % RING, path],
            far_sem,
            (k, level, path),
            {"replica": flip(rep, bit)},
        )

    def own_piece(k, path, block):
        return work.at[
            k % slots,
            block,
            pl.ds(pl.multiple_of(starts[path][far], piece), piece),
            pl.ds(path * side, side),
        ]

    def place_piece(k, path, block):
        return out_ref.at[
            spot(k),
            block,
            pl.ds(pl.multiple_of(starts[path][far], piece), piece),
            pl.ds(path * side, side),
        ]

    def settle(k, path):
        block = pl.ds(0, shards_n) if k < natives else place
        return pltpu.make_async_copy(
            own_piece(k, path, block), place_piece(k, path, block), own_sem.at[k % 2, path]
        )

    def turned(k, path, step, sending):
        to = lax.rem(place + step, shards_n)
        shard = place if sending else lax.rem(place - step + shards_n, shards_n)
        return remote(
            own_piece(k, path, to),
            place_piece(k, path, shard),
            turn_sem,
            (k - natives, path, step - 1),
            {"shard": to},
        )

    def spread(k, path, level):
        size = piece << level
        bit = orders[path][far - 1 - level]
        here = out_ref.at[
            spot(k),
            :,
            pl.ds(pl.multiple_of(starts[path][far - level], size), size),
            pl.ds(path * side, side),
        ]
        return remote(here, here, plane_sem, (k, level, path), {"replica": flip(rep, bit)})

    def spread_core(k):
        here = out_ref.at[spot(k), :, pl.ds(mine, half), :]
        return remote(here, here, core_sem, (1, k), {"replica": flip(rep, 0)})

    def put(offset, sums):
        for i in range(sums.shape[1] // 128):
            vec_sum[pl.ds(offset // 128 + i, 1), :] = sums[:, i * 128 : (i + 1) * 128]

    def compute(k):
        if k < natives:
            narrow_load(k).wait()
            if k + 1 < natives:
                narrow_load(k + 1).start()
        if k == 0:
            big_load(0).wait()
        if k == natives:
            big_load(1).wait()
        if k == natives + hiddens:
            big_load(2).wait()
        slot = k % slots
        which = 1 if natives <= k < natives + hiddens else 0

        def block(g, carry):
            if k < natives:
                left = narrow[k % 2]
                right = big[which, :, pl.ds(pl.multiple_of(g * cols, cols), cols)]
            else:
                left = big[which, :, pl.ds(pl.multiple_of(g * rows, rows), rows)]
                if k < natives + hiddens:
                    right = pre[:, (k - natives) * cols : (k - natives + 1) * cols]
                else:
                    third = k - natives - hiddens
                    right = joined[:, third * cols : (third + 1) * cols]
            work[slot, g] = dot_rows(left, right).astype(jnp.bfloat16)
            return carry

        lax.fori_loop(0, shards_n, block, 0)
        to_core(k).start()

    def add(k, start, size, left, width, got):
        def block(g, carry):
            where = (k % slots, g, pl.ds(pl.multiple_of(start, size), size), pl.ds(left, width))
            work[where] = (
                work[where].astype(jnp.float32) + got(g).astype(jnp.float32)
            ).astype(jnp.bfloat16)
            return carry

        lax.fori_loop(0, shards_n, block, 0)

    def grad_mixed():
        proj_load().wait()

        def block(i, carry):
            some = pl.ds(pl.multiple_of(i * TALL, TALL), TALL)
            heads[3, some, :] = dot_cols(big[0, some, :], wide_rows[1]).astype(jnp.bfloat16)
            return carry

        lax.fori_loop(0, tokens // TALL, block, 0)
        down_load(1).start()
        own = pl.ds(pl.multiple_of(place * cols, cols), cols)
        put(4 * width + place * cols, jnp.sum(big[0, :, own].astype(jnp.float32), 0, keepdims=True))

    def grad_pre(k):
        for copy in pre_loads(k):
            copy.wait()

        def block(i, total):
            some = pl.ds(pl.multiple_of(i * TALL, TALL), TALL)
            found = dot_cols(big[0, some, :], wide_rows[k % 2]) * slope[k % 2, some, :].astype(
                jnp.float32
            )
            low = found.astype(jnp.bfloat16)
            pre[some, k * cols : (k + 1) * cols] = low
            return total + jnp.sum(low.astype(jnp.float32), 0, keepdims=True)

        total = lax.fori_loop(0, tokens // TALL, block, jnp.zeros((1, cols), jnp.float32))
        put(8 * width + (place * hiddens + k) * cols, total)
        if k + 2 < hiddens:
            for copy in pre_loads(k + 2):
                copy.start()

    def turn_rows(found, some):
        lead = found[:, :128]
        lead = (
            lead * tables_ref[0, some, :]
            + pltpu.roll(lead, 96, 1) * tables_ref[1, some, :]
            - pltpu.roll(lead, 32, 1) * tables_ref[2, some, :]
        )
        return jnp.concatenate([lead, found[:, 128:]], 1)

    def attention(head):
        lanes = pl.ds(head * HEAD, HEAD)
        scale = 1.0 / math.sqrt(HEAD)
        key_sum[...] = jnp.zeros_like(key_sum)
        value_sum[...] = jnp.zeros_like(value_sum)
        sums = [jnp.zeros((1, HEAD), jnp.float32)] * 3
        for i in range(tokens // TILE):
            some, keys = pl.ds(i * TILE, TILE), pl.ds(0, (i + 1) * TILE)
            query = heads[0, some, lanes]
            key = heads[1, keys, lanes]
            probs = causal_probs(query, key, first_ref[some, :], i * TILE)
            grad = heads[3, some, lanes]
            grad_probs = dot_cols(grad, heads[2, keys, lanes])
            delta = jnp.sum(probs * grad_probs, -1, keepdims=True)
            low = (probs * (grad_probs - delta)).astype(jnp.bfloat16)
            found = turn_rows(dot(low, key) * scale, some).astype(jnp.bfloat16)
            joined[some, pl.ds(head * HEAD, HEAD)] = found
            sums[0] = sums[0] + jnp.sum(found.astype(jnp.float32), 0, keepdims=True)
            key_sum[keys, :] = key_sum[keys, :] + dot_rows(low, query)
            value_sum[keys, :] = value_sum[keys, :] + dot_rows(probs.astype(jnp.bfloat16), grad)
        for i in range(tokens // TILE):
            some = pl.ds(i * TILE, TILE)
            for third, found in (
                (1, turn_rows(key_sum[some, :] * scale, some)),
                (2, value_sum[some, :]),
            ):
                low = found.astype(jnp.bfloat16)
                joined[some, pl.ds(third * cols + head * HEAD, HEAD)] = low
                sums[third] = sums[third] + jnp.sum(low.astype(jnp.float32), 0, keepdims=True)
        for third in range(3):
            put(5 * width + third * width + place * cols + head * HEAD, sums[third])

    def sum_part(j, step, sending):
        to = lax.rem(place + step, shards_n)
        shard = place if sending else lax.rem(place - step + shards_n, shards_n)
        some = pl.ds(j * TILE, TILE)
        source = shared.at[pl.ds(pl.multiple_of(to * local, local), local), some]
        if step == 0:
            return pltpu.make_async_copy(source, sum_out.at[place, :, some], sum_sem.at[0, j, 0])
        return remote(source, sum_out.at[shard, :, some], sum_sem, (j, step), {"shard": to})

    def tile(j):
        for copy in tile_loads(j):
            copy.wait()
        if j + 1 < width // TILE:
            for copy in tile_loads(j + 1):
                copy.start()
        lanes = pl.ds(j * TILE, TILE)
        owner, begin = divmod(j * TILE, cols)
        theirs_at = slice(begin, begin + TILE)

        def block(i, totals):
            some = pl.ds(pl.multiple_of(i * TALL, TALL), TALL)
            normed = (tile_x[j % 2, some, :].astype(jnp.float32) - stats_ref[0, some, :]) * stats_ref[
                1, some, :
            ]
            mlp = dot_cols(pre[some, :], tile_up[j % 2])
            attn = dot_cols(joined[some, :], tile_qkv[j % 2])
            shared[some, lanes] = (
                attn * small_ref[owner, 0:1, theirs_at].astype(jnp.float32)
                + mlp * small_ref[owner, 3:4, theirs_at].astype(jnp.float32)
            ).astype(jnp.bfloat16)
            found = (attn * normed, attn, mlp * normed, mlp)
            return tuple(t + jnp.sum(f, 0, keepdims=True) for t, f in zip(totals, found))

        zero = jnp.zeros((1, TILE), jnp.float32)
        totals = lax.fori_loop(0, tokens // TALL, block, (zero,) * 4)
        for number, total in enumerate(totals):
            put(number * width + j * TILE, total)
        for step in range(shards_n):
            sum_part(j, step, True).start()

    def stage(k, number):
        if number == 0:
            compute(k)
        elif number == 1:
            to_core(k).wait()
            add(k, mine, half, 0, cols, lambda g: from_core[k % RING, g])
            for path in range(2):
                to_far(k, 0, path).start()
        elif number <= 1 + far:
            level = number - 2
            for path in range(2):
                to_far(k, level, path).wait()
                size = half >> (level + 1)
                add(
                    k,
                    starts[path][level + 1],
                    size,
                    path * side,
                    side,
                    lambda g: from_far[level][k % RING, path, g],
                )
                if level + 1 < far:
                    to_far(k, level + 1, path).start()
                else:
                    if k >= natives:
                        for step in range(1, shards_n):
                            turned(k, path, step, True).start()
                    settle(k, path).start()
        elif number == 2 + far:
            for path in range(2):
                settle(k, path).wait()
                if k >= natives:
                    for step in range(1, shards_n):
                        turned(k, path, step, False).wait_recv()
                spread(k, path, 0).start()
            if k >= natives:
                for path in range(2):
                    for step in range(1, shards_n):
                        turned(k, path, step, True).wait_send()
        elif number <= 2 + 2 * far:
            level = number - 3 - far
            for path in range(2):
                spread(k, path, level).wait()
                if level + 1 < far:
                    spread(k, path, level + 1).start()
            if level + 1 == far:
                spread_core(k).start()
        else:
            spread_core(k).wait()

    stages = 4 + 2 * far
    n_heads, n_tiles = cols // HEAD, width // TILE
    extras = {0: [grad_mixed, partial(grad_pre, 0)]}
    for k in range(1, hiddens):
        extras.setdefault(k, []).append(partial(grad_pre, k))
    for head in range(n_heads):
        extras.setdefault(1 + head, []).append(partial(attention, head))
    extras[hiddens] = [big_load(2).start]
    tile_at = hiddens + 1
    for j in range(n_tiles):
        extras.setdefault(tile_at + j, []).append(partial(tile, j))
    vec_at = max(extras) + 1

    for copy in [narrow_load(0), big_load(0), proj_load()] + pre_loads(0):
        copy.start()
    slope_load(1).start()
    for copy in [heads_load(), big_load(1)] + tile_loads(0):
        copy.start()
    vec_sum[...] = jnp.zeros_like(vec_sum)
    greet(rep, place, replicas, shards_n)
    peers = [{"replica": flip(rep, bit)} for bit in range(bits)]
    peers += [{"shard": flip(place, bit)} for bit in range(shards_n.bit_length() - 1)]

    def vec_copy(number):
        return remote(vec_sum, vec_got.at[number], vec_sem, (number,), peers[number])

    for tick in range(max(chunks + stages - 1, vec_at + len(peers) + 1)):
        for number in reversed(range(stages)):
            if 0 <= tick - number < chunks:
                stage(tick - number, number)
        if tick == 0:
            heads_load().wait()
        for extra in extras.get(tick, []):
            extra()
        turn_of = tick - vec_at
        if 0 < turn_of <= len(peers):
            vec_copy(turn_of - 1).wait()
            vec_sum[...] = vec_sum[...] + vec_got[turn_of - 1]
        if 0 <= turn_of < len(peers):
            vec_copy(turn_of).start()
    vec_out[...] = vec_sum[...]
    for j in range(n_tiles):
        for step in range(shards_n):
            sum_part(j, step, False).wait()


def summed_grads(*operands):
    act, up, mixed, mlp_in = operands[:4]
    replicas, count = lax.axis_size("replica"), lax.axis_size("shard")
    bits = replicas.bit_length() - 1
    far = bits - 1
    tokens, width = up.shape
    cols = width // count
    hidden = act.shape[1]
    hiddens = hidden // cols
    natives = hiddens + 1
    chunks = natives + hiddens + 3
    peers = bits + count.bit_length() - 1
    slots = 2 + far
    vector = ((8 * width + count * hidden) // 128, 128)
    any_spec = pl.BlockSpec(memory_space=pl.ANY)
    vmem_spec = pl.BlockSpec(memory_space=pltpu.VMEM)
    low = lambda *shape: pltpu.VMEM(shape, jnp.bfloat16)
    full = lambda *shape: pltpu.VMEM(shape, jnp.float32)
    dma = lambda *shape: pltpu.SemaphoreType.DMA(shape)
    return pl.pallas_call(
        partial(grads_kernel, replicas, count),
        out_shape=(
            jax.ShapeDtypeStruct((chunks, count, cols, cols), jnp.bfloat16),
            jax.ShapeDtypeStruct(vector, jnp.float32),
            jax.ShapeDtypeStruct((count, tokens // count, width), jnp.bfloat16),
        ),
        in_specs=[any_spec] * 12 + [vmem_spec] * 4,
        out_specs=(any_spec, vmem_spec, any_spec),
        scratch_shapes=[
            low(slots, count, cols, cols),
            low(RING, count, cols // 2, cols),
        ]
        + [low(RING, 2, count, cols >> (level + 2), cols // 2) for level in range(far)]
        + [
            low(2, tokens, width),
            low(2, tokens, cols),
            low(tokens, hidden),
            low(tokens, 3 * cols),
            low(2, cols, width),
            low(2, tokens, cols),
            low(4, tokens, cols),
            full(tokens, HEAD),
            full(tokens, HEAD),
            low(2, tokens, TILE),
            low(2, TILE, hidden),
            low(2, TILE, 3 * cols),
            low(tokens, width),
            full(peers, *vector),
            full(*vector),
            dma(20),
            dma(2, 2, chunks),
            dma(2, chunks, far, 2),
            dma(2, chunks - natives, 2, count - 1),
            dma(2, 2),
            dma(2, chunks, far, 2),
            dma(2, peers),
            dma(2, width // TILE, count),
        ],
        compiler_params=pltpu.CompilerParams(
            collective_id=1, has_side_effects=True, vmem_limit_bytes=60 * 2**20
        ),
        cost_estimate=pl.CostEstimate(
            flops=4 * tokens * chunks * count * cols * cols,
            bytes_accessed=600_000_000,
            transcendentals=0,
        ),
    )(*operands)


def last_kernel(
    up_blocks,
    down_blocks,
    out_blocks,
    qkv_blocks,
    parts_ref,
    branch_ref,
    x_ref,
    g_ref,
    small_ref,
    vec_ref,
    layer_out,
    input_out,
    up_out,
    down_out,
    out_out,
    qkv_out,
    *thin_outs,
):
    number, count, _, cols = up_blocks.shape
    for g in range(count):
        lanes = slice(g * cols, (g + 1) * cols)
        for k in range(number):
            at = (g * number + k) * cols
            up_out[:, at : at + cols] = up_blocks[k, g].astype(jnp.float32)
        for k in range(3):
            at = (k * count + g) * cols
            qkv_out[:, at : at + cols] = qkv_blocks[k, g].astype(jnp.float32)
        down_out[:, lanes] = down_blocks[0, g].astype(jnp.float32)
        out_out[:, lanes] = out_blocks[0, g].astype(jnp.float32)
    rows = x_ref[...].astype(jnp.float32)
    normed, inverse_std = normalize(rows)
    grad = sum(parts_ref[g].astype(jnp.float32) for g in range(count))
    input_out[...] = g_ref[...].astype(jnp.float32) + norm_backward(grad, normed, inverse_std)
    for g in range(count):
        lanes = slice(g * cols, (g + 1) * cols)
        bias = small_ref[g, 2:3, :].astype(jnp.float32) + small_ref[g, 5:6, :].astype(jnp.float32)
        layer_out[:, lanes] = (
            rows[:, lanes] + branch_ref[:, lanes].astype(jnp.float32) + bias
        ).astype(jnp.bfloat16)

    @pl.when(pl.program_id(0) == 0)
    def _():
        place = lax.axis_index("shard")
        width = count * cols
        for thin, start in zip(thin_outs, (0, 1, 4, 4, 2, 3, 5, 8)):
            length = thin.shape[0]
            first = (start * width + place * length) // 128
            for i in range(length // 128):
                thin[i * 128 : (i + 1) * 128] = vec_ref[first + i, :]


def last(blocks, parts, branch, x, g, small, vector):
    count, rows, cols = blocks.shape[1:]
    number = (blocks.shape[0] - 4) // 2
    local, width = x.shape
    steps = local // 16
    some, tall = rows // steps, number * rows // steps
    turns = rows // tall
    whole = lambda i: (i, 0)
    thin = [rows] * 6 + [3 * rows, number * rows]
    return pl.pallas_call(
        last_kernel,
        out_shape=(
            jax.ShapeDtypeStruct((local, width), jnp.bfloat16),
            jax.ShapeDtypeStruct((local, width), jnp.float32),
            jax.ShapeDtypeStruct((rows, number * width), jnp.float32),
            jax.ShapeDtypeStruct((number * rows, width), jnp.float32),
            jax.ShapeDtypeStruct((rows, width), jnp.float32),
            jax.ShapeDtypeStruct((rows, 3 * width), jnp.float32),
        )
        + tuple(jax.ShapeDtypeStruct((length,), jnp.float32) for length in thin),
        grid=(steps,),
        in_specs=[
            pl.BlockSpec((number, count, some, cols), lambda i: (0, 0, i, 0)),
            pl.BlockSpec((1, count, tall, cols), lambda i: (number + i // turns, 0, i % turns, 0)),
            pl.BlockSpec((1, count, some, cols), lambda i: (2 * number, 0, i, 0)),
            pl.BlockSpec((3, count, some, cols), lambda i: ((2 * number + 1) // 3, 0, i, 0)),
            pl.BlockSpec((count, 16, width), lambda i: (0, i, 0)),
            pl.BlockSpec((16, width), whole),
            pl.BlockSpec((16, width), whole),
            pl.BlockSpec((16, width), whole),
            pl.BlockSpec(small.shape, lambda i: (0, 0, 0)),
            pl.BlockSpec(vector.shape, lambda i: (0, 0)),
        ],
        out_specs=(
            pl.BlockSpec((16, width), whole),
            pl.BlockSpec((16, width), whole),
            pl.BlockSpec((some, number * width), whole),
            pl.BlockSpec((tall, width), whole),
            pl.BlockSpec((some, width), whole),
            pl.BlockSpec((some, 3 * width), whole),
        )
        + tuple(pl.BlockSpec((length,), lambda i: (0,)) for length in thin),
        compiler_params=pltpu.CompilerParams(vmem_limit_bytes=62 * 2**20),
    )(blocks, blocks, blocks, blocks, parts, branch, x, g, small, vector)


def shards(
    layer_input,
    attn_gain,
    attn_shift,
    qkv_weight,
    qkv_bias,
    out_weight,
    out_bias,
    mlp_gain,
    mlp_shift,
    up_weight,
    up_bias,
    down_weight,
    down_bias,
    seq_lengths,
    upstream,
):
    local_rows = layer_input.shape[0]
    count = lax.axis_size("shard")
    group_rows = local_rows * count
    place = lax.axis_index("shard")
    part = D // count
    hidden = up_bias.shape[0]

    params = [attn_gain, attn_shift, out_bias, mlp_gain, mlp_shift, down_bias]
    params += [qkv_bias[i * part : (i + 1) * part] for i in range(3)]
    row = lax.broadcasted_iota(jnp.int32, (16, part), 0)
    small = jnp.zeros((16, part), jnp.bfloat16)
    for i, param in enumerate(params):
        small = jnp.where(row == i, param[None], small)

    frequency = np.power(np.float32(ROPE_BASE), -np.arange(ROT // 2, dtype=np.float32) * np.float32(2.0 / ROT))
    known = forward(
        small,
        up_weight,
        qkv_weight,
        layer_input,
        upstream,
        down_weight,
        out_weight,
        up_bias.astype(jnp.float32)[None],
        jnp.asarray(np.tile(frequency, 128 // (ROT // 2))[None]),
        seq_lengths,
    )
    branch_own = lax.psum_scatter(known["branch"], "shard", scatter_dimension=0, tiled=True)
    grads, vector, normed_parts = summed_grads(
        known["act"],
        known["g"],
        known["mixed"],
        known["mlp_in"],
        known["attn_in"],
        known["slope"],
        down_weight,
        out_weight,
        known["heads"],
        known["x"],
        known["up_cols"],
        known["qkv_cols"],
        known["tables"],
        known["first"],
        known["stats"],
        known["small"],
    )
    grads, branch_own = lax.optimization_barrier((grads, branch_own))
    layer_output, input_grad, up_grad, down_grad, out_grad, qkv_grad, *thin = last(
        grads, normed_parts, branch_own, layer_input, upstream, known["small"], vector
    )
    return (
        layer_output,
        input_grad,
        thin[0],
        thin[1],
        qkv_grad,
        thin[6],
        out_grad,
        thin[2],
        thin[4],
        thin[5],
        up_grad,
        thin[7],
        down_grad,
        thin[3],
    )


def solution(mesh):
    in_specs = (
        P(("replica", "shard"), None),
        P("shard"),
        P("shard"),
        P("shard", None),
        P("shard"),
        P("shard", None),
        P("shard"),
        P("shard"),
        P("shard"),
        P("shard", None),
        P("shard"),
        P("shard", None),
        P("shard"),
        P("replica", None),
        P(("replica", "shard"), None),
    )
    out_specs = (
        P(("replica", "shard"), None),
        P(("replica", "shard"), None),
        P("shard"),
        P("shard"),
        P("shard", None),
        P("shard"),
        P("shard", None),
        P("shard"),
        P("shard"),
        P("shard"),
        P("shard", None),
        P("shard"),
        P("shard", None),
        P("shard"),
    )
    return jax.shard_map(shards, mesh=mesh, in_specs=in_specs, out_specs=out_specs, check_vma=False)
```

```python
from functools import partial
import math

import jax
import jax.numpy as jnp
import numpy as np
from jax import lax
from jax.experimental import pallas as pl
from jax.experimental.pallas import tpu as pltpu
from jax.sharding import PartitionSpec as P

D = 2048
HEADS = 8
HEAD = 256
ROT = 64


EPSILON = 1e-05
ROPE_BASE = 10000.0
NEG_LARGE = -1e30
MESH = pl.DeviceIdType.MESH
CONTRACT_ROWS = (((0,), (0,)), ((), ()))
CONTRACT_COLS = (((1,), (1,)), ((), ()))


def normalize(layer_rows):
    centered = layer_rows - jnp.mean(layer_rows, -1, keepdims=True)
    variance = jnp.mean(centered * centered, -1, keepdims=True)
    inverse_std = lax.rsqrt(variance + EPSILON)
    return (centered * inverse_std, inverse_std)


def norm_backward(grad_normed, normed, inverse_std):
    mean_grad = jnp.mean(grad_normed, -1, keepdims=True)
    mean_cross = jnp.mean(grad_normed * normed, -1, keepdims=True)
    return (grad_normed - mean_grad - normed * mean_cross) * inverse_std


def dot(left, right):
    return jnp.dot(left, right, preferred_element_type=jnp.float32)


def dot_rows(left, right):
    return lax.dot_general(left, right, CONTRACT_ROWS, preferred_element_type=jnp.float32)


def dot_cols(left, right):
    return lax.dot_general(left, right, CONTRACT_COLS, preferred_element_type=jnp.float32)


def bit_of(index, bit):
    return lax.rem(lax.div(index, 1 << bit), 2)


def flip(index, bit):
    return index + (1 << bit) * (1 - 2 * bit_of(index, bit))


def plane_orders(replicas):
    far = list(range(1, replicas.bit_length() - 1))
    return far, far[1:] + far[:1]


def remote(src, dst, sems, at, device):
    return pltpu.make_async_remote_copy(
        src_ref=src,
        dst_ref=dst,
        send_sem=sems.at[(0,) + at],
        recv_sem=sems.at[(1,) + at],
        device_id=device,
        device_id_type=MESH,
    )


def greet(rep, place, replicas, shards_n):
    barrier = pltpu.get_barrier_semaphore()
    bits = replicas.bit_length() - 1
    for bit in range(bits):
        pl.semaphore_signal(
            barrier, inc=1, device_id={"replica": flip(rep, bit)}, device_id_type=MESH
        )
    for step in range(1, shards_n):
        pl.semaphore_signal(
            barrier,
            inc=1,
            device_id={"shard": lax.rem(place + step, shards_n)},
            device_id_type=MESH,
        )
    pl.semaphore_wait(barrier, bits + shards_n - 1)


TILE = 256
TALL = 1024


def causal_probs(query, key, first, row):
    shape = (query.shape[0], key.shape[0])
    scores = dot_cols(query, key) * (1.0 / math.sqrt(HEAD))
    at = lax.broadcasted_iota(jnp.int32, shape, 1)
    upto = lax.broadcasted_iota(jnp.int32, shape, 0) + row
    scores = jnp.where((at >= first) & (at <= upto), scores, NEG_LARGE)
    shifted = jnp.exp(scores - jnp.max(scores, -1, keepdims=True))
    return shifted * (1.0 / jnp.sum(shifted, -1, keepdims=True))


def forward_kernel(
    replicas,
    shards_n,
    small_ref,
    up_ref,
    qkv_ref,
    x_ref,
    g_ref,
    down_ref,
    proj_ref,
    bias_ref,
    frequency_ref,
    lengths_ref,
    small_out,
    up_out,
    qkv_out,
    x_out,
    g_out,
    mlp_out,
    attn_out,
    act_out,
    slope_out,
    heads_out,
    mixed_out,
    branch_out,
    stats_out,
    tables_out,
    first_out,
    small_low,
    small,
    x_rows,
    mlp,
    attn,
    up,
    qkv,
    act,
    slope,
    heads,
    mixed,
    down,
    proj,
    branch,
    own_sem,
    load_sem,
    keep_sem,
    small_sem,
    turn_sem,
    plane_sem,
    hop_sem,
    g_sem,
):
    rep, place = lax.axis_index("replica"), lax.axis_index("shard")
    bits = replicas.bit_length() - 1
    width, hidden = up_out.shape
    part = width // shards_n
    wide = qkv_out.shape[2]
    rows = part // replicas
    tokens = x_out.shape[0]
    local = tokens // shards_n
    cols = down.shape[2]
    orders = [order + [0] for order in plane_orders(replicas)]
    starts = []
    for order in orders:
        start = 0
        for level, bit in enumerate(order):
            start = start + bit_of(rep, bit) * (rows << level)
        starts.append(start)

    items = [(thing, step) for thing in range(2) for step in range(1, shards_n)]

    def source(third, shard, path):
        some = pl.ds(pl.multiple_of(starts[path], rows), rows)
        if third is None:
            at = shard * hidden + path * (hidden // 2)
            return up_ref.at[some, pl.ds(pl.multiple_of(at, 128), hidden // 2)]
        at = third * width + shard * wide + path * (wide // 2)
        return qkv_ref.at[some, pl.ds(pl.multiple_of(at, 128), wide // 2)]

    def target(third, shard, start, count, path):
        some = pl.ds(pl.multiple_of(shard * part + start, rows), count)
        if third is None:
            return up_out.at[some, pl.ds(path * (hidden // 2), hidden // 2)]
        return qkv_out.at[third, some, pl.ds(path * (wide // 2), wide // 2)]

    def turned(item, path, sending):
        thing, step = items[item]
        to = lax.rem(place + step, shards_n)
        shard = place if sending else lax.rem(place - step + shards_n, shards_n)
        return [
            remote(
                source(third, to, path),
                target(third, shard, starts[path], rows, path),
                turn_sem,
                (item, path, third or 0),
                {"shard": to},
            )
            for third in (range(3) if thing else (None,))
        ]

    def spread(item, path, level):
        thing, step = items[item]
        shard = lax.rem(place - step + shards_n, shards_n)
        order = orders[path]
        start = 0
        for above in range(level, bits):
            start = start + bit_of(rep, order[above]) * (rows << above)
        here = target(pl.ds(0, 3) if thing else None, shard, start, rows << level, path)
        return remote(
            here, here, plane_sem, (item, path, level), {"replica": flip(rep, order[level])}
        )

    def small_copy(step, sending):
        to = lax.rem(place + step, shards_n)
        shard = place if sending else lax.rem(place - step + shards_n, shards_n)
        return remote(small_ref, small_out.at[shard], small_sem, (step,), {"shard": to})

    def column_tick(thing, tick):
        for level in reversed(range(bits + 1)):
            if not 0 <= tick - level < shards_n - 1:
                continue
            item = thing * (shards_n - 1) + tick - level
            for path in range(2):
                if level == 0:
                    for copy in turned(item, path, False):
                        copy.wait_recv()
                else:
                    spread(item, path, level - 1).wait_recv()
                if level < bits:
                    spread(item, path, level).start()

    def block_rows(block):
        return pl.ds(pl.multiple_of(block * local, local), local)

    def hop(way, step, sending):
        sign = 1 - 2 * way
        block = place - sign * (step if sending else step + 1)
        there = x_out.at[block_rows(block), :]
        return remote(
            x_ref if sending and step == 0 else there,
            there,
            hop_sem,
            (way, step),
            {"shard": lax.rem(place + sign + shards_n, shards_n)},
        )

    def upstream_copy(step, sending):
        to = lax.rem(place + step, shards_n)
        shard = place if sending else lax.rem(place - step + shards_n, shards_n)
        return remote(g_ref, g_out.at[block_rows(shard), :], g_sem, (step,), {"shard": to})

    def holds(way, step):
        return place >= step if way == 0 else place + step < shards_n

    def goes(way, step):
        onward = place + 1 < shards_n if way == 0 else place >= 1
        return holds(way, step) & onward

    def send_hop(step):
        for way in range(2):

            @pl.when(goes(way, step))
            def _():
                hop(way, step, True).start()

    def pass_on(step):
        for way in range(2):

            @pl.when(holds(way, step))
            def _():
                hop(way, step - 1, False).wait_recv()

        if step + 1 < shards_n:
            send_hop(step)

    def load(number, src, dst):
        return pltpu.make_async_copy(src, dst, load_sem.at[number])

    def keep(number, src, dst):
        return pltpu.make_async_copy(src, dst, keep_sem.at[number])

    def norm(block, from_ref, slot):
        copy = load(slot, from_ref, x_rows.at[slot])
        copy.start()
        copy.wait()

        def some_rows(i, carry):
            here = pl.ds(pl.multiple_of(i * 32, 32), 32)
            there = pl.ds(pl.multiple_of(block * local + i * 32, 32), 32)
            values = x_rows[slot, here, :].astype(jnp.float32)
            mean = jnp.mean(values, -1, keepdims=True)
            centered = values - mean
            scale = lax.rsqrt(jnp.mean(centered * centered, -1, keepdims=True) + EPSILON)
            stats_out[0, there, :] = mean
            stats_out[1, there, :] = scale
            normed = centered * scale
            for z in range(shards_n):
                lanes = slice(z * part, (z + 1) * part)
                some = normed[:, lanes]
                attn[there, lanes] = (some * small[z, 0:1, :] + small[z, 1:2, :]).astype(jnp.bfloat16)
                mlp[there, lanes] = (some * small[z, 3:4, :] + small[z, 4:5, :]).astype(jnp.bfloat16)
            return carry

        lax.fori_loop(0, local // 32, some_rows, 0)

    def hidden_units(block):
        here = block_rows(block)

        def some_cols(k, carry):
            lanes = pl.ds(pl.multiple_of(k * cols, cols), cols)
            found = dot(mlp[here, :], up[:, lanes]) + bias_ref[0:1, lanes]
            cdf = 0.5 * (1.0 + lax.erf(found * math.sqrt(0.5)))
            act[here, lanes] = (found * cdf).astype(jnp.bfloat16)
            bell = jnp.exp(-0.5 * found * found) * (1.0 / math.sqrt(2.0 * math.pi))
            slope[here, lanes] = (cdf + found * bell).astype(jnp.bfloat16)
            return carry

        lax.fori_loop(0, hidden // cols, some_cols, 0)

    def tables(i, carry):
        some = local // 2
        here = pl.ds(pl.multiple_of(i * some, some), some)
        token = lax.broadcasted_iota(jnp.int32, (some, 128), 0) + i * some
        lane = lax.broadcasted_iota(jnp.int32, (some, 128), 1)
        first, end = jnp.zeros((some, 128), jnp.int32), 0
        for j in range(lengths_ref.shape[1]):
            length = lengths_ref[0, j]
            end = end + length
            first = first + jnp.where(token >= end, length, 0)
        first_out[here, :] = first[:, :1]
        angles = (token - first).astype(jnp.float32) * frequency_ref[0:1, :]
        sine = jnp.sin(angles)
        tables_out[0, here, :] = jnp.where(lane < ROT, jnp.cos(angles), 1.0)
        tables_out[1, here, :] = jnp.where(lane < ROT // 2, sine, 0.0)
        tables_out[2, here, :] = jnp.where((lane >= ROT // 2) & (lane < ROT), sine, 0.0)
        return carry

    def on_step(step, todo):
        for way in range(2):
            if step == 0 and way == 1:
                continue
            block = place - (1 - 2 * way) * step

            @pl.when(holds(way, step))
            def _():
                todo(block, way)

    def project(third):
        number = third * shards_n + place
        bias = small[lax.div(number, 3), pl.ds(6 + lax.rem(number, 3), 1), :]

        def some_rows(i, carry):
            here = pl.ds(pl.multiple_of(i * TALL, TALL), TALL)
            found = dot(attn[here, :], qkv[third]) + bias
            for head in range(wide // HEAD):
                mine = found[:, head * HEAD : (head + 1) * HEAD]
                if third < 2:
                    lead = mine[:, :128]
                    lead = (
                        lead * tables_out[0, here, :]
                        - pltpu.roll(lead, 96, 1) * tables_out[1, here, :]
                        + pltpu.roll(lead, 32, 1) * tables_out[2, here, :]
                    )
                    mine = jnp.concatenate([lead, mine[:, 128:]], 1)
                heads[third, here, head * HEAD : (head + 1) * HEAD] = mine.astype(jnp.bfloat16)
            return carry

        lax.fori_loop(0, tokens // TALL, some_rows, 0)

    def attend(head):
        lanes = slice(head * HEAD, (head + 1) * HEAD)
        for i in range(tokens // TILE):
            here, keys = slice(i * TILE, (i + 1) * TILE), slice(0, (i + 1) * TILE)
            probs = causal_probs(heads[0, here, lanes], heads[1, keys, lanes], first_out[here, :], i * TILE)
            mixed[here, lanes] = dot(probs.astype(jnp.bfloat16), heads[2, keys, lanes]).astype(jnp.bfloat16)

    def down_load(j):
        return load(4 + j % 2, down_ref.at[:, pl.ds(j * cols, cols)], down.at[j % 2])

    def branch_keep(j):
        return keep(6 + j, branch.at[j % 2], branch_out.at[:, pl.ds(j * cols, cols)])

    def branch_cols(j):
        down_load(j).wait()
        if j >= 2:
            branch_keep(j - 2).wait()

        def some_rows(i, carry):
            here = pl.ds(pl.multiple_of(i * TALL, TALL), TALL)
            found = dot(act[here, :], down[j % 2]) + dot(mixed[here, :], proj[:, j * cols : (j + 1) * cols])
            branch[j % 2, here, :] = found.astype(jnp.bfloat16)
            return carry

        lax.fori_loop(0, tokens // TALL, some_rows, 0)
        branch_keep(j).start()
        if j + 2 < width // cols:
            down_load(j + 2).start()

    greet(rep, place, replicas, shards_n)
    for step in range(1, shards_n):
        small_copy(step, True).start()
    for item in range(shards_n - 1):
        for path in range(2):
            for copy in turned(item, path, True):
                copy.start()
    send_hop(0)
    own = [
        (small_ref, small_out.at[place]),
        (
            up_ref.at[:, pl.ds(pl.multiple_of(place * hidden, 128), hidden)],
            up_out.at[pl.ds(pl.multiple_of(place * part, part), part), :],
        ),
        (x_ref, x_out.at[block_rows(place), :]),
        (g_ref, g_out.at[block_rows(place), :]),
    ] + [
        (
            qkv_ref.at[:, pl.ds(pl.multiple_of(third * width + place * wide, 128), wide)],
            qkv_out.at[third, pl.ds(pl.multiple_of(place * part, part), part), :],
        )
        for third in range(3)
    ]
    own = [pltpu.make_async_copy(src, dst, own_sem.at[i]) for i, (src, dst) in enumerate(own)]
    for copy in own:
        copy.start()
    down_load(0).start()
    down_load(1).start()
    load_proj = load(6, proj_ref, proj)
    load_proj.start()

    lax.fori_loop(0, 2 * shards_n, tables, 0)
    for step in range(1, shards_n):
        small_copy(step, False).wait()
    own[0].wait()
    load_small = load(0, small_out, small_low)
    load_small.start()
    load_small.wait()
    small[...] = small_low[...].astype(jnp.float32)
    on_step(0, lambda block, way: norm(block, x_ref, way))

    load_up = load(2, up_out, up)
    load_qkv = load(3, qkv_out, qkv)
    ticks = [list(range(shards_n - 1 + bits)) for thing in range(2)]

    def some_ticks(thing, number):
        for tick in ticks[thing][:number]:
            column_tick(thing, tick)
        del ticks[thing][:number]

    def send_upstream(to_ends):
        for other in range(1, shards_n):
            to = lax.rem(place + other, shards_n)
            at_end = (to == 0) | (to == shards_n - 1)

            @pl.when(at_end if to_ends else jnp.logical_not(at_end))
            def _():
                upstream_copy(other, True).start()

    def norms(step):
        on_step(step, lambda block, way: norm(block, x_out.at[block_rows(block), :], way))

    def units(step):
        on_step(step, lambda block, way: hidden_units(block))

    some_ticks(0, 3)
    pass_on(1)
    norms(1)
    some_ticks(0, len(ticks[0]))
    own[1].wait()
    load_up.start()
    for step in range(2, shards_n - 1):
        pass_on(step)
    for item in range(shards_n - 1, len(items)):
        for path in range(2):
            for copy in turned(item, path, True):
                copy.start()
    send_upstream(False)
    load_up.wait()
    units(0)
    for step in range(2, shards_n - 1):
        norms(step)
    some_ticks(1, 1)
    units(1)
    some_ticks(1, 1)
    for way in range(2):

        @pl.when(goes(way, shards_n - 2))
        def _():
            hop(way, shards_n - 2, True).wait_send()

    send_upstream(True)
    pass_on(shards_n - 1)
    norms(shards_n - 1)
    some_ticks(1, 1)
    keeps = [keep(0, mlp, mlp_out), keep(1, attn, attn_out)]
    keeps[0].start()
    keeps[1].start()
    for step in range(2, shards_n):
        units(step)
        some_ticks(1, 1)
    some_ticks(1, len(ticks[1]))
    for copy in own[4:]:
        copy.wait()
    load_qkv.start()
    keeps += [keep(2, act, act_out), keep(3, slope, slope_out)]
    keeps[2].start()
    keeps[3].start()
    load_qkv.wait()
    for third in range(3):
        project(third)
    keeps.append(keep(4, heads, heads_out))
    keeps[4].start()
    for head in range(wide // HEAD):
        attend(head)
    keeps.append(keep(5, mixed, mixed_out))
    keeps[5].start()
    load_proj.wait()
    for j in range(width // cols):
        branch_cols(j)
    for step in range(1, shards_n):
        upstream_copy(step, False).wait()
    for j in range(max(width // cols - 2, 0), width // cols):
        branch_keep(j).wait()
    for copy in keeps:
        copy.wait()
    for item in range(len(items)):
        for path in range(2):
            for copy in turned(item, path, True):
                copy.wait_send()
            for level in range(bits):
                spread(item, path, level).wait_send()
    for step in range(shards_n - 2):
        for way in range(2):

            @pl.when(goes(way, step))
            def _():
                hop(way, step, True).wait_send()

    for copy in own[2:4]:
        copy.wait()


def forward(small, up_weight, qkv_weight, x, g, down_weight, proj_weight, bias, frequency, lengths):
    replicas, count = lax.axis_size("replica"), lax.axis_size("shard")
    bits = replicas.bit_length() - 1
    local, width = x.shape
    tokens = local * count
    hidden, wide = up_weight.shape[1] // count, width // count
    cols = wide
    items = 2 * (count - 1)
    any_spec = pl.BlockSpec(memory_space=pl.ANY)
    vmem_spec = pl.BlockSpec(memory_space=pltpu.VMEM)
    shapes = dict(
        small=(count,) + small.shape,
        up_cols=(width, hidden),
        qkv_cols=(3, width, wide),
        x=(tokens, width),
        g=(tokens, width),
        mlp_in=(tokens, width),
        attn_in=(tokens, width),
        act=(tokens, hidden),
        slope=(tokens, hidden),
        heads=(3, tokens, wide),
        mixed=(tokens, wide),
        branch=(tokens, width),
    )
    low = lambda *shape: pltpu.VMEM(shape, jnp.bfloat16)
    dma = lambda *shape: pltpu.SemaphoreType.DMA(shape)
    found = pl.pallas_call(
        partial(forward_kernel, replicas, count),
        out_shape=tuple(jax.ShapeDtypeStruct(shape, jnp.bfloat16) for shape in shapes.values())
        + (
            jax.ShapeDtypeStruct((2, tokens, 1), jnp.float32),
            jax.ShapeDtypeStruct((3, tokens, 128), jnp.float32),
            jax.ShapeDtypeStruct((tokens, 1), jnp.int32),
        ),
        in_specs=[any_spec] * 7 + [vmem_spec] * 2 + [pl.BlockSpec(memory_space=pltpu.SMEM)],
        out_specs=(any_spec,) * len(shapes) + (vmem_spec,) * 3,
        scratch_shapes=[
            low(*shapes["small"]),
            pltpu.VMEM(shapes["small"], jnp.float32),
            low(2, local, width),
            low(tokens, width),
            low(tokens, width),
            low(width, hidden),
            low(3, width, wide),
            low(tokens, hidden),
            low(tokens, hidden),
            low(3, tokens, wide),
            low(tokens, wide),
            low(2, hidden, cols),
            low(wide, width),
            low(2, tokens, cols),
            dma(7),
            dma(7),
            dma(6 + width // cols),
            dma(2, count),
            dma(2, items, 2, 3),
            dma(2, items, 2, bits),
            dma(2, 2, count - 1),
            dma(2, count),
        ],
        compiler_params=pltpu.CompilerParams(
            collective_id=0, has_side_effects=True, vmem_limit_bytes=58 * 2**20
        ),
        cost_estimate=pl.CostEstimate(
            flops=2 * tokens * width * (hidden * 2 + wide * 4),
            bytes_accessed=500_000_000,
            transcendentals=0,
        ),
    )(small, up_weight, qkv_weight, x, g, down_weight, proj_weight, bias, frequency, lengths)
    return dict(zip(list(shapes) + ["stats", "tables", "first"], found))


RING = 3


def grads_kernel(
    replicas,
    shards_n,
    act_ref,
    up_ref,
    mixed_ref,
    mlp_ref,
    attn_ref,
    slope_ref,
    down_ref,
    proj_ref,
    heads_ref,
    rows_ref,
    cols_up_ref,
    cols_qkv_ref,
    tables_ref,
    first_ref,
    stats_ref,
    small_ref,
    out_ref,
    vec_out,
    sum_out,
    work,
    from_core,
    *rest,
):
    rep, place = lax.axis_index("replica"), lax.axis_index("shard")
    bits = replicas.bit_length() - 1
    far = bits - 1
    from_far = rest[:far]
    (
        big,
        narrow,
        pre,
        joined,
        wide_rows,
        slope,
        heads,
        key_sum,
        value_sum,
        tile_x,
        tile_up,
        tile_qkv,
        shared,
        vec_got,
        vec_sum,
        load_sem,
        core_sem,
        far_sem,
        turn_sem,
        own_sem,
        plane_sem,
        vec_sem,
        sum_sem,
    ) = rest[far:]
    chunks, _, rows, cols = out_ref.shape
    slots = work.shape[0]
    half, side = rows // 2, cols // 2
    piece = rows // replicas
    orders = plane_orders(replicas)
    core = bit_of(rep, 0)
    tokens, width = up_ref.shape
    local = tokens // shards_n
    hiddens = pre.shape[1] // cols
    natives = hiddens + 1
    mine = pl.multiple_of(core * half, half)
    theirs = pl.multiple_of((1 - core) * half, half)

    starts = []
    for order in orders:
        line, size = [core * half], half
        for bit in order:
            size //= 2
            line.append(line[-1] + bit_of(rep, bit) * size)
        starts.append(line)

    def spot(k):
        if k < natives:
            return k + hiddens
        return k - natives if k < natives + hiddens else k

    def load(source, target, number):
        return pltpu.make_async_copy(source, target, load_sem.at[number])

    def narrow_load(k):
        source = act_ref.at[:, pl.ds(k * cols, cols)] if k < hiddens else mixed_ref
        return load(source, narrow.at[k % 2], k % 2)

    def big_load(which):
        return load((up_ref, mlp_ref, attn_ref)[which], big.at[which % 2], 2 + which)

    def down_load(k):
        return load(down_ref.at[pl.ds(k * cols, cols), :], wide_rows.at[k % 2], 5 + k % 2)

    def slope_load(k):
        return load(slope_ref.at[:, pl.ds(k * cols, cols)], slope.at[k % 2], 7 + k % 2)

    def pre_loads(k):
        return [down_load(k), slope_load(k)]

    def proj_load():
        return load(proj_ref, wide_rows.at[1], 6)

    def heads_load():
        return load(heads_ref, heads.at[pl.ds(0, 3)], 9)

    def tile_loads(j):
        some = pl.ds(j * TILE, TILE)
        return [
            load(rows_ref.at[:, some], tile_x.at[j % 2], 10 + j % 2),
            load(cols_up_ref.at[some, :], tile_up.at[j % 2], 12 + j % 2),
        ] + [
            load(
                cols_qkv_ref.at[third, some, :],
                tile_qkv.at[j % 2, :, pl.ds(third * cols, cols)],
                14 + 2 * third + j % 2,
            )
            for third in range(3)
        ]

    def to_core(k):
        return remote(
            work.at[k % slots, :, pl.ds(theirs, half), :],
            from_core.at[k % RING],
            core_sem,
            (0, k),
            {"replica": flip(rep, 0)},
        )

    def to_far(k, level, path):
        size = half >> (level + 1)
        bit = orders[path][level]
        start = starts[path][level] + (1 - bit_of(rep, bit)) * size
        return remote(
            work.at[k % slots, :, pl.ds(pl.multiple_of(start, size), size), pl.ds(path * side, side)],
            from_far[level].at[k % RING, path],
            far_sem,
            (k, level, path),
            {"replica": flip(rep, bit)},
        )

    def own_piece(k, path, block):
        return work.at[
            k % slots,
            block,
            pl.ds(pl.multiple_of(starts[path][far], piece), piece),
            pl.ds(path * side, side),
        ]

    def place_piece(k, path, block):
        return out_ref.at[
            spot(k),
            block,
            pl.ds(pl.multiple_of(starts[path][far], piece), piece),
            pl.ds(path * side, side),
        ]

    def settle(k, path):
        block = pl.ds(0, shards_n) if k < natives else place
        return pltpu.make_async_copy(
            own_piece(k, path, block), place_piece(k, path, block), own_sem.at[k % 2, path]
        )

    def turned(k, path, step, sending):
        to = lax.rem(place + step, shards_n)
        shard = place if sending else lax.rem(place - step + shards_n, shards_n)
        return remote(
            own_piece(k, path, to),
            place_piece(k, path, shard),
            turn_sem,
            (k - natives, path, step - 1),
            {"shard": to},
        )

    def spread(k, path, level):
        size = piece << level
        bit = orders[path][far - 1 - level]
        here = out_ref.at[
            spot(k),
            :,
            pl.ds(pl.multiple_of(starts[path][far - level], size), size),
            pl.ds(path * side, side),
        ]
        return remote(here, here, plane_sem, (k, level, path), {"replica": flip(rep, bit)})

    def spread_core(k):
        here = out_ref.at[spot(k), :, pl.ds(mine, half), :]
        return remote(here, here, core_sem, (1, k), {"replica": flip(rep, 0)})

    def put(offset, sums):
        for i in range(sums.shape[1] // 128):
            vec_sum[pl.ds(offset // 128 + i, 1), :] = sums[:, i * 128 : (i + 1) * 128]

    def compute(k):
        if k < natives:
            narrow_load(k).wait()
            if k + 1 < natives:
                narrow_load(k + 1).start()
        if k == 0:
            big_load(0).wait()
        if k == natives:
            big_load(1).wait()
        if k == natives + hiddens:
            big_load(2).wait()
        slot = k % slots
        which = 1 if natives <= k < natives + hiddens else 0

        def block(g, carry):
            if k < natives:
                left = narrow[k % 2]
                right = big[which, :, pl.ds(pl.multiple_of(g * cols, cols), cols)]
            else:
                left = big[which, :, pl.ds(pl.multiple_of(g * rows, rows), rows)]
                if k < natives + hiddens:
                    right = pre[:, (k - natives) * cols : (k - natives + 1) * cols]
                else:
                    third = k - natives - hiddens
                    right = joined[:, third * cols : (third + 1) * cols]
            work[slot, g] = dot_rows(left, right).astype(jnp.bfloat16)
            return carry

        lax.fori_loop(0, shards_n, block, 0)
        to_core(k).start()

    def add(k, start, size, left, width, got):
        def block(g, carry):
            where = (k % slots, g, pl.ds(pl.multiple_of(start, size), size), pl.ds(left, width))
            work[where] = (
                work[where].astype(jnp.float32) + got(g).astype(jnp.float32)
            ).astype(jnp.bfloat16)
            return carry

        lax.fori_loop(0, shards_n, block, 0)

    def grad_mixed():
        proj_load().wait()

        def block(i, carry):
            some = pl.ds(pl.multiple_of(i * TALL, TALL), TALL)
            heads[3, some, :] = dot_cols(big[0, some, :], wide_rows[1]).astype(jnp.bfloat16)
            return carry

        lax.fori_loop(0, tokens // TALL, block, 0)
        down_load(1).start()
        own = pl.ds(pl.multiple_of(place * cols, cols), cols)
        put(4 * width + place * cols, jnp.sum(big[0, :, own].astype(jnp.float32), 0, keepdims=True))

    def grad_pre(k):
        for copy in pre_loads(k):
            copy.wait()

        def block(i, total):
            some = pl.ds(pl.multiple_of(i * TALL, TALL), TALL)
            found = dot_cols(big[0, some, :], wide_rows[k % 2]) * slope[k % 2, some, :].astype(
                jnp.float32
            )
            low = found.astype(jnp.bfloat16)
            pre[some, k * cols : (k + 1) * cols] = low
            return total + jnp.sum(low.astype(jnp.float32), 0, keepdims=True)

        total = lax.fori_loop(0, tokens // TALL, block, jnp.zeros((1, cols), jnp.float32))
        put(8 * width + (place * hiddens + k) * cols, total)
        if k + 2 < hiddens:
            for copy in pre_loads(k + 2):
                copy.start()

    def turn_rows(found, some):
        lead = found[:, :128]
        lead = (
            lead * tables_ref[0, some, :]
            + pltpu.roll(lead, 96, 1) * tables_ref[1, some, :]
            - pltpu.roll(lead, 32, 1) * tables_ref[2, some, :]
        )
        return jnp.concatenate([lead, found[:, 128:]], 1)

    def attention(head):
        lanes = pl.ds(head * HEAD, HEAD)
        scale = 1.0 / math.sqrt(HEAD)
        key_sum[...] = jnp.zeros_like(key_sum)
        value_sum[...] = jnp.zeros_like(value_sum)
        sums = [jnp.zeros((1, HEAD), jnp.float32)] * 3
        for i in range(tokens // TILE):
            some, keys = pl.ds(i * TILE, TILE), pl.ds(0, (i + 1) * TILE)
            query = heads[0, some, lanes]
            key = heads[1, keys, lanes]
            probs = causal_probs(query, key, first_ref[some, :], i * TILE)
            grad = heads[3, some, lanes]
            grad_probs = dot_cols(grad, heads[2, keys, lanes])
            delta = jnp.sum(probs * grad_probs, -1, keepdims=True)
            low = (probs * (grad_probs - delta)).astype(jnp.bfloat16)
            found = turn_rows(dot(low, key) * scale, some).astype(jnp.bfloat16)
            joined[some, pl.ds(head * HEAD, HEAD)] = found
            sums[0] = sums[0] + jnp.sum(found.astype(jnp.float32), 0, keepdims=True)
            key_sum[keys, :] = key_sum[keys, :] + dot_rows(low, query)
            value_sum[keys, :] = value_sum[keys, :] + dot_rows(probs.astype(jnp.bfloat16), grad)
        for i in range(tokens // TILE):
            some = pl.ds(i * TILE, TILE)
            for third, found in (
                (1, turn_rows(key_sum[some, :] * scale, some)),
                (2, value_sum[some, :]),
            ):
                low = found.astype(jnp.bfloat16)
                joined[some, pl.ds(third * cols + head * HEAD, HEAD)] = low
                sums[third] = sums[third] + jnp.sum(low.astype(jnp.float32), 0, keepdims=True)
        for third in range(3):
            put(5 * width + third * width + place * cols + head * HEAD, sums[third])

    def sum_part(j, step, sending):
        to = lax.rem(place + step, shards_n)
        shard = place if sending else lax.rem(place - step + shards_n, shards_n)
        some = pl.ds(j * TILE, TILE)
        source = shared.at[pl.ds(pl.multiple_of(to * local, local), local), some]
        if step == 0:
            return pltpu.make_async_copy(source, sum_out.at[place, :, some], sum_sem.at[0, j, 0])
        return remote(source, sum_out.at[shard, :, some], sum_sem, (j, step), {"shard": to})

    def tile(j):
        for copy in tile_loads(j):
            copy.wait()
        if j + 1 < width // TILE:
            for copy in tile_loads(j + 1):
                copy.start()
        lanes = pl.ds(j * TILE, TILE)
        owner, begin = divmod(j * TILE, cols)
        theirs_at = slice(begin, begin + TILE)

        def block(i, totals):
            some = pl.ds(pl.multiple_of(i * TALL, TALL), TALL)
            normed = (tile_x[j % 2, some, :].astype(jnp.float32) - stats_ref[0, some, :]) * stats_ref[
                1, some, :
            ]
            mlp = dot_cols(pre[some, :], tile_up[j % 2])
            attn = dot_cols(joined[some, :], tile_qkv[j % 2])
            shared[some, lanes] = (
                attn * small_ref[owner, 0:1, theirs_at].astype(jnp.float32)
                + mlp * small_ref[owner, 3:4, theirs_at].astype(jnp.float32)
            ).astype(jnp.bfloat16)
            found = (attn * normed, attn, mlp * normed, mlp)
            return tuple(t + jnp.sum(f, 0, keepdims=True) for t, f in zip(totals, found))

        zero = jnp.zeros((1, TILE), jnp.float32)
        totals = lax.fori_loop(0, tokens // TALL, block, (zero,) * 4)
        for number, total in enumerate(totals):
            put(number * width + j * TILE, total)
        for step in range(shards_n):
            sum_part(j, step, True).start()

    def stage(k, number):
        if number == 0:
            compute(k)
        elif number == 1:
            to_core(k).wait()
            add(k, mine, half, 0, cols, lambda g: from_core[k % RING, g])
            for path in range(2):
                to_far(k, 0, path).start()
        elif number <= 1 + far:
            level = number - 2
            for path in range(2):
                to_far(k, level, path).wait()
                size = half >> (level + 1)
                add(
                    k,
                    starts[path][level + 1],
                    size,
                    path * side,
                    side,
                    lambda g: from_far[level][k % RING, path, g],
                )
                if level + 1 < far:
                    to_far(k, level + 1, path).start()
                else:
                    if k >= natives:
                        for step in range(1, shards_n):
                            turned(k, path, step, True).start()
                    settle(k, path).start()
        elif number == 2 + far:
            for path in range(2):
                settle(k, path).wait()
                if k >= natives:
                    for step in range(1, shards_n):
                        turned(k, path, step, False).wait_recv()
                spread(k, path, 0).start()
            if k >= natives:
                for path in range(2):
                    for step in range(1, shards_n):
                        turned(k, path, step, True).wait_send()
        elif number <= 2 + 2 * far:
            level = number - 3 - far
            for path in range(2):
                spread(k, path, level).wait()
                if level + 1 < far:
                    spread(k, path, level + 1).start()
            if level + 1 == far:
                spread_core(k).start()
        else:
            spread_core(k).wait()

    stages = 4 + 2 * far
    n_heads, n_tiles = cols // HEAD, width // TILE
    extras = {0: [grad_mixed, partial(grad_pre, 0)]}
    for k in range(1, hiddens):
        extras.setdefault(k, []).append(partial(grad_pre, k))
    for head in range(n_heads):
        extras.setdefault(1 + head, []).append(partial(attention, head))
    extras[hiddens] = [big_load(2).start]
    tile_at = hiddens + 1
    for j in range(n_tiles):
        extras.setdefault(tile_at + j, []).append(partial(tile, j))
    vec_at = max(extras) + 1

    for copy in [narrow_load(0), big_load(0), proj_load()] + pre_loads(0):
        copy.start()
    slope_load(1).start()
    for copy in [heads_load(), big_load(1)] + tile_loads(0):
        copy.start()
    vec_sum[...] = jnp.zeros_like(vec_sum)
    greet(rep, place, replicas, shards_n)
    peers = [{"replica": flip(rep, bit)} for bit in range(bits)]
    peers += [{"shard": flip(place, bit)} for bit in range(shards_n.bit_length() - 1)]

    def vec_copy(number):
        return remote(vec_sum, vec_got.at[number], vec_sem, (number,), peers[number])

    for tick in range(max(chunks + stages - 1, vec_at + len(peers) + 1)):
        for number in reversed(range(stages)):
            if 0 <= tick - number < chunks:
                stage(tick - number, number)
        if tick == 0:
            heads_load().wait()
        for extra in extras.get(tick, []):
            extra()
        turn_of = tick - vec_at
        if 0 < turn_of <= len(peers):
            vec_copy(turn_of - 1).wait()
            vec_sum[...] = vec_sum[...] + vec_got[turn_of - 1]
        if 0 <= turn_of < len(peers):
            vec_copy(turn_of).start()
    vec_out[...] = vec_sum[...]
    for j in range(n_tiles):
        for step in range(shards_n):
            sum_part(j, step, False).wait()


def summed_grads(*operands):
    act, up, mixed, mlp_in = operands[:4]
    replicas, count = lax.axis_size("replica"), lax.axis_size("shard")
    bits = replicas.bit_length() - 1
    far = bits - 1
    tokens, width = up.shape
    cols = width // count
    hidden = act.shape[1]
    hiddens = hidden // cols
    natives = hiddens + 1
    chunks = natives + hiddens + 3
    peers = bits + count.bit_length() - 1
    slots = 2 + far
    vector = ((8 * width + count * hidden) // 128, 128)
    any_spec = pl.BlockSpec(memory_space=pl.ANY)
    vmem_spec = pl.BlockSpec(memory_space=pltpu.VMEM)
    low = lambda *shape: pltpu.VMEM(shape, jnp.bfloat16)
    full = lambda *shape: pltpu.VMEM(shape, jnp.float32)
    dma = lambda *shape: pltpu.SemaphoreType.DMA(shape)
    return pl.pallas_call(
        partial(grads_kernel, replicas, count),
        out_shape=(
            jax.ShapeDtypeStruct((chunks, count, cols, cols), jnp.bfloat16),
            jax.ShapeDtypeStruct(vector, jnp.float32),
            jax.ShapeDtypeStruct((count, tokens // count, width), jnp.bfloat16),
        ),
        in_specs=[any_spec] * 12 + [vmem_spec] * 4,
        out_specs=(any_spec, vmem_spec, any_spec),
        scratch_shapes=[
            low(slots, count, cols, cols),
            low(RING, count, cols // 2, cols),
        ]
        + [low(RING, 2, count, cols >> (level + 2), cols // 2) for level in range(far)]
        + [
            low(2, tokens, width),
            low(2, tokens, cols),
            low(tokens, hidden),
            low(tokens, 3 * cols),
            low(2, cols, width),
            low(2, tokens, cols),
            low(4, tokens, cols),
            full(tokens, HEAD),
            full(tokens, HEAD),
            low(2, tokens, TILE),
            low(2, TILE, hidden),
            low(2, TILE, 3 * cols),
            low(tokens, width),
            full(peers, *vector),
            full(*vector),
            dma(20),
            dma(2, 2, chunks),
            dma(2, chunks, far, 2),
            dma(2, chunks - natives, 2, count - 1),
            dma(2, 2),
            dma(2, chunks, far, 2),
            dma(2, peers),
            dma(2, width // TILE, count),
        ],
        compiler_params=pltpu.CompilerParams(
            collective_id=1, has_side_effects=True, vmem_limit_bytes=60 * 2**20
        ),
        cost_estimate=pl.CostEstimate(
            flops=4 * tokens * chunks * count * cols * cols,
            bytes_accessed=600_000_000,
            transcendentals=0,
        ),
    )(*operands)


def last_kernel(
    up_blocks,
    down_blocks,
    out_blocks,
    qkv_blocks,
    parts_ref,
    branch_ref,
    x_ref,
    g_ref,
    small_ref,
    vec_ref,
    layer_out,
    input_out,
    up_out,
    down_out,
    out_out,
    qkv_out,
    *thin_outs,
):
    number, count, _, cols = up_blocks.shape
    for g in range(count):
        lanes = slice(g * cols, (g + 1) * cols)
        for k in range(number):
            at = (g * number + k) * cols
            up_out[:, at : at + cols] = up_blocks[k, g].astype(jnp.float32)
        for k in range(3):
            at = (k * count + g) * cols
            qkv_out[:, at : at + cols] = qkv_blocks[k, g].astype(jnp.float32)
        down_out[:, lanes] = down_blocks[0, g].astype(jnp.float32)
        out_out[:, lanes] = out_blocks[0, g].astype(jnp.float32)
    rows = x_ref[...].astype(jnp.float32)
    normed, inverse_std = normalize(rows)
    grad = sum(parts_ref[g].astype(jnp.float32) for g in range(count))
    input_out[...] = g_ref[...].astype(jnp.float32) + norm_backward(grad, normed, inverse_std)
    for g in range(count):
        lanes = slice(g * cols, (g + 1) * cols)
        bias = small_ref[g, 2:3, :].astype(jnp.float32) + small_ref[g, 5:6, :].astype(jnp.float32)
        layer_out[:, lanes] = (
            rows[:, lanes] + branch_ref[:, lanes].astype(jnp.float32) + bias
        ).astype(jnp.bfloat16)

    @pl.when(pl.program_id(0) == 0)
    def _():
        place = lax.axis_index("shard")
        width = count * cols
        for thin, start in zip(thin_outs, (0, 1, 4, 4, 2, 3, 5, 8)):
            length = thin.shape[0]
            first = (start * width + place * length) // 128
            for i in range(length // 128):
                thin[i * 128 : (i + 1) * 128] = vec_ref[first + i, :]


def last(blocks, parts, branch, x, g, small, vector):
    count, rows, cols = blocks.shape[1:]
    number = (blocks.shape[0] - 4) // 2
    local, width = x.shape
    steps = local // 16
    some, tall = rows // steps, number * rows // steps
    turns = rows // tall
    whole = lambda i: (i, 0)
    thin = [rows] * 6 + [3 * rows, number * rows]
    return pl.pallas_call(
        last_kernel,
        out_shape=(
            jax.ShapeDtypeStruct((local, width), jnp.bfloat16),
            jax.ShapeDtypeStruct((local, width), jnp.float32),
            jax.ShapeDtypeStruct((rows, number * width), jnp.float32),
            jax.ShapeDtypeStruct((number * rows, width), jnp.float32),
            jax.ShapeDtypeStruct((rows, width), jnp.float32),
            jax.ShapeDtypeStruct((rows, 3 * width), jnp.float32),
        )
        + tuple(jax.ShapeDtypeStruct((length,), jnp.float32) for length in thin),
        grid=(steps,),
        in_specs=[
            pl.BlockSpec((number, count, some, cols), lambda i: (0, 0, i, 0)),
            pl.BlockSpec((1, count, tall, cols), lambda i: (number + i // turns, 0, i % turns, 0)),
            pl.BlockSpec((1, count, some, cols), lambda i: (2 * number, 0, i, 0)),
            pl.BlockSpec((3, count, some, cols), lambda i: ((2 * number + 1) // 3, 0, i, 0)),
            pl.BlockSpec((count, 16, width), lambda i: (0, i, 0)),
            pl.BlockSpec((16, width), whole),
            pl.BlockSpec((16, width), whole),
            pl.BlockSpec((16, width), whole),
            pl.BlockSpec(small.shape, lambda i: (0, 0, 0)),
            pl.BlockSpec(vector.shape, lambda i: (0, 0)),
        ],
        out_specs=(
            pl.BlockSpec((16, width), whole),
            pl.BlockSpec((16, width), whole),
            pl.BlockSpec((some, number * width), whole),
            pl.BlockSpec((tall, width), whole),
            pl.BlockSpec((some, width), whole),
            pl.BlockSpec((some, 3 * width), whole),
        )
        + tuple(pl.BlockSpec((length,), lambda i: (0,)) for length in thin),
        compiler_params=pltpu.CompilerParams(vmem_limit_bytes=62 * 2**20),
    )(blocks, blocks, blocks, blocks, parts, branch, x, g, small, vector)


def shards(
    layer_input,
    attn_gain,
    attn_shift,
    qkv_weight,
    qkv_bias,
    out_weight,
    out_bias,
    mlp_gain,
    mlp_shift,
    up_weight,
    up_bias,
    down_weight,
    down_bias,
    seq_lengths,
    upstream,
):
    local_rows = layer_input.shape[0]
    count = lax.axis_size("shard")
    group_rows = local_rows * count
    place = lax.axis_index("shard")
    part = D // count
    hidden = up_bias.shape[0]

    params = [attn_gain, attn_shift, out_bias, mlp_gain, mlp_shift, down_bias]
    params += [qkv_bias[i * part : (i + 1) * part] for i in range(3)]
    row = lax.broadcasted_iota(jnp.int32, (16, part), 0)
    small = jnp.zeros((16, part), jnp.bfloat16)
    for i, param in enumerate(params):
        small = jnp.where(row == i, param[None], small)

    frequency = np.power(np.float32(ROPE_BASE), -np.arange(ROT // 2, dtype=np.float32) * np.float32(2.0 / ROT))
    known = forward(
        small,
        up_weight,
        qkv_weight,
        layer_input,
        upstream,
        down_weight,
        out_weight,
        up_bias.astype(jnp.float32)[None],
        jnp.asarray(np.tile(frequency, 128 // (ROT // 2))[None]),
        seq_lengths,
    )
    branch_own = lax.psum_scatter(known["branch"], "shard", scatter_dimension=0, tiled=True)
    grads, vector, normed_parts = summed_grads(
        known["act"],
        known["g"],
        known["mixed"],
        known["mlp_in"],
        known["attn_in"],
        known["slope"],
        down_weight,
        out_weight,
        known["heads"],
        known["x"],
        known["up_cols"],
        known["qkv_cols"],
        known["tables"],
        known["first"],
        known["stats"],
        known["small"],
    )
    grads, branch_own = lax.optimization_barrier((grads, branch_own))
    layer_output, input_grad, up_grad, down_grad, out_grad, qkv_grad, *thin = last(
        grads, normed_parts, branch_own, layer_input, upstream, known["small"], vector
    )
    return (
        layer_output,
        input_grad,
        thin[0],
        thin[1],
        qkv_grad,
        thin[6],
        out_grad,
        thin[2],
        thin[4],
        thin[5],
        up_grad,
        thin[7],
        down_grad,
        thin[3],
    )


def solution(mesh):
    in_specs = (
        P(("replica", "shard"), None),
        P("shard"),
        P("shard"),
        P("shard", None),
        P("shard"),
        P("shard", None),
        P("shard"),
        P("shard"),
        P("shard"),
        P("shard", None),
        P("shard"),
        P("shard", None),
        P("shard"),
        P("replica", None),
        P(("replica", "shard"), None),
    )
    out_specs = (
        P(("replica", "shard"), None),
        P(("replica", "shard"), None),
        P("shard"),
        P("shard"),
        P("shard", None),
        P("shard"),
        P("shard", None),
        P("shard"),
        P("shard"),
        P("shard"),
        P("shard", None),
        P("shard"),
        P("shard", None),
        P("shard"),
    )
    return jax.shard_map(shards, mesh=mesh, in_specs=in_specs, out_specs=out_specs, check_vma=False)
```
